512 devices in a mesh: gz: 128 (over z_hi, x, y, core), gy: 4 (over z_lo).
Axes of the slice: x: 4, y: 4, z: 16 (z_hi: 4, z_lo: 4; z = z_hi * 4 + z_lo), core: 2. Of those that a mesh axis runs over, the one named last changes fastest.
Arguments:
- density: float32 [512, 128, 512], P('gz', 'gy'), may hold values from 0.1 to 10
- right_side: float32 [512, 128, 512], P('gz', 'gy'), may hold values from -6 to 6
- pressure_guess: float32 [512, 128, 512], P('gz', 'gy'), may hold values from -6 to 6
Outputs:
- pressure: float32 [512, 128, 512], P('gz', 'gy')
The draws below stay inside these ranges and needn't reach their ends.
All inputs are finite; a program needn't handle non-finite values.
Results may differ from the reference program's by a relative error of at most 0.0001.
Values sent between devices are 32-bit elements; how exact they have to be, the bound alone decides.
A program may use at most 128 MiB of HBM per device.

```python
import math
import jax
import jax.numpy as jnp
from jax import lax

CX = 512
COARSE_SWEEPS = 8
NY = 128
NZ = 512


def draw_right_side(key, part):
    key = jax.random.fold_in(key, 7)
    rough_part = jax.random.truncated_normal(key, -6.0, 6.0, (NZ, NY, CX), jnp.float32)
    return rough_part


def draw_density(key, part):
    key = jax.random.fold_in(key, 11)
    heights = (jnp.arange(NZ, dtype=jnp.float32) + 0.5) / NZ
    trend = 0.3 * jnp.exp(math.log(10.0) * heights)
    rough_log = jax.random.uniform(key, (NZ, NY, CX), jnp.float32, math.log(1.0 / 3.0), math.log(10.0 / 3.0))
    return jnp.clip(trend[:, None, None] * jnp.exp(rough_log), 0.1, 10.0)


def shard_levels(key, dims, split, low, largest):
    factor_of, own = 1.0, jax.random.fold_in(key, 6)
    for position, parts in split:
        steps = jnp.exp(jax.random.uniform(jax.random.fold_in(own, position), (parts,), jnp.float32, low / len(split), largest / len(split)))
        factor_of = factor_of * jnp.repeat(steps, dims[position] // parts).reshape([-1 if axis == position else 1 for axis in range(len(dims))])
    return factor_of


def gaussian(rng, extent, deviation, bound, cuts=(), held_as=jnp.bfloat16):
    drawn = deviation * jax.random.normal(rng, extent, jnp.float32)
    if cuts:
        drawn = drawn * shard_levels(rng, extent, cuts, -0.22, 0.18)
    return jnp.clip(drawn, -bound, bound).astype(held_as)


def setup_inputs(seed: int = 0) -> dict:
    splits = jax.random.split(jax.random.key(seed), 4)
    density = draw_density(jax.random.fold_in(splits[3], 71), 0)
    right_side = draw_right_side(jax.random.fold_in(splits[3], 71), 0)
    pressure_guess = gaussian(splits[2], (NZ, NY, CX), 1.0, 6.0, ((0, 128), (1, 4)), jnp.float32)
    return dict(density=density, right_side=right_side, pressure_guess=pressure_guess)


relaxation = 0.8


def edge_pad(values, axis_num):
    length = values.shape[axis_num]
    first_layer = lax.slice_in_dim(values, 0, 1, axis=axis_num)
    last_layer = lax.slice_in_dim(values, length - 1, length, axis=axis_num)
    return jnp.concatenate([first_layer, values, last_layer], axis=axis_num)


def zero_pad(values, axis_num):
    widths = [(0, 0)] * values.ndim
    widths[axis_num] = (1, 1)
    return jnp.pad(values, widths)


def coefficients(density):
    face_list = []
    for axis_num in range(3):
        padded = edge_pad(density, axis_num)
        length = padded.shape[axis_num]
        low_side = lax.slice_in_dim(padded, 0, length - 1, axis=axis_num)
        high_side = lax.slice_in_dim(padded, 1, length, axis=axis_num)
        face_list.append(2.0 / (low_side + high_side))
    parts_list = []
    for axis_num in range(3):
        length = density.shape[axis_num]
        parts_list.append(lax.slice_in_dim(face_list[axis_num], 0, length, axis=axis_num))
        parts_list.append(lax.slice_in_dim(face_list[axis_num], 1, length + 1, axis=axis_num))
    diagonal = parts_list[0] + parts_list[1] + parts_list[2] + parts_list[3] + parts_list[4] + parts_list[5]
    return face_list, diagonal


def apply_operator(values, coeffs, level_scale):
    face_list, diagonal = coeffs
    summed = diagonal * values
    for axis_num in range(3):
        face_arr = face_list[axis_num]
        length = values.shape[axis_num]
        padded = zero_pad(values, axis_num)
        summed = summed - lax.slice_in_dim(face_arr, 0, length, axis=axis_num) * lax.slice_in_dim(padded, 0, length, axis=axis_num)
        summed = summed - lax.slice_in_dim(face_arr, 1, length + 1, axis=axis_num) * lax.slice_in_dim(padded, 2, length + 2, axis=axis_num)
    return level_scale * summed


def jacobi(values, source, coeffs, level_scale):
    return values + relaxation * (source - apply_operator(values, coeffs, level_scale)) / (level_scale * coeffs[1])


def restrict(values):
    depth, height, breadth = values.shape
    return values.reshape(depth // 2, 2, height // 2, 2, breadth // 2, 2).mean(axis=(1, 3, 5))


def prolong_axis(coarse, axis_num):
    length = coarse.shape[axis_num]
    padded = zero_pad(coarse, axis_num)
    even_part = 0.75 * coarse + 0.25 * lax.slice_in_dim(padded, 0, length, axis=axis_num)
    odd_part = 0.75 * coarse + 0.25 * lax.slice_in_dim(padded, 2, length + 2, axis=axis_num)
    stacked = jnp.stack([even_part, odd_part], axis=axis_num + 1)
    new_shape = list(coarse.shape)
    new_shape[axis_num] = 2 * length
    return stacked.reshape(new_shape)


def prolong(coarse):
    return prolong_axis(prolong_axis(prolong_axis(coarse, 0), 1), 2)


def reference(density, right_side, pressure_guess):
    dens_one = restrict(density)
    dens_two = restrict(dens_one)
    dens_three = restrict(dens_two)
    coeffs_zero = coefficients(density)
    coeffs_one = coefficients(dens_one)
    coeffs_two = coefficients(dens_two)
    coeffs_three = coefficients(dens_three)
    smoothed = jacobi(pressure_guess, right_side, coeffs_zero, 1.0)
    source_one = restrict(right_side - apply_operator(smoothed, coeffs_zero, 1.0))
    corr_one = jacobi(jnp.zeros_like(source_one), source_one, coeffs_one, 0.25)
    source_two = restrict(source_one - apply_operator(corr_one, coeffs_one, 0.25))
    corr_two = jacobi(jnp.zeros_like(source_two), source_two, coeffs_two, 0.0625)
    source_three = restrict(source_two - apply_operator(corr_two, coeffs_two, 0.0625))
    corr_three = jnp.zeros_like(source_three)
    resid = source_three
    direction = source_three
    norm_now = jnp.sum(resid * resid)
    for sweep_num in range(COARSE_SWEEPS):
        image = apply_operator(direction, coeffs_three, 0.015625)
        alpha = norm_now / jnp.sum(direction * image)
        corr_three = corr_three + alpha * direction
        resid = resid - alpha * image
        norm_next = jnp.sum(resid * resid)
        direction = resid + (norm_next / norm_now) * direction
        norm_now = norm_next
    up_two = jacobi(corr_two + prolong(corr_three), source_two, coeffs_two, 0.0625)
    up_one = jacobi(corr_one + prolong(up_two), source_one, coeffs_one, 0.25)
    return jacobi(smoothed + prolong(up_one), right_side, coeffs_zero, 1.0)
```

```python
import functools

import jax
import jax.numpy as jnp
from jax import lax
from jax.experimental import pallas as pl
from jax.experimental.pallas import tpu as pltpu
from jax.sharding import PartitionSpec as P

MESH = pl.DeviceIdType.MESH
SWEEPS = 8
OMEGA = 0.8
F32 = jnp.float32
PAD = 8


def dot(a, b):
    return jnp.dot(a, b, precision=lax.Precision.HIGHEST, preferred_element_type=F32)


def twice_inverse(total):
    guess = pltpu.reciprocal(total, approx=True)
    return guess * (4.0 - 2.0 * total * guess)


def iota(shape, axis):
    return lax.broadcasted_iota(jnp.int32, shape, axis)


def pair_matrix(fine):
    rows, cols = iota((fine, fine // 2), 0), iota((fine, fine // 2), 1)
    return jnp.where(rows // 2 == cols, 1.0, 0.0).astype(F32)


def spread_matrix(coarse):
    rows, cols = iota((coarse, 2 * coarse), 0), iota((coarse, 2 * coarse), 1)
    parent = cols // 2
    near = parent + 2 * (cols % 2) - 1
    return (jnp.where(rows == parent, 0.75, 0.0) + jnp.where(rows == near, 0.25, 0.0)).astype(F32)


def padded_spread_matrix(coarse):
    shape = (2 * coarse + 2 * PAD, coarse + 2 * PAD)
    rows, cols = iota(shape, 0), iota(shape, 1)
    parent = rows // 2 + PAD // 2
    near = parent + 2 * (rows % 2) - 1
    return (jnp.where(cols == parent, 0.75, 0.0) + jnp.where(cols == near, 0.25, 0.0)).astype(F32)


class Level:
    def __init__(self, shape, chunk, rho, bx, by, bz, dg, idg):
        self.planes, self.rows, self.cols = shape
        self.chunk = chunk
        self.rho, self.bx, self.by, self.bz, self.dg, self.idg = rho, bx, by, bz, dg, idg

    def chunks(self):
        return [(r, self.chunk) for r in range(0, self.rows, self.chunk)]

    def faces_x(self, plane):
        n = self.cols
        for r, m in self.chunks():
            rho = self.rho[plane + 1, PAD + r : PAD + r + m, :]
            lane = iota((m, n), 1)
            low = twice_inverse(rho + jnp.where(lane == 0, rho, pltpu.roll(rho, 1, 1)))
            high = jnp.where(lane == n - 1, twice_inverse(rho + rho), pltpu.roll(low, n - 1, 1))
            self.dg[plane, r : r + m, :] = low + high
            self.bx[plane, r : r + m, :] = jnp.where(lane == 0, 0.0, low)

    def faces_y(self, plane):
        for r, m in self.chunks():
            low = self.rho[plane + 1, PAD - 1 + r : PAD - 1 + r + m, :]
            high = self.rho[plane + 1, PAD + r : PAD + r + m, :]
            self.by[plane, r : r + m, :] = twice_inverse(low + high)
        end = PAD + self.rows
        low = self.rho[plane + 1, end - 1 : end, :]
        high = self.rho[plane + 1, end : end + 1, :]
        self.by[plane, self.rows : self.rows + 1, :] = twice_inverse(low + high)

    def faces_z(self, face):
        for r, m in self.chunks():
            low = self.rho[face, PAD + r : PAD + r + m, :]
            high = self.rho[face + 1, PAD + r : PAD + r + m, :]
            self.bz[face, r : r + m, :] = twice_inverse(low + high)

    def diagonal(self, plane):
        for r, m in self.chunks():
            total = self.dg[plane, r : r + m, :]
            total = total + self.by[plane, r : r + m, :] + self.by[plane, r + 1 : r + 1 + m, :]
            total = total + self.bz[plane, r : r + m, :] + self.bz[plane + 1, r : r + m, :]
            self.dg[plane, r : r + m, :] = total
            self.idg[plane, r : r + m, :] = (0.5 * OMEGA) * twice_inverse(total)

    def mask_y(self, plane, low, high):
        self.by[plane, 0:1, :] = self.by[plane, 0:1, :] * low
        self.by[plane, self.rows : self.rows + 1, :] = self.by[plane, self.rows : self.rows + 1, :] * high

    def mask_z(self, low, high):
        self.bz[0] = self.bz[0] * low
        self.bz[self.planes] = self.bz[self.planes] * high

    def neighbours(self, val, plane, r, m):
        n = self.cols
        rows = slice(PAD + r, PAD + r + m)
        here = val[plane + 1, rows, :]
        bx = self.bx[plane, r : r + m, :]
        total = self.bz[plane, r : r + m, :] * val[plane, rows, :]
        total = total + self.bz[plane + 1, r : r + m, :] * val[plane + 2, rows, :]
        total = total + self.by[plane, r : r + m, :] * val[plane + 1, PAD - 1 + r : PAD - 1 + r + m, :]
        total = total + self.by[plane, r + 1 : r + 1 + m, :] * val[plane + 1, PAD + 1 + r : PAD + 1 + r + m, :]
        total = total + bx * pltpu.roll(here, 1, 1)
        total = total + pltpu.roll(bx * here, n - 1, 1)
        return here, total


def kernel(
    dens_in, right_in, guess_in, out,
    rho0, val0, smo0, src0, res0, bx0, by0, bz0, dg0, idg0,
    rho1, val1, up1, src1, res1, bx1, by1, bz1, dg1, idg1,
    rho2, val2, up2, src2, res2, bx2, by2, bz2, dg2, idg2,
    rows_out, rows_in, message, inbox_dens, inbox_src, tile, wide_dens, wide_src,
    rho3, bx3, by3, bz3, dg3, dir3, res3, img3, cor3, pair_tmp,
    local_sem, send_sem, recv_sem,
):
    gz, gy = lax.axis_index("gz"), lax.axis_index("gy")
    nz, ny = 128, 4
    core, ypos, xpos, zhi = gz % 2, (gz // 2) % 4, (gz // 8) % 4, gz // 32
    zpos = zhi * 4 + gy

    def gz_of(zh, x, y, c):
        return ((zh * 4 + x) * 4 + y) * 2 + c

    up_z, down_z = (gz + 1) % nz, (gz + nz - 1) % nz
    up_y, down_y = (gy + 1) % ny, (gy + ny - 1) % ny
    column = []
    for d in range(16):
        for k in range(2):
            if d or k:
                z = (zpos + d) % 16
                column.append((gz_of(z // 4, xpos, ypos, (core + k) % 2), z % 4))
    layer = []
    for i in range(4):
        for j in range(4):
            if i or j:
                layer.append((gz_of(zhi, (xpos + i) % 4, (ypos + j) % 4, core), gy))
    faces = [(up_z, gy), (down_z, gy), (gz, up_y), (gz, down_y)]
    corners = [(up_z, up_y), (up_z, down_y), (down_z, up_y), (down_z, down_y)]
    greeted = faces + corners + column + layer

    barrier = pltpu.get_barrier_semaphore()
    for device in greeted:
        pl.semaphore_signal(barrier, inc=1, device_id=device, device_id_type=MESH)

    local = []
    for i, (source, target) in enumerate(
        ((dens_in, rho0.at[1:5, 8:40, :]), (guess_in, val0.at[1:5, 8:40, :]), (right_in, src0))
    ):
        copy = pltpu.make_async_copy(source, target, local_sem.at[i])
        copy.start()
        local.append(copy)

    count = [0]

    def send(source, target, device):
        i = count[0]
        count[0] = i + 1
        copy = pltpu.make_async_remote_copy(
            src_ref=source, dst_ref=target, send_sem=send_sem.at[i], recv_sem=recv_sem.at[i],
            device_id=device, device_id_type=MESH,
        )
        copy.start()
        return copy

    def wait_recv(copies):
        for copy in copies:
            copy.wait_recv()

    def wait_send(copies):
        for copy in copies:
            copy.wait_send()

    fine = Level((4, 32, 512), 8, rho0, bx0, by0, bz0, dg0, idg0)
    middle = Level((2, 16, 256), 16, rho1, bx1, by1, bz1, dg1, idg1)
    coarse = Level((1, 8, 128), 8, rho2, bx2, by2, bz2, dg2, idg2)

    z_low = jnp.where(gz > 0, 1.0, 0.0).astype(F32)
    z_high = jnp.where(gz < nz - 1, 1.0, 0.0).astype(F32)
    y_low = jnp.where(gy > 0, 1.0, 0.0).astype(F32)
    y_high = jnp.where(gy < ny - 1, 1.0, 0.0).astype(F32)

    pair_x0, pair_x1 = pair_matrix(512), pair_matrix(256)
    pair_y0 = jnp.where(iota((16, 32), 1) // 2 == iota((16, 32), 0), 0.125, 0.0).astype(F32)
    pair_y1 = jnp.where(iota((8, 16), 1) // 2 == iota((8, 16), 0), 0.125, 0.0).astype(F32)

    def restrict0(read):
        return [dot(pair_y0, dot(read(2 * k) + read(2 * k + 1), pair_x0)) for k in range(2)]

    def restrict1(read):
        return dot(pair_y1, dot(read(0) + read(1), pair_x1))

    half_rows, half_cols = iota((128, 256), 0), iota((128, 256), 1)
    to_halves = jnp.where((half_cols % 64 == half_rows // 2) & ((half_cols < 64) | (half_cols >= 192)), 0.125, 0.0).astype(F32)

    def pack_message(field, value):
        pair_tmp[...] = dot(value, to_halves)
        for r in range(2):
            t = 4 * r
            message[field, r : r + 1, :] = (
                pair_tmp[t : t + 1, 0:128] + pair_tmp[t + 1 : t + 2, 0:128]
                + pair_tmp[t + 2 : t + 3, 128:256] + pair_tmp[t + 3 : t + 4, 128:256]
            )

    def gather_column(field, inbox):
        inbox[zhi, core, gy] = message[field]
        return [send(message.at[field], inbox.at[zhi, core, gy], device) for device in column]

    def gather_layer(field, inbox, wide):
        for zh in range(4):
            for y in range(4):
                tile[field, zh, 2 * y : 2 * y + 2, :] = inbox[zh, 0, y] + inbox[zh, 1, y]
        slot = xpos * 4 + ypos
        wide[slot] = tile[field]
        return [send(tile.at[field], wide.at[slot], device) for device in layer]

    local[0].wait()
    own1 = restrict0(lambda k: rho0[k + 1, 8:40, :])
    for k in range(2):
        rho1[k + 1, 8:24, :] = own1[k]
    own2 = restrict1(lambda k: own1[k])
    rho2[1, 8:16, :] = own2
    pack_message(0, own2)
    local[1].wait()
    for k in range(4):
        for f, ref in ((0, rho0), (1, val0)):
            rows_out[0, f, k : k + 1, :] = ref[k + 1, 39:40, :]
            rows_out[1, f, k : k + 1, :] = ref[k + 1, 8:9, :]

    pl.semaphore_wait(barrier, len(greeted))

    z_dens = [
        send(rho0.at[4, 8:40, :], rho0.at[0, 8:40, :], faces[0]),
        send(rho0.at[1, 8:40, :], rho0.at[5, 8:40, :], faces[1]),
    ]
    z_vals = [
        send(val0.at[4, 8:40, :], val0.at[0, 8:40, :], faces[0]),
        send(val0.at[1, 8:40, :], val0.at[5, 8:40, :], faces[1]),
    ]
    y_both = [
        send(rows_out.at[0, 0:2], rows_in.at[0, 0:2], faces[2]),
        send(rows_out.at[1, 0:2], rows_in.at[1, 0:2], faces[3]),
    ]

    def trade(ref, planes, rows):
        top = PAD + rows
        return [
            send(ref.at[planes, 8:top, :], ref.at[0, 8:top, :], faces[0]),
            send(ref.at[1, 8:top, :], ref.at[planes + 1, 8:top, :], faces[1]),
            send(ref.at[1 : planes + 1, rows : rows + 8, :], ref.at[1 : planes + 1, 0:8, :], faces[2]),
            send(ref.at[1 : planes + 1, 8:16, :], ref.at[1 : planes + 1, top : top + 8, :], faces[3]),
        ]

    dens1_copies = trade(rho1, 2, 16)
    dens2_copies = trade(rho2, 1, 8)
    column_dens = gather_column(0, inbox_dens)

    def fill_y(ref, planes, rows):
        top = PAD + rows
        for k in range(1, planes + 1):
            ref[k, 7:8, :] = jnp.where(gy == 0, ref[k, 8:9, :], ref[k, 7:8, :])
            ref[k, top : top + 1, :] = jnp.where(gy == ny - 1, ref[k, top - 1 : top, :], ref[k, top : top + 1, :])

    def fill_z(ref, planes, rows):
        top = PAD + rows
        ref[0, 8:top, :] = jnp.where(gz == 0, ref[1, 8:top, :], ref[0, 8:top, :])
        ref[planes + 1, 8:top, :] = jnp.where(gz == nz - 1, ref[planes, 8:top, :], ref[planes + 1, 8:top, :])

    for k in range(4):
        fine.faces_x(k)
    for face in (1, 2, 3):
        fine.faces_z(face)
    wait_recv(y_both)
    for k in range(4):
        for f, ref in ((0, rho0), (1, val0)):
            ref[k + 1, 7:8, :] = rows_in[0, f, k : k + 1, :]
            ref[k + 1, 40:41, :] = rows_in[1, f, k : k + 1, :]
    fill_y(rho0, 4, 32)
    for k in range(4):
        fine.faces_y(k)
    local[2].wait()

    def smooth(plane):
        for r, m in fine.chunks():
            here, near = fine.neighbours(val0, plane, r, m)
            smo0[plane + 1, 8 + r : 8 + r + m, :] = (1.0 - OMEGA) * here + (
                src0[plane, r : r + m, :] + near
            ) * fine.idg[plane, r : r + m, :]

    for k in (1, 2):
        fine.diagonal(k)
        fine.mask_y(k, y_low, y_high)
        smooth(k)
    wait_recv(z_dens)
    fill_z(rho0, 4, 32)
    for face in (0, 4):
        fine.faces_z(face)
    for k in (0, 3):
        fine.diagonal(k)
        fine.mask_y(k, y_low, y_high)
    fine.mask_z(z_low, z_high)
    wait_recv(z_vals)
    smooth(3)
    z_smooth = [send(smo0.at[4, 8:40, :], smo0.at[0, 8:40, :], faces[0])]
    smooth(0)
    z_smooth.append(send(smo0.at[1, 8:40, :], smo0.at[5, 8:40, :], faces[1]))
    for k in range(4):
        rows_out[0, 2, k : k + 1, :] = smo0[k + 1, 39:40, :]
        rows_out[1, 2, k : k + 1, :] = smo0[k + 1, 8:9, :]
    y_smooth = [
        send(rows_out.at[0, 2], rows_in.at[0, 2], faces[2]),
        send(rows_out.at[1, 2], rows_in.at[1, 2], faces[3]),
    ]

    def coefficients(level, copies):
        wait_recv(copies)
        fill_y(level.rho, level.planes, level.rows)
        fill_z(level.rho, level.planes, level.rows)
        for k in range(level.planes):
            level.faces_x(k)
            level.faces_y(k)
        for k in range(level.planes + 1):
            level.faces_z(k)
        for k in range(level.planes):
            level.diagonal(k)
            level.mask_y(k, y_low, y_high)
        level.mask_z(z_low, z_high)

    wait_recv(column_dens)
    layer_dens = gather_layer(0, inbox_dens, wide_dens)
    coefficients(middle, dens1_copies)
    coefficients(coarse, dens2_copies)

    wait_recv(y_smooth)
    for k in range(4):
        smo0[k + 1, 7:8, :] = rows_in[0, 2, k : k + 1, :]
        smo0[k + 1, 40:41, :] = rows_in[1, 2, k : k + 1, :]

    def residual(plane):
        for r, m in fine.chunks():
            here, near = fine.neighbours(smo0, plane, r, m)
            res0[plane, r : r + m, :] = src0[plane, r : r + m, :] - fine.dg[plane, r : r + m, :] * here + near

    for k in (1, 2):
        residual(k)
    wait_recv(z_smooth)
    for k in (0, 3):
        residual(k)

    source1 = restrict0(lambda k: res0[k])
    for k in range(2):
        src1[k] = source1[k]
        val1[k + 1, 8:24, :] = 4.0 * source1[k] * middle.idg[k]
    copies1 = trade(val1, 2, 16)

    wait_recv(layer_dens)
    lane, sub = iota((8, 128), 1), iota((8, 128), 0)
    right_half = lane >= 64
    first_x, last_x = (lane % 64) == 0, (lane % 64) == 63
    first_y, last_y = (lane < 64) & (sub == 0), (lane >= 64) & (sub == 7)

    def lower_y(v):
        q = pltpu.roll(v, 64, 1)
        return jnp.where(right_half, q, pltpu.roll(q, 1, 0))

    def upper_y(v):
        q = pltpu.roll(v, 64, 1)
        return jnp.where(right_half, pltpu.roll(q, 7, 0), q)

    scale3 = 0.015625
    for zh in range(4):
        for s in range(16):
            rho3[1 + 16 * zh + s] = wide_dens[s, zh]
    rho3[0] = rho3[1]
    rho3[65] = rho3[64]

    def face3(k, _):
        bz3[k] = scale3 * twice_inverse(rho3[k] + rho3[k + 1])
        return 0

    lax.fori_loop(0, 65, face3, 0)

    def coef3(k, _):
        rho = rho3[k + 1]
        edge = twice_inverse(rho + rho)
        low = twice_inverse(rho + jnp.where(first_x, rho, pltpu.roll(rho, 1, 1)))
        total = low + jnp.where(last_x, edge, pltpu.roll(low, 127, 1))
        bx3[k] = jnp.where(first_x, 0.0, scale3 * low)
        low = twice_inverse(rho + jnp.where(first_y, rho, lower_y(rho)))
        total = total + low + jnp.where(last_y, edge, upper_y(low))
        by3[k] = jnp.where(first_y, 0.0, scale3 * low)
        dg3[k] = scale3 * total + bz3[k] + bz3[k + 1]
        return 0

    lax.fori_loop(0, 64, coef3, 0, unroll=4)

    wait_recv(copies1)

    def residual1(k):
        here, near = middle.neighbours(val1, k, 0, 16)
        return (1.0 - OMEGA) * src1[k] + 0.25 * near

    source2 = restrict1(residual1)
    src2[0] = source2
    val2[1, 8:16, :] = 16.0 * source2 * coarse.idg[0]
    copies2 = trade(val2, 1, 8)
    wait_recv(copies2)
    here, near = coarse.neighbours(val2, 0, 0, 8)
    pack_message(1, (1.0 - OMEGA) * source2 + 0.0625 * near)
    column_src = gather_column(1, inbox_src)
    wait_recv(column_src)
    layer_src = gather_layer(1, inbox_src, wide_src)
    wait_recv(layer_src)

    zero_plane = jnp.zeros((8, 128), F32)
    dir3[0] = zero_plane
    dir3[65] = zero_plane
    for k in (0, 1, 66, 67):
        cor3[k] = zero_plane
    total = zero_plane
    for zh in range(4):
        for s in range(16):
            v = wide_src[s, zh]
            k = 16 * zh + s
            dir3[k + 1] = v
            res3[k] = v
            cor3[k + 2] = zero_plane
            total = total + v * v

    def whole(v):
        return jnp.sum(jnp.sum(v, axis=0, keepdims=True), axis=1, keepdims=True)

    def sweep(step, norm):
        def apply(k, acc):
            v = dir3[k + 1]
            bx, by = bx3[k], by3[k]
            image = dg3[k] * v - bz3[k] * dir3[k] - bz3[k + 1] * dir3[k + 2]
            image = image - by * lower_y(v) - upper_y(by * v)
            image = image - bx * pltpu.roll(v, 1, 1) - pltpu.roll(bx * v, 127, 1)
            img3[k] = image
            return acc + v * image

        bottom = whole(lax.fori_loop(0, 64, apply, zero_plane, unroll=16))
        alpha = norm / bottom

        def advance(k, acc):
            cor3[k + 2] = cor3[k + 2] + alpha * dir3[k + 1]
            r = res3[k] - alpha * img3[k]
            res3[k] = r
            return acc + r * r

        norm_next = whole(lax.fori_loop(0, 64, advance, zero_plane, unroll=16))
        beta = norm_next / norm

        def turn(k, _):
            dir3[k + 1] = res3[k] + beta * dir3[k + 1]
            return 0

        lax.fori_loop(0, 64, turn, 0, unroll=16)
        return norm_next

    lax.fori_loop(0, SWEEPS, sweep, whole(total))

    spread_rows, spread_cols = iota((128, 256), 0), iota((128, 256), 1)
    fine_x = spread_cols % 128
    parent = fine_x // 2
    near = parent + 2 * (fine_x % 2) - 1
    half = spread_cols // 128
    inside = (near >= 0) & (near < 64)
    from_halves = (
        jnp.where(spread_rows == parent + 64 * half, 0.75, 0.0)
        + jnp.where((spread_rows == near + 64 * half) & inside, 0.25, 0.0)
    ).astype(F32)
    row_at, col_at = iota((24, 16), 0) + 8 * gy - 8, iota((24, 16), 1)
    coarse_y = 2 * (col_at % 8) + col_at // 8
    row_up = row_at + 8
    parent_y = row_up // 2 - 4
    near_y = parent_y + 2 * (row_up % 2) - 1
    rows_from = (
        jnp.where(coarse_y == parent_y, 0.75, 0.0) + jnp.where(coarse_y == near_y, 0.25, 0.0)
    ).astype(F32)
    wait_send(copies2)
    for d in (-1, 0, 1):
        plane = gz + d + 4
        index = plane // 2
        other = index + 2 * (plane % 2) - 1
        mixed = 0.75 * cor3[index] + 0.25 * cor3[other]
        x_done = dot(mixed, from_halves)
        stacked = jnp.concatenate([x_done[:, 0:128], x_done[:, 128:256]], axis=0)
        val2[d + 1] = val2[d + 1] + dot(rows_from, stacked)

    here, near = coarse.neighbours(val2, 0, 0, 8)
    up2[1, 8:16, :] = (1.0 - OMEGA) * here + (16.0 * src2[0] + near) * coarse.idg[0]

    def trade_all(ref, planes, rows):
        top = PAD + rows
        copies = trade(ref, planes, rows)
        lowest, highest = slice(8, 16), slice(rows, rows + 8)
        copies.append(send(ref.at[planes, highest, :], ref.at[0, 0:8, :], corners[0]))
        copies.append(send(ref.at[planes, lowest, :], ref.at[0, top : top + 8, :], corners[1]))
        copies.append(send(ref.at[1, highest, :], ref.at[planes + 1, 0:8, :], corners[2]))
        copies.append(send(ref.at[1, lowest, :], ref.at[planes + 1, top : top + 8, :], corners[3]))
        return copies

    def clear_outside(ref, planes, rows):
        top = PAD + rows
        for k in range(planes + 2):
            ref[k, 0:8, :] = ref[k, 0:8, :] * y_low
            ref[k, top : top + 8, :] = ref[k, top : top + 8, :] * y_high
        ref[0] = ref[0] * z_low
        ref[planes + 1] = ref[planes + 1] * z_high

    spread_x1, spread_x0 = spread_matrix(128), spread_matrix(256)
    spread_y1, spread_y0 = padded_spread_matrix(8), padded_spread_matrix(16)

    def prolong(ref, planes, target, spread_x, spread_y):
        wide = [dot(spread_y, dot(ref[k], spread_x)) for k in range(planes + 2)]
        for k in range(2 * planes + 2):
            parent_z = (k + 1) // 2
            near_z = parent_z + 1 if k % 2 == 0 else parent_z - 1
            target[k] = target[k] + 0.75 * wide[parent_z] + 0.25 * wide[near_z]

    up2_copies = trade_all(up2, 1, 8)
    wait_recv(up2_copies)
    clear_outside(up2, 1, 8)
    wait_send(copies1)
    prolong(up2, 1, val1, spread_x1, spread_y1)
    for k in range(2):
        here, near = middle.neighbours(val1, k, 0, 16)
        up1[k + 1, 8:24, :] = (1.0 - OMEGA) * here + (4.0 * src1[k] + near) * middle.idg[k]
    up1_copies = trade_all(up1, 2, 16)
    wait_recv(up1_copies)
    clear_outside(up1, 2, 16)
    wait_send(z_smooth)
    prolong(up1, 2, smo0, spread_x0, spread_y0)
    for k in range(4):
        for r, m in fine.chunks():
            here, near = fine.neighbours(smo0, k, r, m)
            out[k, r : r + m, :] = (1.0 - OMEGA) * here + (src0[k, r : r + m, :] + near) * fine.idg[k, r : r + m, :]

    wait_send(
        z_dens + z_vals + y_both + dens1_copies + dens2_copies + column_dens + y_smooth + layer_dens
        + column_src + layer_src + up2_copies + up1_copies
    )


def level_scratch(planes, rows, cols):
    padded = pltpu.VMEM((planes + 2, rows + 2 * PAD, cols), F32)
    own = pltpu.VMEM((planes, rows, cols), F32)
    return [
        padded, padded, padded, own, own,
        own, pltpu.VMEM((planes, rows + 8, cols), F32), pltpu.VMEM((planes + 1, rows, cols), F32), own, own,
    ]


COPIES = 6 + 8 + 4 + 4 + 4 + 62 + 30 + 16


def per_device(density, right_side, pressure_guess):
    coarsest = pltpu.VMEM((64, 8, 128), F32)
    return pl.pallas_call(
        kernel,
        out_shape=jax.ShapeDtypeStruct(density.shape, F32),
        in_specs=[pl.BlockSpec(memory_space=pl.ANY)] * 3,
        out_specs=pl.BlockSpec(memory_space=pltpu.VMEM),
        scratch_shapes=[
            *level_scratch(4, 32, 512),
            *level_scratch(2, 16, 256),
            *level_scratch(1, 8, 128),
            pltpu.VMEM((2, 3, 4, 512), F32),
            pltpu.VMEM((2, 3, 4, 512), F32),
            pltpu.VMEM((2, 2, 128), F32),
            pltpu.VMEM((4, 2, 4, 2, 128), F32),
            pltpu.VMEM((4, 2, 4, 2, 128), F32),
            pltpu.VMEM((2, 4, 8, 128), F32),
            pltpu.VMEM((16, 4, 8, 128), F32),
            pltpu.VMEM((16, 4, 8, 128), F32),
            pltpu.VMEM((66, 8, 128), F32),
            coarsest, coarsest, pltpu.VMEM((65, 8, 128), F32), coarsest,
            pltpu.VMEM((66, 8, 128), F32), coarsest, coarsest, pltpu.VMEM((68, 8, 128), F32),
            pltpu.VMEM((8, 256), F32),
            pltpu.SemaphoreType.DMA((3,)),
            pltpu.SemaphoreType.DMA((COPIES,)),
            pltpu.SemaphoreType.DMA((COPIES,)),
        ],
        compiler_params=pltpu.CompilerParams(
            collective_id=0, has_side_effects=True, vmem_limit_bytes=32 * 1024 * 1024
        ),
        cost_estimate=pl.CostEstimate(flops=20_000_000, bytes_accessed=1 << 20, transcendentals=0),
    )(density, right_side, pressure_guess)


def solution(mesh):
    spec = P("gz", "gy", None)
    return jax.shard_map(per_device, mesh=mesh, in_specs=(spec, spec, spec), out_specs=spec, check_vma=False)
```

```python
import functools

import jax
import jax.numpy as jnp
from jax import lax
from jax.experimental import pallas as pl
from jax.experimental.pallas import tpu as pltpu
from jax.sharding import PartitionSpec as P

MESH = pl.DeviceIdType.MESH
SWEEPS = 8
OMEGA = 0.8
F32 = jnp.float32
PAD = 8


def dot(a, b):
    return jnp.dot(a, b, precision=lax.Precision.HIGHEST, preferred_element_type=F32)


def twice_inverse(total):
    guess = pltpu.reciprocal(total, approx=True)
    return guess * (4.0 - 2.0 * total * guess)


def iota(shape, axis):
    return lax.broadcasted_iota(jnp.int32, shape, axis)


def pair_matrix(fine):
    rows, cols = iota((fine, fine // 2), 0), iota((fine, fine // 2), 1)
    return jnp.where(rows // 2 == cols, 1.0, 0.0).astype(F32)


def spread_matrix(coarse):
    rows, cols = iota((coarse, 2 * coarse), 0), iota((coarse, 2 * coarse), 1)
    parent = cols // 2
    near = parent + 2 * (cols % 2) - 1
    return (jnp.where(rows == parent, 0.75, 0.0) + jnp.where(rows == near, 0.25, 0.0)).astype(F32)


def padded_spread_matrix(coarse):
    shape = (2 * coarse + 2 * PAD, coarse + 2 * PAD)
    rows, cols = iota(shape, 0), iota(shape, 1)
    parent = rows // 2 + PAD // 2
    near = parent + 2 * (rows % 2) - 1
    return (jnp.where(cols == parent, 0.75, 0.0) + jnp.where(cols == near, 0.25, 0.0)).astype(F32)


class Level:
    def __init__(self, shape, chunk, rho, bx, by, bz, dg, idg):
        self.planes, self.rows, self.cols = shape
        self.chunk = chunk
        self.rho, self.bx, self.by, self.bz, self.dg, self.idg = rho, bx, by, bz, dg, idg

    def chunks(self):
        return [(r, self.chunk) for r in range(0, self.rows, self.chunk)]

    def faces_x(self, plane):
        n = self.cols
        for r, m in self.chunks():
            rho = self.rho[plane + 1, PAD + r : PAD + r + m, :]
            lane = iota((m, n), 1)
            low = twice_inverse(rho + jnp.where(lane == 0, rho, pltpu.roll(rho, 1, 1)))
            high = jnp.where(lane == n - 1, twice_inverse(rho + rho), pltpu.roll(low, n - 1, 1))
            self.dg[plane, r : r + m, :] = low + high
            self.bx[plane, r : r + m, :] = jnp.where(lane == 0, 0.0, low)

    def faces_y(self, plane):
        for r, m in self.chunks():
            low = self.rho[plane + 1, PAD - 1 + r : PAD - 1 + r + m, :]
            high = self.rho[plane + 1, PAD + r : PAD + r + m, :]
            self.by[plane, r : r + m, :] = twice_inverse(low + high)
        end = PAD + self.rows
        low = self.rho[plane + 1, end - 1 : end, :]
        high = self.rho[plane + 1, end : end + 1, :]
        self.by[plane, self.rows : self.rows + 1, :] = twice_inverse(low + high)

    def faces_z(self, face):
        for r, m in self.chunks():
            low = self.rho[face, PAD + r : PAD + r + m, :]
            high = self.rho[face + 1, PAD + r : PAD + r + m, :]
            self.bz[face, r : r + m, :] = twice_inverse(low + high)

    def diagonal(self, plane):
        for r, m in self.chunks():
            total = self.dg[plane, r : r + m, :]
            total = total + self.by[plane, r : r + m, :] + self.by[plane, r + 1 : r + 1 + m, :]
            total = total + self.bz[plane, r : r + m, :] + self.bz[plane + 1, r : r + m, :]
            self.dg[plane, r : r + m, :] = total
            self.idg[plane, r : r + m, :] = (0.5 * OMEGA) * twice_inverse(total)

    def mask_y(self, plane, faces):
        for row, factor in faces:
            self.by[plane, row : row + 1, :] = self.by[plane, row : row + 1, :] * factor

    def mask_z(self, faces):
        for face, factor in faces:
            self.bz[face] = self.bz[face] * factor

    def neighbours(self, val, plane, r, m):
        n = self.cols
        rows = slice(PAD + r, PAD + r + m)
        here = val[plane + 1, rows, :]
        bx = self.bx[plane, r : r + m, :]
        total = self.bz[plane, r : r + m, :] * val[plane, rows, :]
        total = total + self.bz[plane + 1, r : r + m, :] * val[plane + 2, rows, :]
        total = total + self.by[plane, r : r + m, :] * val[plane + 1, PAD - 1 + r : PAD - 1 + r + m, :]
        total = total + self.by[plane, r + 1 : r + 1 + m, :] * val[plane + 1, PAD + 1 + r : PAD + 1 + r + m, :]
        total = total + bx * pltpu.roll(here, 1, 1)
        total = total + pltpu.roll(bx * here, n - 1, 1)
        return here, total


def kernel(
    dens_in, right_in, guess_in, out,
    rho0, val0, smo0, src0, res0, bx0, by0, bz0, dg0, idg0,
    rho1, pair1, bx1, by1, bz1, dg1, idg1,
    rho2, pair2, bx2, by2, bz2, dg2, idg2,
    rows_out, rows_in, message, inbox_dens, inbox_src, tile, wide_dens, wide_src,
    rho3, bx3, by3, bz3, dg3, dir3, res3, img3, cor3, pair_tmp,
    local_sem, send_sem, recv_sem,
):
    gz, gy = lax.axis_index("gz"), lax.axis_index("gy")
    nz, ny = 128, 4
    core, ypos, xpos, zhi = gz % 2, (gz // 2) % 4, (gz // 8) % 4, gz // 32
    zpos = zhi * 4 + gy

    def gz_of(zh, x, y, c):
        return ((zh * 4 + x) * 4 + y) * 2 + c

    up_z, down_z = (gz + 1) % nz, (gz + nz - 1) % nz
    up_y, down_y = (gy + 1) % ny, (gy + ny - 1) % ny
    column = []
    for d in range(16):
        for k in range(2):
            if d or k:
                z = (zpos + d) % 16
                column.append((gz_of(z // 4, xpos, ypos, (core + k) % 2), z % 4))
    layer = []
    for i in range(4):
        for j in range(4):
            if i or j:
                layer.append((gz_of(zhi, (xpos + i) % 4, (ypos + j) % 4, core), gy))
    faces = [(up_z, gy), (down_z, gy), (gz, up_y), (gz, down_y)]
    around = []
    for dz in (1, -1, 2, -2, 3, -3):
        for dy in (0, 1, -1):
            around.append((dz, dy, ((gz + dz + nz) % nz, (gy + dy + ny) % ny)))
    corners = [(dz, dy, device) for dz, dy, device in around if abs(dz) == 1 and dy]
    greeted = faces[2:] + [device for _, _, device in around] + column + layer

    barrier = pltpu.get_barrier_semaphore()
    for device in greeted:
        pl.semaphore_signal(barrier, inc=1, device_id=device, device_id_type=MESH)

    local = []
    for i, (source, target) in enumerate(
        ((dens_in, rho0.at[1:5, 8:40, :]), (guess_in, val0.at[1:5, 8:40, :]), (right_in, src0))
    ):
        copy = pltpu.make_async_copy(source, target, local_sem.at[i])
        copy.start()
        local.append(copy)

    count = [0]

    def send(source, target, device):
        i = count[0]
        count[0] = i + 1
        copy = pltpu.make_async_remote_copy(
            src_ref=source, dst_ref=target, send_sem=send_sem.at[i], recv_sem=recv_sem.at[i],
            device_id=device, device_id_type=MESH,
        )
        copy.start()
        return copy

    def wait_recv(copies):
        for copy in copies:
            copy.wait_recv()

    def wait_send(copies):
        for copy in copies:
            copy.wait_send()

    fine = Level((4, 32, 512), 8, rho0, bx0, by0, bz0, dg0, idg0)
    middle = Level((4, 32, 256), 16, rho1, bx1, by1, bz1, dg1, idg1)
    coarse = Level((5, 24, 128), 24, rho2, bx2, by2, bz2, dg2, idg2)
    val1, src1, val2, src2 = pair1.at[0], pair1.at[1], pair2.at[0], pair2.at[1]

    z_low = jnp.where(gz > 0, 1.0, 0.0).astype(F32)
    z_high = jnp.where(gz < nz - 1, 1.0, 0.0).astype(F32)
    y_low = jnp.where(gy > 0, 1.0, 0.0).astype(F32)
    y_high = jnp.where(gy < ny - 1, 1.0, 0.0).astype(F32)

    pair_x0, pair_x1 = pair_matrix(512), pair_matrix(256)
    pair_y0 = jnp.where(iota((16, 32), 1) // 2 == iota((16, 32), 0), 0.125, 0.0).astype(F32)
    pair_y1 = jnp.where(iota((8, 16), 1) // 2 == iota((8, 16), 0), 0.125, 0.0).astype(F32)

    def restrict0(read):
        return [dot(pair_y0, dot(read(2 * k) + read(2 * k + 1), pair_x0)) for k in range(2)]

    def restrict1(read):
        return dot(pair_y1, dot(read(0) + read(1), pair_x1))

    half_rows, half_cols = iota((128, 256), 0), iota((128, 256), 1)
    to_halves = jnp.where((half_cols % 64 == half_rows // 2) & ((half_cols < 64) | (half_cols >= 192)), 0.125, 0.0).astype(F32)

    def pack_message(field, value):
        pair_tmp[...] = dot(value, to_halves)
        for r in range(2):
            t = 4 * r
            message[field, r : r + 1, :] = (
                pair_tmp[t : t + 1, 0:128] + pair_tmp[t + 1 : t + 2, 0:128]
                + pair_tmp[t + 2 : t + 3, 128:256] + pair_tmp[t + 3 : t + 4, 128:256]
            )

    def gather_column(field, inbox):
        inbox[zhi, core, gy] = message[field]
        return [send(message.at[field], inbox.at[zhi, core, gy], device) for device in column]

    def gather_layer(field, inbox, wide):
        for zh in range(4):
            for y in range(4):
                tile[field, zh, 2 * y : 2 * y + 2, :] = inbox[zh, 0, y] + inbox[zh, 1, y]
        slot = xpos * 4 + ypos
        wide[slot] = tile[field]
        return [send(tile.at[field], wide.at[slot], device) for device in layer]

    local[0].wait()
    own1 = restrict0(lambda k: rho0[k + 1, 8:40, :])
    for k in range(2):
        rho1[k + 2, 16:32, :] = own1[k]
    own2 = restrict1(lambda k: own1[k])
    rho2[3, 16:24, :] = own2
    pack_message(0, own2)
    local[1].wait()
    for k in range(4):
        for f, ref in ((0, rho0), (1, val0)):
            rows_out[0, f, k : k + 1, :] = ref[k + 1, 39:40, :]
            rows_out[1, f, k : k + 1, :] = ref[k + 1, 8:9, :]

    pl.semaphore_wait(barrier, len(greeted))

    z_dens = [
        send(rho0.at[4, 8:40, :], rho0.at[0, 8:40, :], faces[0]),
        send(rho0.at[1, 8:40, :], rho0.at[5, 8:40, :], faces[1]),
    ]
    z_vals = [
        send(val0.at[4, 8:40, :], val0.at[0, 8:40, :], faces[0]),
        send(val0.at[1, 8:40, :], val0.at[5, 8:40, :], faces[1]),
    ]
    y_both = [
        send(rows_out.at[0, 0:2], rows_in.at[0, 0:2], faces[2]),
        send(rows_out.at[1, 0:2], rows_in.at[1, 0:2], faces[3]),
    ]

    rows1 = {0: (slice(16, 32), slice(16, 32)), 1: (slice(24, 32), slice(8, 16)), -1: (slice(16, 24), slice(32, 40))}
    rows2 = {dy: (slice(16, 24), slice(16 - 8 * dy, 24 - 8 * dy)) for dy in (0, 1, -1)}
    y_ways = ((1, faces[2]), (-1, faces[3]))
    z_ways = ((1, faces[0]), (-1, faces[1]))

    def planes1(dz):
        return slice(2 - 2 * dz, 4 - 2 * dz)

    dens1_copies = [
        send(rho1.at[2:4, 16:32, :], rho1.at[planes1(dz), 16:32, :], device) for dz, device in z_ways
    ]
    for dy, device in y_ways:
        source, target = rows1[dy]
        dens1_copies.append(send(rho1.at[2:4, source, :], rho1.at[2:4, target, :], device))
    for dz, dy, device in corners:
        source, target = rows1[dy]
        dens1_copies.append(send(rho1.at[2:4, source, :], rho1.at[planes1(dz), target, :], device))
    column_dens = gather_column(0, inbox_dens)

    def fill_y(ref, planes, rows, first):
        last = first + rows - 1
        for k in planes:
            ref[k, first - 1 : first, :] = jnp.where(gy == 0, ref[k, first : first + 1, :], ref[k, first - 1 : first, :])
            ref[k, last + 1 : last + 2, :] = jnp.where(
                gy == ny - 1, ref[k, last : last + 1, :], ref[k, last + 1 : last + 2, :]
            )

    def fill_z(ref, own, planes, rows, reach):
        for i in range(reach):
            low, high = own - 1 - i * planes, own + planes + i * planes
            ref[low, rows, :] = jnp.where(gz == i, ref[low + 1, rows, :], ref[low, rows, :])
            ref[high, rows, :] = jnp.where(gz == nz - 1 - i, ref[high - 1, rows, :], ref[high, rows, :])

    for k in range(4):
        fine.faces_x(k)
    for face in (1, 2, 3):
        fine.faces_z(face)
    wait_recv(y_both)
    for k in range(4):
        for f, ref in ((0, rho0), (1, val0)):
            ref[k + 1, 7:8, :] = rows_in[0, f, k : k + 1, :]
            ref[k + 1, 40:41, :] = rows_in[1, f, k : k + 1, :]
    fill_y(rho0, range(1, 5), 32, 8)
    for k in range(4):
        fine.faces_y(k)
    local[2].wait()

    def smooth(plane):
        for r, m in fine.chunks():
            here, near = fine.neighbours(val0, plane, r, m)
            smo0[plane + 1, 8 + r : 8 + r + m, :] = (1.0 - OMEGA) * here + (
                src0[plane, r : r + m, :] + near
            ) * fine.idg[plane, r : r + m, :]

    for k in (1, 2):
        fine.diagonal(k)
        fine.mask_y(k, ((0, y_low), (32, y_high)))
        smooth(k)
    wait_recv(z_dens)
    fill_z(rho0, 1, 4, slice(8, 40), 1)
    for face in (0, 4):
        fine.faces_z(face)
    for k in (0, 3):
        fine.diagonal(k)
        fine.mask_y(k, ((0, y_low), (32, y_high)))
    fine.mask_z(((0, z_low), (4, z_high)))
    wait_recv(z_vals)
    smooth(3)
    z_smooth = [send(smo0.at[4, 8:40, :], smo0.at[0, 8:40, :], faces[0])]
    smooth(0)
    z_smooth.append(send(smo0.at[1, 8:40, :], smo0.at[5, 8:40, :], faces[1]))
    for k in range(4):
        rows_out[0, 2, k : k + 1, :] = smo0[k + 1, 39:40, :]
        rows_out[1, 2, k : k + 1, :] = smo0[k + 1, 8:9, :]
    y_smooth = [
        send(rows_out.at[0, 2], rows_in.at[0, 2], faces[2]),
        send(rows_out.at[1, 2], rows_in.at[1, 2], faces[3]),
    ]

    dens2_copies = [
        send(rho2.at[3, 16:24, :], rho2.at[3, rows2[dy][1], :], device) for dy, device in y_ways
    ]
    for dz, dy, device in around:
        dens2_copies.append(send(rho2.at[3, 16:24, :], rho2.at[3 - dz, rows2[dy][1], :], device))

    def coefficients(level, z_faces):
        for k in range(level.planes):
            level.faces_x(k)
            level.faces_y(k)
        for k in range(level.planes + 1):
            level.faces_z(k)
        for k in range(level.planes):
            level.diagonal(k)
            level.mask_y(k, ((8, y_low), (level.rows - 8, y_high)))
        level.mask_z(z_faces)

    wait_recv(dens1_copies)
    fill_y(rho1, range(6), 16, 16)
    fill_z(rho1, 2, 2, slice(8, 40), 1)
    coefficients(middle, ((1, z_low), (3, z_high)))
    wait_recv(column_dens)
    layer_dens = gather_layer(0, inbox_dens, wide_dens)

    wait_recv(y_smooth)
    for k in range(4):
        smo0[k + 1, 7:8, :] = rows_in[0, 2, k : k + 1, :]
        smo0[k + 1, 40:41, :] = rows_in[1, 2, k : k + 1, :]

    def residual(plane):
        for r, m in fine.chunks():
            here, near = fine.neighbours(smo0, plane, r, m)
            res0[plane, r : r + m, :] = src0[plane, r : r + m, :] - fine.dg[plane, r : r + m, :] * here + near

    for k in (1, 2):
        residual(k)
    wait_recv(z_smooth)
    for k in (0, 3):
        residual(k)

    source1 = restrict0(lambda k: res0[k])
    for k in range(2):
        src1[k + 2, 16:32, :] = source1[k]
        val1[k + 2, 16:32, :] = 4.0 * source1[k] * idg1[k + 1, 8:24, :]
    copies1 = [
        send(val1.at[3, 16:32, :], val1.at[1, 16:32, :], faces[0]),
        send(val1.at[2, 16:32, :], val1.at[4, 16:32, :], faces[1]),
    ]
    for dy, device in y_ways:
        source, target = rows1[dy]
        copies1.append(send(val1.at[2:4, source, :], val1.at[2:4, target, :], device))

    wait_recv(dens2_copies)
    fill_y(rho2, range(7), 8, 16)
    fill_z(rho2, 3, 1, slice(8, 32), 3)

    def inside_z(face):
        at = gz + face - 2
        return jnp.where((at > 0) & (at < nz), 1.0, 0.0).astype(F32)

    coefficients(coarse, [(face, inside_z(face)) for face in range(6)])

    wait_recv(layer_dens)
    lane, sub = iota((8, 128), 1), iota((8, 128), 0)
    right_half = lane >= 64
    first_x, last_x = (lane % 64) == 0, (lane % 64) == 63
    first_y, last_y = (lane < 64) & (sub == 0), (lane >= 64) & (sub == 7)

    def lower_y(v):
        q = pltpu.roll(v, 64, 1)
        return jnp.where(right_half, q, pltpu.roll(q, 1, 0))

    def upper_y(v):
        q = pltpu.roll(v, 64, 1)
        return jnp.where(right_half, pltpu.roll(q, 7, 0), q)

    scale3 = 0.015625
    for zh in range(4):
        for s in range(16):
            rho3[1 + 16 * zh + s] = wide_dens[s, zh]
    rho3[0] = rho3[1]
    rho3[65] = rho3[64]

    def face3(k, _):
        bz3[k] = scale3 * twice_inverse(rho3[k] + rho3[k + 1])
        return 0

    lax.fori_loop(0, 65, face3, 0)

    def coef3(k, _):
        rho = rho3[k + 1]
        edge = twice_inverse(rho + rho)
        low = twice_inverse(rho + jnp.where(first_x, rho, pltpu.roll(rho, 1, 1)))
        total = low + jnp.where(last_x, edge, pltpu.roll(low, 127, 1))
        bx3[k] = jnp.where(first_x, 0.0, scale3 * low)
        low = twice_inverse(rho + jnp.where(first_y, rho, lower_y(rho)))
        total = total + low + jnp.where(last_y, edge, upper_y(low))
        by3[k] = jnp.where(first_y, 0.0, scale3 * low)
        dg3[k] = scale3 * total + bz3[k] + bz3[k + 1]
        return 0

    lax.fori_loop(0, 64, coef3, 0, unroll=4)

    wait_recv(copies1)

    def residual1(k):
        here, near = middle.neighbours(val1, k + 1, 8, 16)
        return (1.0 - OMEGA) * source1[k] + 0.25 * near

    source2 = restrict1(residual1)
    src2[3, 16:24, :] = source2
    val2[3, 16:24, :] = 16.0 * source2 * idg2[2, 8:16, :]
    copies2 = [send(val2.at[3, 16:24, :], val2.at[3, rows2[dy][1], :], device) for dy, device in y_ways]
    for dz, device in z_ways:
        copies2.append(send(val2.at[3, 16:24, :], val2.at[3 - dz, 16:24, :], device))
    wait_recv(copies2)
    here, near = coarse.neighbours(val2, 2, 8, 8)
    pack_message(1, (1.0 - OMEGA) * source2 + 0.0625 * near)
    column_src = gather_column(1, inbox_src)

    more1 = [
        send(val1.at[2, 16:32, :], val1.at[0, 16:32, :], faces[0]),
        send(val1.at[3, 16:32, :], val1.at[5, 16:32, :], faces[1]),
    ]
    for dz, device in z_ways:
        more1.append(send(src1.at[2:4, 16:32, :], src1.at[planes1(dz), 16:32, :], device))
    for dy, device in y_ways:
        source, target = rows1[dy]
        more1.append(send(src1.at[2:4, source, :], src1.at[2:4, target, :], device))
    for dz, dy, device in corners:
        source, target = rows1[dy]
        more1.append(send(pair1.at[:, 2:4, source, :], pair1.at[:, planes1(dz), target, :], device))
    more2 = [send(src2.at[3, 16:24, :], src2.at[3, rows2[dy][1], :], device) for dy, device in y_ways]
    for dz, dy, device in around:
        if abs(dz) == 1 and dy == 0:
            more2.append(send(src2.at[3, 16:24, :], src2.at[3 - dz, 16:24, :], device))
        else:
            more2.append(send(pair2.at[:, 3, 16:24, :], pair2.at[:, 3 - dz, rows2[dy][1], :], device))

    wait_recv(column_src)
    layer_src = gather_layer(1, inbox_src, wide_src)
    wait_recv(layer_src)

    zero_plane = jnp.zeros((8, 128), F32)
    dir3[0] = zero_plane
    dir3[65] = zero_plane
    for k in (0, 1, 66, 67):
        cor3[k] = zero_plane
    total = zero_plane
    for zh in range(4):
        for s in range(16):
            v = wide_src[s, zh]
            k = 16 * zh + s
            dir3[k + 1] = v
            res3[k] = v
            cor3[k + 2] = zero_plane
            total = total + v * v

    def whole(v):
        return jnp.sum(jnp.sum(v, axis=0, keepdims=True), axis=1, keepdims=True)

    def sweep(step, norm):
        def apply(k, acc):
            v = dir3[k + 1]
            bx, by = bx3[k], by3[k]
            image = dg3[k] * v - bz3[k] * dir3[k] - bz3[k + 1] * dir3[k + 2]
            image = image - by * lower_y(v) - upper_y(by * v)
            image = image - bx * pltpu.roll(v, 1, 1) - pltpu.roll(bx * v, 127, 1)
            img3[k] = image
            return acc + v * image

        bottom = whole(lax.fori_loop(0, 64, apply, zero_plane, unroll=16))
        alpha = norm / bottom

        def advance(k, acc):
            cor3[k + 2] = cor3[k + 2] + alpha * dir3[k + 1]
            r = res3[k] - alpha * img3[k]
            res3[k] = r
            return acc + r * r

        norm_next = whole(lax.fori_loop(0, 64, advance, zero_plane, unroll=16))
        beta = norm_next / norm

        def turn(k, _):
            dir3[k + 1] = res3[k] + beta * dir3[k + 1]
            return 0

        lax.fori_loop(0, 64, turn, 0, unroll=16)
        return norm_next

    lax.fori_loop(0, SWEEPS, sweep, whole(total))

    spread_rows, spread_cols = iota((128, 256), 0), iota((128, 256), 1)
    fine_x = spread_cols % 128
    parent = fine_x // 2
    near = parent + 2 * (fine_x % 2) - 1
    half = spread_cols // 128
    inside = (near >= 0) & (near < 64)
    from_halves = (
        jnp.where(spread_rows == parent + 64 * half, 0.75, 0.0)
        + jnp.where((spread_rows == near + 64 * half) & inside, 0.25, 0.0)
    ).astype(F32)
    row_at, col_at = iota((24, 16), 0) + 8 * gy - 8, iota((24, 16), 1)
    coarse_y = 2 * (col_at % 8) + col_at // 8
    row_up = row_at + 8
    parent_y = row_up // 2 - 4
    near_y = parent_y + 2 * (row_up % 2) - 1
    rows_from = (
        jnp.where(coarse_y == parent_y, 0.75, 0.0) + jnp.where(coarse_y == near_y, 0.25, 0.0)
    ).astype(F32)
    mixed = []
    for d in range(-3, 4):
        plane = gz + d + 4
        index = plane // 2
        other = index + 2 * (plane % 2) - 1
        mixed.append(0.75 * cor3[index] + 0.25 * cor3[other])
    x_done = dot(jnp.concatenate(mixed, axis=0), from_halves)
    wait_recv(more1 + more2)
    wait_send(copies1 + copies2 + more1 + more2 + z_smooth)
    for k in range(7):
        own = x_done[8 * k : 8 * k + 8]
        stacked = jnp.concatenate([own[:, 0:128], own[:, 128:256]], axis=0)
        val2[k, 8:32, :] = val2[k, 8:32, :] + dot(rows_from, stacked)

    def in_grid(shape, first_row, rows, plane, planes):
        row = iota(shape, 0)
        at = row + first_row
        good = (row > 0) & (row < shape[0] - 1) & (at >= 0) & (at < rows)
        return good & (plane >= 0) & (plane < planes)

    ups = []
    for k in range(5):
        here, near = coarse.neighbours(val2, k, 0, 24)
        up = (1.0 - OMEGA) * here + (16.0 * src2[k + 1, 8:32, :] + near) * idg2[k]
        ups.append(jnp.where(in_grid((24, 128), 8 * gy - 8, 8 * ny, gz + k - 2, nz), up, 0.0))

    spread_x1, spread_x0 = spread_matrix(128), spread_matrix(256)
    spread_y1, spread_y0 = padded_spread_matrix(8), padded_spread_matrix(16)

    def prolong(ups, target, first, rows, spread_x, spread_y):
        height = ups[0].shape[0]
        x_done = dot(jnp.concatenate(ups, axis=0), spread_x)
        wide = [dot(spread_y, x_done[height * k : height * (k + 1)]) for k in range(len(ups))]
        for k in range(6):
            parent_z = (k + first) // 2
            near_z = parent_z + 2 * ((k + first) % 2) - 1
            target[k, rows, :] = target[k, rows, :] + 0.75 * wide[parent_z] + 0.25 * wide[near_z]

    prolong(ups, val1, 2, slice(8, 40), spread_x1, spread_y1)
    ups = []
    for k in range(4):
        parts = []
        for r, m in middle.chunks():
            here, near = middle.neighbours(val1, k, r, m)
            source = src1[k + 1, 8 + r : 8 + r + m, :]
            parts.append((1.0 - OMEGA) * here + (4.0 * source + near) * idg1[k, r : r + m, :])
        up = jnp.concatenate(parts, axis=0)
        ups.append(jnp.where(in_grid((32, 256), 16 * gy - 8, 16 * ny, 2 * gz + k - 1, 2 * nz), up, 0.0))
    prolong(ups, smo0, 1, slice(0, 48), spread_x0, spread_y0)
    for k in range(4):
        for r, m in fine.chunks():
            here, near = fine.neighbours(smo0, k, r, m)
            out[k, r : r + m, :] = (1.0 - OMEGA) * here + (src0[k, r : r + m, :] + near) * fine.idg[k, r : r + m, :]

    wait_send(
        z_dens + z_vals + y_both + dens1_copies + dens2_copies + column_dens + y_smooth + layer_dens
        + column_src + layer_src
    )


def coefficient_scratch(planes, rows, cols):
    own = pltpu.VMEM((planes, rows, cols), F32)
    return [own, pltpu.VMEM((planes, rows + 8, cols), F32), pltpu.VMEM((planes + 1, rows, cols), F32), own, own]


COPIES = 6 + 8 + 20 + 4 + 14 + 24 + 62 + 30


def per_device(density, right_side, pressure_guess):
    coarsest = pltpu.VMEM((64, 8, 128), F32)
    return pl.pallas_call(
        kernel,
        out_shape=jax.ShapeDtypeStruct(density.shape, F32),
        in_specs=[pl.BlockSpec(memory_space=pl.ANY)] * 3,
        out_specs=pl.BlockSpec(memory_space=pltpu.VMEM),
        scratch_shapes=[
            *[pltpu.VMEM((6, 48, 512), F32)] * 3,
            *[pltpu.VMEM((4, 32, 512), F32)] * 2,
            *coefficient_scratch(4, 32, 512),
            pltpu.VMEM((6, 48, 256), F32),
            pltpu.VMEM((2, 6, 48, 256), F32),
            *coefficient_scratch(4, 32, 256),
            pltpu.VMEM((7, 40, 128), F32),
            pltpu.VMEM((2, 7, 40, 128), F32),
            *coefficient_scratch(5, 24, 128),
            pltpu.VMEM((2, 3, 4, 512), F32),
            pltpu.VMEM((2, 3, 4, 512), F32),
            pltpu.VMEM((2, 2, 128), F32),
            pltpu.VMEM((4, 2, 4, 2, 128), F32),
            pltpu.VMEM((4, 2, 4, 2, 128), F32),
            pltpu.VMEM((2, 4, 8, 128), F32),
            pltpu.VMEM((16, 4, 8, 128), F32),
            pltpu.VMEM((16, 4, 8, 128), F32),
            pltpu.VMEM((66, 8, 128), F32),
            coarsest, coarsest, pltpu.VMEM((65, 8, 128), F32), coarsest,
            pltpu.VMEM((66, 8, 128), F32), coarsest, coarsest, pltpu.VMEM((68, 8, 128), F32),
            pltpu.VMEM((8, 256), F32),
            pltpu.SemaphoreType.DMA((3,)),
            pltpu.SemaphoreType.DMA((COPIES,)),
            pltpu.SemaphoreType.DMA((COPIES,)),
        ],
        compiler_params=pltpu.CompilerParams(
            collective_id=0, has_side_effects=True, vmem_limit_bytes=32 * 1024 * 1024
        ),
        cost_estimate=pl.CostEstimate(flops=20_000_000, bytes_accessed=1 << 20, transcendentals=0),
    )(density, right_side, pressure_guess)


def solution(mesh):
    spec = P("gz", "gy", None)
    return jax.shard_map(per_device, mesh=mesh, in_specs=(spec, spec, spec), out_specs=spec, check_vma=False)
```

```python
import functools

import jax
import jax.numpy as jnp
from jax import lax
from jax.experimental import pallas as pl
from jax.experimental.pallas import tpu as pltpu
from jax.sharding import PartitionSpec as P

MESH = pl.DeviceIdType.MESH
SWEEPS = 8
OMEGA = 0.8
F32 = jnp.float32
PAD = 8


def dot(values, weights):
    rows = values.shape[0]
    if rows % 16:
        values = jnp.concatenate([values, jnp.zeros((16 - rows % 16, values.shape[1]), F32)], axis=0)
    total = values.shape[0]
    first = values.astype(jnp.bfloat16).astype(F32)
    rest = values - first
    second = rest.astype(jnp.bfloat16).astype(F32)
    parts = jnp.concatenate([first, second, rest - second], axis=0).astype(jnp.bfloat16)
    out = jnp.dot(parts, weights, preferred_element_type=F32)
    return (out[0:total] + out[total : 2 * total] + out[2 * total :])[0:rows]


def twice_inverse(total):
    guess = pltpu.reciprocal(total, approx=True)
    return guess * (4.0 - 2.0 * total * guess)


def iota(shape, axis):
    return lax.broadcasted_iota(jnp.int32, shape, axis)


def pair_matrix():
    rows, cols = iota((256, 128), 0), iota((256, 128), 1)
    return jnp.where(rows // 2 == cols, 0.125, 0.0).astype(jnp.bfloat16)


def spread_matrix(coarse):
    rows, cols = iota((coarse, 2 * coarse), 0), iota((coarse, 2 * coarse), 1)
    parent = cols // 2
    near = parent + 2 * (cols % 2) - 1
    return (jnp.where(rows == parent, 0.75, 0.0) + jnp.where(rows == near, 0.25, 0.0)).astype(jnp.bfloat16)


class Level:
    def __init__(self, shape, chunk, rho, bx, by, bz, dg, idg):
        self.planes, self.rows, self.cols = shape
        self.chunk = chunk
        self.rho, self.bx, self.by, self.bz, self.dg, self.idg = rho, bx, by, bz, dg, idg

    def chunks(self):
        return [(r, self.chunk) for r in range(0, self.rows, self.chunk)]

    def faces_x(self, plane):
        n = self.cols
        for r, m in self.chunks():
            rho = self.rho[plane + 1, PAD + r : PAD + r + m, :]
            lane = iota((m, n), 1)
            low = twice_inverse(rho + jnp.where(lane == 0, rho, pltpu.roll(rho, 1, 1)))
            high = jnp.where(lane == n - 1, twice_inverse(rho + rho), pltpu.roll(low, n - 1, 1))
            self.dg[plane, r : r + m, :] = low + high
            self.bx[plane, r : r + m, :] = jnp.where(lane == 0, 0.0, low)

    def faces_y(self, plane):
        for r, m in self.chunks():
            low = self.rho[plane + 1, PAD - 1 + r : PAD - 1 + r + m, :]
            high = self.rho[plane + 1, PAD + r : PAD + r + m, :]
            self.by[plane, r : r + m, :] = twice_inverse(low + high)
        end = PAD + self.rows
        low = self.rho[plane + 1, end - 1 : end, :]
        high = self.rho[plane + 1, end : end + 1, :]
        self.by[plane, self.rows : self.rows + 1, :] = twice_inverse(low + high)

    def faces_z(self, face):
        for r, m in self.chunks():
            low = self.rho[face, PAD + r : PAD + r + m, :]
            high = self.rho[face + 1, PAD + r : PAD + r + m, :]
            self.bz[face, r : r + m, :] = twice_inverse(low + high)

    def diagonal(self, plane):
        for r, m in self.chunks():
            total = self.dg[plane, r : r + m, :]
            total = total + self.by[plane, r : r + m, :] + self.by[plane, r + 1 : r + 1 + m, :]
            total = total + self.bz[plane, r : r + m, :] + self.bz[plane + 1, r : r + m, :]
            self.dg[plane, r : r + m, :] = total
            self.idg[plane, r : r + m, :] = (0.5 * OMEGA) * twice_inverse(total)

    def mask_y(self, plane, faces):
        for row, factor in faces:
            self.by[plane, row : row + 1, :] = self.by[plane, row : row + 1, :] * factor

    def mask_z(self, faces):
        for face, factor in faces:
            self.bz[face] = self.bz[face] * factor

    def neighbours(self, val, plane, r, m):
        n = self.cols
        rows = slice(PAD + r, PAD + r + m)
        here = val[plane + 1, rows, :]
        bx = self.bx[plane, r : r + m, :]
        total = self.bz[plane, r : r + m, :] * val[plane, rows, :]
        total = total + self.bz[plane + 1, r : r + m, :] * val[plane + 2, rows, :]
        total = total + self.by[plane, r : r + m, :] * val[plane + 1, PAD - 1 + r : PAD - 1 + r + m, :]
        total = total + self.by[plane, r + 1 : r + 1 + m, :] * val[plane + 1, PAD + 1 + r : PAD + 1 + r + m, :]
        total = total + bx * pltpu.roll(here, 1, 1)
        total = total + pltpu.roll(bx * here, n - 1, 1)
        return here, total


def kernel(
    dens_in, right_in, guess_in, out,
    rho0, val0, smo0, src0, res0, bx0, by0, bz0, dg0, idg0,
    rho1, pair1, near1, bx1, by1, bz1, dg1, idg1,
    rho2, pair2, bx2, by2, bz2, dg2, idg2,
    rows_out, rows_in, message, inbox_dens, inbox_src, tile, wide_dens, wide_src,
    rho3, bx3, by3, bz3, dg3, dir3, res3, img3, cor3, pair_tmp, pair_rows, fine_rows, result,
    far_smooth, face_rows, z_out, z_in, y_out, y_in, d_out, d_in, local_sem, out_sem, send_sem, recv_sem,
):
    gz, gy = lax.axis_index("gz"), lax.axis_index("gy")
    nz, ny = 128, 4
    core, ypos, xpos, zhi = gz % 2, (gz // 2) % 4, (gz // 8) % 4, gz // 32
    zpos = zhi * 4 + gy

    def gz_of(zh, x, y, c):
        return ((zh * 4 + x) * 4 + y) * 2 + c

    up_z, down_z = (gz + 1) % nz, (gz + nz - 1) % nz
    up_y, down_y = (gy + 1) % ny, (gy + ny - 1) % ny
    column = []
    for d in range(16):
        for k in range(2):
            if d or k:
                z = (zpos + d) % 16
                column.append((gz_of(z // 4, xpos, ypos, (core + k) % 2), z % 4))
    layer = []
    for i in range(4):
        for j in range(4):
            if i or j:
                layer.append((gz_of(zhi, (xpos + i) % 4, (ypos + j) % 4, core), gy))
    faces = [(up_z, gy), (down_z, gy), (gz, up_y), (gz, down_y)]
    around = []
    for dz in (1, -1, 2, -2, 3, -3):
        for dy in (0, 1, -1):
            around.append((dz, dy, ((gz + dz + nz) % nz, (gy + dy + ny) % ny)))
    corners = [(dz, dy, device) for dz, dy, device in around if abs(dz) == 1 and dy]
    greeted = faces[2:] + [device for _, _, device in around] + column + layer

    barrier = pltpu.get_barrier_semaphore()
    for device in greeted:
        pl.semaphore_signal(barrier, inc=1, device_id=device, device_id_type=MESH)

    local = []
    for i, (source, target) in enumerate(
        ((dens_in, rho0.at[1:5, 8:40, :]), (guess_in, val0.at[1:5, 8:40, :]), (right_in, src0))
    ):
        copy = pltpu.make_async_copy(source, target, local_sem.at[i])
        copy.start()
        local.append(copy)

    count = [0]

    def send(source, target, device):
        i = count[0]
        count[0] = i + 1
        copy = pltpu.make_async_remote_copy(
            src_ref=source, dst_ref=target, send_sem=send_sem.at[i], recv_sem=recv_sem.at[i],
            device_id=device, device_id_type=MESH,
        )
        copy.start()
        return copy

    def wait_recv(copies):
        for copy in copies:
            copy.wait_recv()

    def wait_send(copies):
        for copy in copies:
            copy.wait_send()

    fine = Level((4, 32, 512), 8, rho0, bx0, by0, bz0, dg0, idg0)
    middle = Level((4, 32, 256), 16, rho1, bx1, by1, bz1, dg1, idg1)
    coarse = Level((5, 24, 128), 24, rho2, bx2, by2, bz2, dg2, idg2)
    val1, src1, val2, src2 = pair1.at[0], pair1.at[1], pair2.at[0], pair2.at[1]

    z_low = jnp.where(gz > 0, 1.0, 0.0).astype(F32)
    z_high = jnp.where(gz < nz - 1, 1.0, 0.0).astype(F32)
    y_low = jnp.where(gy > 0, 1.0, 0.0).astype(F32)
    y_high = jnp.where(gy < ny - 1, 1.0, 0.0).astype(F32)

    pair_x = pair_matrix()

    def halve_x(blocks):
        rows = sum(block.shape[0] for block in blocks)
        summed = dot(jnp.concatenate([b[:, 0:256] for b in blocks] + [b[:, 256:512] for b in blocks], axis=0), pair_x)
        out, at = [], 0
        for block in blocks:
            n = block.shape[0]
            out.append((summed[at : at + n], summed[rows + at : rows + at + n]))
            at += n
        return out

    def halve_y(slot, value):
        n = value.shape[0]
        pair_rows[slot, 0:n, :] = value
        return pair_rows[slot, pl.ds(0, n // 2, stride=2), :] + pair_rows[slot, pl.ds(1, n // 2, stride=2), :]

    def halve_xy(blocks):
        return [
            jnp.concatenate([halve_y(2 * i, left), halve_y(2 * i + 1, right)], axis=1)
            for i, (left, right) in enumerate(halve_x(blocks))
        ]

    def restrict1(read):
        return halve_y(0, dot(read(0) + read(1), pair_x))

    half_rows, half_cols = iota((128, 256), 0), iota((128, 256), 1)
    to_halves = jnp.where((half_cols % 64 == half_rows // 2) & ((half_cols < 64) | (half_cols >= 192)), 0.125, 0.0).astype(jnp.bfloat16)

    def pack_message(field, value):
        pair_tmp[...] = dot(value, to_halves)
        for r in range(2):
            t = 4 * r
            message[field, r : r + 1, :] = (
                pair_tmp[t : t + 1, 0:128] + pair_tmp[t + 1 : t + 2, 0:128]
                + pair_tmp[t + 2 : t + 3, 128:256] + pair_tmp[t + 3 : t + 4, 128:256]
            )

    def gather_column(field, inbox):
        inbox[zhi, core, gy] = message[field]
        return [send(message.at[field], inbox.at[zhi, core, gy], device) for device in column]

    def gather_layer(field, inbox, wide):
        for zh in range(4):
            for y in range(4):
                tile[field, zh, 2 * y : 2 * y + 2, :] = inbox[zh, 0, y] + inbox[zh, 1, y]
        slot = xpos * 4 + ypos
        wide[slot] = tile[field]
        return [send(tile.at[field], wide.at[slot], device) for device in layer]

    local[0].wait()
    own1 = halve_xy([rho0[2 * k + 1, 8:40, :] + rho0[2 * k + 2, 8:40, :] for k in range(2)])
    for k in range(2):
        rho1[k + 2, 16:32, :] = own1[k]
    own2 = restrict1(lambda k: own1[k])
    rho2[3, 16:24, :] = own2
    pack_message(0, own2)
    local[1].wait()
    for k in range(4):
        for f, ref in ((0, rho0), (1, val0)):
            rows_out[0, f, k : k + 1, :] = ref[k + 1, 39:40, :]
            rows_out[1, f, k : k + 1, :] = ref[k + 1, 8:9, :]

    for k in (0, 5):
        smo0[k, 8:40, :] = jnp.zeros((32, 512), F32)
    for k in range(1, 5):
        smo0[k, 7:8, :] = jnp.zeros((1, 512), F32)
        smo0[k, 40:41, :] = jnp.zeros((1, 512), F32)

    pl.semaphore_wait(barrier, len(greeted))

    z_dens = [
        send(rho0.at[4, 8:40, :], rho0.at[0, 8:40, :], faces[0]),
        send(rho0.at[1, 8:40, :], rho0.at[5, 8:40, :], faces[1]),
    ]
    z_vals = [
        send(val0.at[4, 8:40, :], val0.at[0, 8:40, :], faces[0]),
        send(val0.at[1, 8:40, :], val0.at[5, 8:40, :], faces[1]),
    ]
    y_both = [
        send(rows_out.at[0, 0:2], rows_in.at[0, 0:2], faces[2]),
        send(rows_out.at[1, 0:2], rows_in.at[1, 0:2], faces[3]),
    ]

    rows1 = {0: (slice(16, 32), slice(16, 32)), 1: (slice(24, 32), slice(8, 16)), -1: (slice(16, 24), slice(32, 40))}
    rows2 = {dy: (slice(16, 24), slice(16 - 8 * dy, 24 - 8 * dy)) for dy in (0, 1, -1)}
    y_ways = ((1, faces[2]), (-1, faces[3]))
    z_ways = ((1, faces[0]), (-1, faces[1]))

    def planes1(dz):
        return slice(2 - 2 * dz, 4 - 2 * dz)

    dens1_copies = [
        send(rho1.at[2:4, 16:32, :], rho1.at[planes1(dz), 16:32, :], device) for dz, device in z_ways
    ]
    for dy, device in y_ways:
        source, target = rows1[dy]
        dens1_copies.append(send(rho1.at[2:4, source, :], rho1.at[2:4, target, :], device))
    for dz, dy, device in corners:
        source, target = rows1[dy]
        dens1_copies.append(send(rho1.at[2:4, source, :], rho1.at[planes1(dz), target, :], device))
    column_dens = gather_column(0, inbox_dens)

    def fill_y(ref, planes, rows, first):
        last = first + rows - 1
        for k in planes:
            ref[k, first - 1 : first, :] = jnp.where(gy == 0, ref[k, first : first + 1, :], ref[k, first - 1 : first, :])
            ref[k, last + 1 : last + 2, :] = jnp.where(
                gy == ny - 1, ref[k, last : last + 1, :], ref[k, last + 1 : last + 2, :]
            )

    def fill_z(ref, own, planes, rows, reach):
        for i in range(reach):
            low, high = own - 1 - i * planes, own + planes + i * planes
            ref[low, rows, :] = jnp.where(gz == i, ref[low + 1, rows, :], ref[low, rows, :])
            ref[high, rows, :] = jnp.where(gz == nz - 1 - i, ref[high - 1, rows, :], ref[high, rows, :])

    for k in range(4):
        fine.faces_x(k)
    for face in (1, 2, 3):
        fine.faces_z(face)
    wait_recv(y_both)
    for k in range(4):
        for f, ref in ((0, rho0), (1, val0)):
            ref[k + 1, 7:8, :] = rows_in[0, f, k : k + 1, :]
            ref[k + 1, 40:41, :] = rows_in[1, f, k : k + 1, :]
    fill_y(rho0, range(1, 5), 32, 8)
    for k in range(4):
        fine.faces_y(k)
    local[2].wait()

    def smooth(plane):
        for r, m in fine.chunks():
            here, near = fine.neighbours(val0, plane, r, m)
            smo0[plane + 1, 8 + r : 8 + r + m, :] = (1.0 - OMEGA) * here + (
                src0[plane, r : r + m, :] + near
            ) * fine.idg[plane, r : r + m, :]

    for k in (1, 2):
        fine.diagonal(k)
        fine.mask_y(k, ((0, y_low), (32, y_high)))
        smooth(k)
    wait_recv(z_dens)
    fill_z(rho0, 1, 4, slice(8, 40), 1)
    for face in (0, 4):
        fine.faces_z(face)
    for k in (0, 3):
        fine.diagonal(k)
        fine.mask_y(k, ((0, y_low), (32, y_high)))
    fine.mask_z(((0, z_low), (4, z_high)))
    wait_recv(z_vals)
    smooth(3)
    smooth(0)

    for plane in range(4):
        for r, m in fine.chunks():
            here, near = fine.neighbours(smo0, plane, r, m)
            res0[plane, r : r + m, :] = src0[plane, r : r + m, :] - dg0[plane, r : r + m, :] * here + near
    for way, (row, cell) in enumerate(((32, 39), (0, 8))):
        for k in range(2):
            lower = by0[2 * k, row : row + 1, :] * smo0[2 * k + 1, cell : cell + 1, :]
            upper = by0[2 * k + 1, row : row + 1, :] * smo0[2 * k + 2, cell : cell + 1, :]
            face_rows[2 * way + k : 2 * way + k + 1, :] = lower + upper
    blocks = halve_x(
        [res0[0] + res0[1], res0[2] + res0[3], bz0[4] * smo0[4, 8:40, :], bz0[0] * smo0[1, 8:40, :], face_rows[...]]
    )
    part0, part1, give_up, give_down = [
        jnp.concatenate([halve_y(2 * i, left), halve_y(2 * i + 1, right)], axis=1)
        for i, (left, right) in enumerate(blocks[:4])
    ]
    give_rows = jnp.concatenate(blocks[4], axis=1)
    parts = (part0, part1)
    z_out[0, 0] = give_up
    z_out[0, 1] = part1
    z_out[1, 0] = give_down
    z_out[1, 1] = part0
    swap_z = [send(z_out.at[way], z_in.at[way], faces[way]) for way in range(2)]
    for way, row in ((0, 15), (1, 0)):
        for k in range(2):
            y_out[way, k : k + 1, :] = parts[k][row : row + 1]
            y_out[way, 2 + k : 3 + k, :] = give_rows[2 * way + k : 2 * way + k + 1]
    swap_y = [send(y_out.at[way], y_in.at[way], faces[2 + way]) for way in range(2)]
    slot_of, swap_d = {}, []
    for i, (dz, dy, device) in enumerate(corners):
        slot_of[dz, dy] = i
        way = (1 - dy) // 2
        plane = (1 + dz) // 2
        give, row = (give_up if dz == 1 else give_down), (15 if dy == 1 else 0)
        d_out[i, 0:1, :] = give_rows[2 * way + plane : 2 * way + plane + 1]
        d_out[i, 1:2, :] = give[row : row + 1]
        swap_d.append(send(d_out.at[i], d_in.at[i], device))
    z_smooth = [
        send(smo0.at[4, 8:40, :], far_smooth.at[0], faces[0]), send(smo0.at[1, 8:40, :], far_smooth.at[1], faces[1])
    ]
    for k in range(4):
        rows_out[0, 2, k : k + 1, :] = smo0[k + 1, 39:40, :]
        rows_out[1, 2, k : k + 1, :] = smo0[k + 1, 8:9, :]
    y_smooth = [send(rows_out.at[way, 2], rows_in.at[way, 2], faces[2 + way]) for way in range(2)]
    dens2_copies = [
        send(rho2.at[3, 16:24, :], rho2.at[3, rows2[dy][1], :], device) for dy, device in y_ways
    ]
    for dz, dy, device in around:
        dens2_copies.append(send(rho2.at[3, 16:24, :], rho2.at[3 - dz, rows2[dy][1], :], device))

    def coefficients(level, z_faces):
        for k in range(level.planes):
            level.faces_x(k)
            level.faces_y(k)
        for k in range(level.planes + 1):
            level.faces_z(k)
        for k in range(level.planes):
            level.diagonal(k)
            level.mask_y(k, ((8, y_low), (level.rows - 8, y_high)))
        level.mask_z(z_faces)

    wait_recv(dens1_copies)
    fill_y(rho1, range(6), 16, 16)
    fill_z(rho1, 2, 2, slice(8, 40), 1)
    coefficients(middle, ((1, z_low), (3, z_high)))
    wait_recv(column_dens)
    layer_dens = gather_layer(0, inbox_dens, wide_dens)

    wait_recv(dens2_copies)
    fill_y(rho2, range(7), 8, 16)
    fill_z(rho2, 3, 1, slice(8, 32), 3)

    def inside_z(face):
        at = gz + face - 2
        return jnp.where((at > 0) & (at < nz), 1.0, 0.0).astype(F32)

    coefficients(coarse, [(face, inside_z(face)) for face in range(6)])

    wait_recv(swap_z + swap_y + swap_d)
    source1 = []
    for k in range(2):
        src1[k + 2, 16:32, :] = parts[k] + z_in[k, 0]
        src1[k + 2, 16:17, :] = src1[k + 2, 16:17, :] + y_in[0, 2 + k : 3 + k, :]
        src1[k + 2, 31:32, :] = src1[k + 2, 31:32, :] + y_in[1, 2 + k : 3 + k, :]
        source1.append(src1[k + 2, 16:32, :])
        corr = 4.0 * source1[k] * idg1[k + 1, 8:24, :]
        val1[k + 2, 16:32, :] = corr
        near1[k + 2, 16:32, :] = corr
    for dz, plane, theirs, mine in ((1, 4, z_in[1, 1], give_up), (-1, 1, z_in[0, 1], give_down)):
        near1[plane, 16:32, :] = theirs + mine
        low, high = slot_of[-dz, 1], slot_of[-dz, -1]
        near1[plane, 16:17, :] = near1[plane, 16:17, :] + d_in[low, 0:1, :]
        near1[plane, 31:32, :] = near1[plane, 31:32, :] + d_in[high, 0:1, :]
        near1[plane, 16:32, :] = 4.0 * near1[plane, 16:32, :] * idg1[plane - 1, 8:24, :]
    for dy, row in ((1, 32), (-1, 15)):
        way = (1 - dy) // 2
        for k, dz in ((0, -1), (1, 1)):
            total = y_in[1 - way, k : k + 1, :] + give_rows[2 * way + k : 2 * way + k + 1]
            corner = slot_of[-dz, -dy]
            total = total + d_in[corner, 1:2, :]
            near1[k + 2, row : row + 1, :] = 4.0 * total * idg1[k + 1, row - 8 : row - 7, :]

    def residual1(k):
        here, near = middle.neighbours(near1, k + 1, 8, 16)
        return (1.0 - OMEGA) * source1[k] + 0.25 * near

    source2 = restrict1(residual1)
    src2[3, 16:24, :] = source2
    val2[3, 16:24, :] = 16.0 * source2 * idg2[2, 8:16, :]
    copies2 = [send(val2.at[3, 16:24, :], val2.at[3, rows2[dy][1], :], device) for dy, device in y_ways]
    for dz, device in z_ways:
        copies2.append(send(val2.at[3, 16:24, :], val2.at[3 - dz, 16:24, :], device))

    wait_recv(layer_dens)
    lane, sub = iota((8, 128), 1), iota((8, 128), 0)
    right_half = lane >= 64
    first_x, last_x = (lane % 64) == 0, (lane % 64) == 63
    first_y, last_y = (lane < 64) & (sub == 0), (lane >= 64) & (sub == 7)

    def lower_y(v):
        q = pltpu.roll(v, 64, 1)
        return jnp.where(right_half, q, pltpu.roll(q, 1, 0))

    def upper_y(v):
        q = pltpu.roll(v, 64, 1)
        return jnp.where(right_half, pltpu.roll(q, 7, 0), q)

    scale3 = 0.015625
    for zh in range(4):
        for s in range(16):
            rho3[1 + 16 * zh + s] = wide_dens[s, zh]
    rho3[0] = rho3[1]
    rho3[65] = rho3[64]

    def face3(k, _):
        bz3[k] = scale3 * twice_inverse(rho3[k] + rho3[k + 1])
        return 0

    lax.fori_loop(0, 65, face3, 0)

    def coef3(k, _):
        rho = rho3[k + 1]
        edge = twice_inverse(rho + rho)
        low = twice_inverse(rho + jnp.where(first_x, rho, pltpu.roll(rho, 1, 1)))
        total = low + jnp.where(last_x, edge, pltpu.roll(low, 127, 1))
        bx3[k] = jnp.where(first_x, 0.0, scale3 * low)
        low = twice_inverse(rho + jnp.where(first_y, rho, lower_y(rho)))
        total = total + low + jnp.where(last_y, edge, upper_y(low))
        by3[k] = jnp.where(first_y, 0.0, scale3 * low)
        dg3[k] = scale3 * total + bz3[k] + bz3[k + 1]
        return 0

    lax.fori_loop(0, 64, coef3, 0, unroll=4)

    wait_recv(copies2)
    here, near = coarse.neighbours(val2, 2, 8, 8)
    pack_message(1, (1.0 - OMEGA) * source2 + 0.0625 * near)
    column_src = gather_column(1, inbox_src)

    more1 = [send(pair1.at[:, 2:4, 16:32, :], pair1.at[:, planes1(dz), 16:32, :], device) for dz, device in z_ways]
    for dy, device in y_ways:
        source, target = rows1[dy]
        more1.append(send(pair1.at[:, 2:4, source, :], pair1.at[:, 2:4, target, :], device))
    for dz, dy, device in corners:
        source, target = rows1[dy]
        more1.append(send(pair1.at[:, 2:4, source, :], pair1.at[:, planes1(dz), target, :], device))
    more2 = [send(src2.at[3, 16:24, :], src2.at[3, rows2[dy][1], :], device) for dy, device in y_ways]
    for dz, dy, device in around:
        if abs(dz) == 1 and dy == 0:
            more2.append(send(src2.at[3, 16:24, :], src2.at[3 - dz, 16:24, :], device))
        else:
            more2.append(send(pair2.at[:, 3, 16:24, :], pair2.at[:, 3 - dz, rows2[dy][1], :], device))

    wait_recv(column_src)
    layer_src = gather_layer(1, inbox_src, wide_src)
    wait_recv(layer_src)

    zero_plane = jnp.zeros((8, 128), F32)
    dir3[0] = zero_plane
    dir3[65] = zero_plane
    for k in (0, 1, 66, 67):
        cor3[k] = zero_plane
    total = zero_plane
    for zh in range(4):
        for s in range(16):
            v = wide_src[s, zh]
            k = 16 * zh + s
            dir3[k + 1] = v
            res3[k] = v
            cor3[k + 2] = zero_plane
            total = total + v * v

    def whole(v):
        return jnp.sum(jnp.sum(v, axis=0, keepdims=True), axis=1, keepdims=True)

    def sweep(step, norm):
        def apply(k, acc):
            v = dir3[k + 1]
            bx, by = bx3[k], by3[k]
            image = dg3[k] * v - bz3[k] * dir3[k] - bz3[k + 1] * dir3[k + 2]
            image = image - by * lower_y(v) - upper_y(by * v)
            image = image - bx * pltpu.roll(v, 1, 1) - pltpu.roll(bx * v, 127, 1)
            img3[k] = image
            return acc + v * image

        bottom = whole(lax.fori_loop(0, 64, apply, zero_plane, unroll=16))
        alpha = norm / bottom

        def advance(k, acc):
            cor3[k + 2] = cor3[k + 2] + alpha * dir3[k + 1]
            r = res3[k] - alpha * img3[k]
            res3[k] = r
            return acc + r * r

        norm_next = whole(lax.fori_loop(0, 64, advance, zero_plane, unroll=16))
        beta = norm_next / norm

        def turn(k, _):
            dir3[k + 1] = res3[k] + beta * dir3[k + 1]
            return 0

        lax.fori_loop(0, 64, turn, 0, unroll=16)
        return norm_next

    lax.fori_loop(0, SWEEPS, sweep, whole(total))

    spread_rows, spread_cols = iota((128, 256), 0), iota((128, 256), 1)
    fine_x = spread_cols % 128
    parent = fine_x // 2
    near = parent + 2 * (fine_x % 2) - 1
    half = spread_cols // 128
    inside = (near >= 0) & (near < 64)
    from_halves = (
        jnp.where(spread_rows == parent + 64 * half, 0.75, 0.0)
        + jnp.where((spread_rows == near + 64 * half) & inside, 0.25, 0.0)
    ).astype(jnp.bfloat16)
    mixed = []
    for d in range(-3, 4):
        plane = gz + d + 4
        index = plane // 2
        other = index + 2 * (plane % 2) - 1
        mixed.append(0.75 * cor3[index] + 0.25 * cor3[other])
    x_done = dot(jnp.concatenate(mixed, axis=0), from_halves)
    wait_recv(more1 + more2 + z_smooth + y_smooth)
    wait_send(copies2 + more1 + more2 + z_smooth)
    first_row, last_row = iota((8, 128), 0) == 0, iota((8, 128), 0) == 7
    window = pl.ds(pl.multiple_of(8 * gy, 8), 24)
    for k in range(7):
        even, odd = x_done[8 * k : 8 * k + 8, 0:128], x_done[8 * k : 8 * k + 8, 128:256]
        fine_rows[k, 0:8, :] = zero_plane
        fine_rows[k, 40:48, :] = zero_plane
        below = jnp.where(first_row, 0.0, pltpu.roll(odd, 1, 0))
        above = jnp.where(last_row, 0.0, pltpu.roll(even, 7, 0))
        fine_rows[k, pl.ds(8, 8, stride=4), :] = 0.75 * even + 0.25 * below
        fine_rows[k, pl.ds(9, 8, stride=4), :] = 0.75 * even + 0.25 * odd
        fine_rows[k, pl.ds(10, 8, stride=4), :] = 0.75 * odd + 0.25 * even
        fine_rows[k, pl.ds(11, 8, stride=4), :] = 0.75 * odd + 0.25 * above
        val2[k, 8:32, :] = val2[k, 8:32, :] + fine_rows[k, window, :]

    def in_grid(shape, first_row, rows, plane, planes):
        row = iota(shape, 0)
        at = row + first_row
        good = (row > 0) & (row < shape[0] - 1) & (at >= 0) & (at < rows)
        return good & (plane >= 0) & (plane < planes)

    ups = []
    for k in range(5):
        here, near = coarse.neighbours(val2, k, 0, 24)
        up = (1.0 - OMEGA) * here + (16.0 * src2[k + 1, 8:32, :] + near) * idg2[k]
        ups.append(jnp.where(in_grid((24, 128), 8 * gy - 8, 8 * ny, gz + k - 2, nz), up, 0.0))

    spread_x1, spread_x0 = spread_matrix(128), spread_matrix(256)

    def prolong(ups, target, first, rows, spread_x):
        height = ups[0].shape[0]
        tall = 2 * height - 16
        n = height - 8
        x_done = dot(jnp.concatenate(ups, axis=0), spread_x)
        tiles = x_done.shape[1] // 128
        for t in range(tiles):
            for k in range(len(ups)):
                pair_rows[t, 0:height, :] = x_done[height * k : height * (k + 1), 128 * t : 128 * (t + 1)]
                here = 0.75 * pair_rows[t, 4 : 4 + n, :]
                fine_rows[k, pl.ds(0, n, stride=2), :] = here + 0.25 * pair_rows[t, 3 : 3 + n, :]
                fine_rows[k, pl.ds(1, n, stride=2), :] = here + 0.25 * pair_rows[t, 5 : 5 + n, :]
            cols = slice(128 * t, 128 * (t + 1))
            for k in range(6):
                parent_z = (k + first) // 2
                near_z = parent_z + 2 * ((k + first) % 2) - 1
                target[k, rows, cols] = (
                    target[k, rows, cols] + 0.75 * fine_rows[parent_z, 0:tall, :] + 0.25 * fine_rows[near_z, 0:tall, :]
                )

    prolong(ups, val1, 2, slice(8, 40), spread_x1)
    ups = []
    for k in range(4):
        parts = []
        for r, m in middle.chunks():
            here, near = middle.neighbours(val1, k, r, m)
            source = src1[k + 1, 8 + r : 8 + r + m, :]
            parts.append((1.0 - OMEGA) * here + (4.0 * source + near) * idg1[k, r : r + m, :])
        up = jnp.concatenate(parts, axis=0)
        ups.append(jnp.where(in_grid((32, 256), 16 * gy - 8, 16 * ny, 2 * gz + k - 1, 2 * nz), up, 0.0))
    for k, plane in ((0, 0), (1, 5)):
        smo0[plane, 8:40, :] = far_smooth[k]
    for k in range(4):
        smo0[k + 1, 7:8, :] = rows_in[0, 2, k : k + 1, :]
        smo0[k + 1, 40:41, :] = rows_in[1, 2, k : k + 1, :]
    prolong(ups, smo0, 1, slice(0, 48), spread_x0)
    outgoing = []
    for k in range(4):
        for r, m in fine.chunks():
            here, near = fine.neighbours(smo0, k, r, m)
            result[k, r : r + m, :] = (1.0 - OMEGA) * here + (src0[k, r : r + m, :] + near) * fine.idg[k, r : r + m, :]
        copy = pltpu.make_async_copy(result.at[k], out.at[k], out_sem.at[k])
        copy.start()
        outgoing.append(copy)

    wait_send(
        z_dens + z_vals + y_both + dens1_copies + dens2_copies + column_dens + y_smooth + layer_dens
        + column_src + layer_src + swap_z + swap_y + swap_d
    )
    for copy in outgoing:
        copy.wait()


def coefficient_scratch(planes, rows, cols):
    own = pltpu.VMEM((planes, rows, cols), F32)
    return [own, pltpu.VMEM((planes, rows + 8, cols), F32), pltpu.VMEM((planes + 1, rows, cols), F32), own, own]


COPIES = 6 + 8 + 20 + 8 + 4 + 4 + 8 + 20 + 62 + 30


def per_device(density, right_side, pressure_guess):
    coarsest = pltpu.VMEM((64, 8, 128), F32)
    return pl.pallas_call(
        kernel,
        out_shape=jax.ShapeDtypeStruct(density.shape, F32),
        in_specs=[pl.BlockSpec(memory_space=pltpu.HBM)] * 3,
        out_specs=pl.BlockSpec(memory_space=pltpu.HBM),
        scratch_shapes=[
            *[pltpu.VMEM((6, 48, 512), F32)] * 3,
            *[pltpu.VMEM((4, 32, 512), F32)] * 2,
            *coefficient_scratch(4, 32, 512),
            pltpu.VMEM((6, 48, 256), F32),
            pltpu.VMEM((2, 6, 48, 256), F32),
            pltpu.VMEM((6, 48, 256), F32),
            *coefficient_scratch(4, 32, 256),
            pltpu.VMEM((7, 40, 128), F32),
            pltpu.VMEM((2, 7, 40, 128), F32),
            *coefficient_scratch(5, 24, 128),
            pltpu.VMEM((2, 3, 4, 512), F32),
            pltpu.VMEM((2, 3, 4, 512), F32),
            pltpu.VMEM((2, 2, 128), F32),
            pltpu.VMEM((4, 2, 4, 2, 128), F32),
            pltpu.VMEM((4, 2, 4, 2, 128), F32),
            pltpu.VMEM((2, 4, 8, 128), F32),
            pltpu.VMEM((16, 4, 8, 128), F32),
            pltpu.VMEM((16, 4, 8, 128), F32),
            pltpu.VMEM((66, 8, 128), F32),
            coarsest, coarsest, pltpu.VMEM((65, 8, 128), F32), coarsest,
            pltpu.VMEM((66, 8, 128), F32), coarsest, coarsest, pltpu.VMEM((68, 8, 128), F32),
            pltpu.VMEM((8, 256), F32),
            pltpu.VMEM((8, 32, 128), F32),
            pltpu.VMEM((7, 48, 128), F32),
            pltpu.VMEM((4, 32, 512), F32),
            pltpu.VMEM((2, 32, 512), F32),
            pltpu.VMEM((8, 512), F32),
            *[pltpu.VMEM((2, 2, 16, 256), F32)] * 2,
            *[pltpu.VMEM((2, 4, 256), F32)] * 2,
            *[pltpu.VMEM((4, 2, 256), F32)] * 2,
            pltpu.SemaphoreType.DMA((3,)),
            pltpu.SemaphoreType.DMA((4,)),
            pltpu.SemaphoreType.DMA((COPIES,)),
            pltpu.SemaphoreType.DMA((COPIES,)),
        ],
        compiler_params=pltpu.CompilerParams(
            collective_id=0, has_side_effects=True, vmem_limit_bytes=32 * 1024 * 1024
        ),
        cost_estimate=pl.CostEstimate(flops=20_000_000, bytes_accessed=1 << 20, transcendentals=0),
    )(density, right_side, pressure_guess)


def solution(mesh):
    spec = P("gz", "gy", None)
    return jax.shard_map(per_device, mesh=mesh, in_specs=(spec, spec, spec), out_specs=spec, check_vma=False)
```

```python
import functools

import jax
import jax.numpy as jnp
from jax import lax
from jax.experimental import pallas as pl
from jax.experimental.pallas import tpu as pltpu
from jax.sharding import PartitionSpec as P

MESH = pl.DeviceIdType.MESH
SWEEPS = 8
OMEGA = 0.8
F32 = jnp.float32
PAD = 8


def dot(values, weights):
    rows = values.shape[0]
    if rows % 16:
        values = jnp.concatenate([values, jnp.zeros((16 - rows % 16, values.shape[1]), F32)], axis=0)
    total = values.shape[0]
    first = values.astype(jnp.bfloat16).astype(F32)
    rest = values - first
    second = rest.astype(jnp.bfloat16).astype(F32)
    parts = jnp.concatenate([first, second, rest - second], axis=0).astype(jnp.bfloat16)
    out = jnp.dot(parts, weights, preferred_element_type=F32)
    return (out[0:total] + out[total : 2 * total] + out[2 * total :])[0:rows]


def twice_inverse(total):
    guess = pltpu.reciprocal(total, approx=True)
    return guess * (4.0 - 2.0 * total * guess)


def iota(shape, axis):
    return lax.broadcasted_iota(jnp.int32, shape, axis)


def pair_matrix():
    rows, cols = iota((256, 128), 0), iota((256, 128), 1)
    return jnp.where(rows // 2 == cols, 0.125, 0.0).astype(jnp.bfloat16)


def spread_matrix(coarse):
    rows, cols = iota((coarse, 2 * coarse), 0), iota((coarse, 2 * coarse), 1)
    parent = cols // 2
    near = parent + 2 * (cols % 2) - 1
    return (jnp.where(rows == parent, 0.75, 0.0) + jnp.where(rows == near, 0.25, 0.0)).astype(jnp.bfloat16)


class Level:
    def __init__(self, shape, chunk, rho, bx, by, bz, dg, idg):
        self.planes, self.rows, self.cols = shape
        self.chunk = chunk
        self.rho, self.bx, self.by, self.bz, self.dg, self.idg = rho, bx, by, bz, dg, idg

        self.span = (0, self.rows)

    def chunks(self):
        return [(r, self.chunk) for r in range(*self.span, self.chunk)]

    def faces_x(self, plane):
        n = self.cols
        for r, m in self.chunks():
            rho = self.rho[plane + 1, PAD + r : PAD + r + m, :]
            lane = iota((m, n), 1)
            low = twice_inverse(rho + jnp.where(lane == 0, rho, pltpu.roll(rho, 1, 1)))
            high = jnp.where(lane == n - 1, twice_inverse(rho + rho), pltpu.roll(low, n - 1, 1))
            self.dg[plane, r : r + m, :] = low + high
            self.bx[plane, r : r + m, :] = jnp.where(lane == 0, 0.0, low)

    def faces_y(self, plane):
        for r, m in self.chunks():
            low = self.rho[plane + 1, PAD - 1 + r : PAD - 1 + r + m, :]
            high = self.rho[plane + 1, PAD + r : PAD + r + m, :]
            self.by[plane, r : r + m, :] = twice_inverse(low + high)
        last = self.span[1]
        low = self.rho[plane + 1, PAD - 1 + last : PAD + last, :]
        high = self.rho[plane + 1, PAD + last : PAD + last + 1, :]
        self.by[plane, last : last + 1, :] = twice_inverse(low + high)

    def faces_z(self, face):
        for r, m in self.chunks():
            low = self.rho[face, PAD + r : PAD + r + m, :]
            high = self.rho[face + 1, PAD + r : PAD + r + m, :]
            self.bz[face, r : r + m, :] = twice_inverse(low + high)

    def diagonal(self, plane):
        for r, m in self.chunks():
            total = self.dg[plane, r : r + m, :]
            total = total + self.by[plane, r : r + m, :] + self.by[plane, r + 1 : r + 1 + m, :]
            total = total + self.bz[plane, r : r + m, :] + self.bz[plane + 1, r : r + m, :]
            self.dg[plane, r : r + m, :] = total
            self.idg[plane, r : r + m, :] = (0.5 * OMEGA) * twice_inverse(total)

    def mask_y(self, plane, faces):
        for row, factor in faces:
            self.by[plane, row : row + 1, :] = self.by[plane, row : row + 1, :] * factor

    def mask_z(self, faces):
        for face, factor in faces:
            self.bz[face] = self.bz[face] * factor

    def neighbours(self, val, plane, r, m):
        n = self.cols
        rows = slice(PAD + r, PAD + r + m)
        here = val[plane + 1, rows, :]
        bx = self.bx[plane, r : r + m, :]
        total = self.bz[plane, r : r + m, :] * val[plane, rows, :]
        total = total + self.bz[plane + 1, r : r + m, :] * val[plane + 2, rows, :]
        total = total + self.by[plane, r : r + m, :] * val[plane + 1, PAD - 1 + r : PAD - 1 + r + m, :]
        total = total + self.by[plane, r + 1 : r + 1 + m, :] * val[plane + 1, PAD + 1 + r : PAD + 1 + r + m, :]
        total = total + bx * pltpu.roll(here, 1, 1)
        total = total + pltpu.roll(bx * here, n - 1, 1)
        return here, total


def kernel(
    dens_in, right_in, guess_in, out,
    rho0, val0, smo0, src0, res0, bx0, by0, bz0, dg0, idg0,
    rho1, pair1, bx1, by1, bz1, dg1, idg1,
    rho2, pair2, bx2, by2, bz2, dg2, idg2,
    rows_out, rows_in, message, inbox_dens, inbox_src, tile, wide_dens, wide_src,
    rho3, bx3, by3, bz3, dg3, dir3, res3, img3, mul3, cor3, pair_tmp, pair_rows, fine_rows, result,
    far_smooth, face_rows, z_out, z_in, y_out, y_in, d_out, d_in, wide_y_out, wide_y_in, wide_d_out, wide_d_in, local_sem, out_sem, send_sem, recv_sem,
):
    gz, gy = lax.axis_index("gz"), lax.axis_index("gy")
    nz, ny = 128, 4
    core, ypos, xpos, zhi = gz % 2, (gz // 2) % 4, (gz // 8) % 4, gz // 32
    zpos = zhi * 4 + gy

    def gz_of(zh, x, y, c):
        return ((zh * 4 + x) * 4 + y) * 2 + c

    up_z, down_z = (gz + 1) % nz, (gz + nz - 1) % nz
    up_y, down_y = (gy + 1) % ny, (gy + ny - 1) % ny
    column = []
    for d in (8, 7, 9, 6, 10, 5, 11, 4, 12, 3, 13, 2, 14, 1, 15, 0):
        for k in range(2):
            if d or k:
                z = (zpos + d) % 16
                column.append((gz_of(z // 4, xpos, ypos, (core + k) % 2), z % 4))
    layer = []
    for i in range(4):
        for j in range(4):
            if i or j:
                layer.append((gz_of(zhi, (xpos + i) % 4, (ypos + j) % 4, core), gy))
    faces = [(up_z, gy), (down_z, gy), (gz, up_y), (gz, down_y)]
    around = []
    for dz in (1, -1, 2, -2, 3, -3):
        for dy in (0, 1, -1):
            around.append((dz, dy, ((gz + dz + nz) % nz, (gy + dy + ny) % ny)))
    corners = [(dz, dy, device) for dz, dy, device in around if abs(dz) == 1 and dy]
    greeted = column + [device for _, _, device in around] + faces[2:] + layer

    barrier = pltpu.get_barrier_semaphore()
    for device in greeted:
        pl.semaphore_signal(barrier, inc=1, device_id=device, device_id_type=MESH)

    local = []
    for i, (source, target) in enumerate(
        ((dens_in, rho0.at[1:5, 8:40, :]), (guess_in, val0.at[1:5, 8:40, :]), (right_in, src0))
    ):
        copy = pltpu.make_async_copy(source, target, local_sem.at[i])
        copy.start()
        local.append(copy)

    count = [0]

    def send(source, target, device):
        i = count[0]
        count[0] = i + 1
        copy = pltpu.make_async_remote_copy(
            src_ref=source, dst_ref=target, send_sem=send_sem.at[i], recv_sem=recv_sem.at[i],
            device_id=device, device_id_type=MESH,
        )
        copy.start()
        return copy

    def wait_recv(copies):
        for copy in copies:
            copy.wait_recv()

    def wait_send(copies):
        for copy in copies:
            copy.wait_send()

    fine = Level((4, 32, 512), 8, rho0, bx0, by0, bz0, dg0, idg0)
    middle = Level((4, 32, 256), 16, rho1, bx1, by1, bz1, dg1, idg1)
    coarse = Level((5, 24, 128), 8, rho2, bx2, by2, bz2, dg2, idg2)
    val1, src1, val2, src2 = pair1.at[0], pair1.at[1], pair2.at[0], pair2.at[1]

    z_low = jnp.where(gz > 0, 1.0, 0.0).astype(F32)
    z_high = jnp.where(gz < nz - 1, 1.0, 0.0).astype(F32)
    y_low = jnp.where(gy > 0, 1.0, 0.0).astype(F32)
    y_high = jnp.where(gy < ny - 1, 1.0, 0.0).astype(F32)

    pair_x = pair_matrix()

    def halve_x(blocks):
        rows = sum(block.shape[0] for block in blocks)
        summed = dot(jnp.concatenate([b[:, 0:256] for b in blocks] + [b[:, 256:512] for b in blocks], axis=0), pair_x)
        out, at = [], 0
        for block in blocks:
            n = block.shape[0]
            out.append((summed[at : at + n], summed[rows + at : rows + at + n]))
            at += n
        return out

    def halve_y(slot, value):
        n = value.shape[0]
        pair_rows[slot, 0:n, :] = value
        return pair_rows[slot, pl.ds(0, n // 2, stride=2), :] + pair_rows[slot, pl.ds(1, n // 2, stride=2), :]

    def halve_xy(blocks):
        return [
            jnp.concatenate([halve_y(2 * i, left), halve_y(2 * i + 1, right)], axis=1)
            for i, (left, right) in enumerate(halve_x(blocks))
        ]

    def restrict1(read):
        return halve_y(0, dot(read(0) + read(1), pair_x))

    half_rows, half_cols = iota((128, 256), 0), iota((128, 256), 1)
    to_halves = jnp.where((half_cols % 64 == half_rows // 2) & ((half_cols < 64) | (half_cols >= 192)), 0.125, 0.0).astype(jnp.bfloat16)

    def pack_message(field, value):
        pair_tmp[...] = dot(value, to_halves)
        for r in range(2):
            t = 4 * r
            message[field, r : r + 1, :] = (
                pair_tmp[t : t + 1, 0:128] + pair_tmp[t + 1 : t + 2, 0:128]
                + pair_tmp[t + 2 : t + 3, 128:256] + pair_tmp[t + 3 : t + 4, 128:256]
            )

    def gather_column(field, inbox):
        inbox[zhi, core, gy] = message[field]
        return [send(message.at[field], inbox.at[zhi, core, gy], device) for device in column]

    def gather_layer(field, inbox, wide):
        for zh in range(4):
            for y in range(4):
                tile[field, zh, 2 * y : 2 * y + 2, :] = inbox[zh, 0, y] + inbox[zh, 1, y]
        slot = xpos * 4 + ypos
        wide[slot] = tile[field]
        return [send(tile.at[field], wide.at[slot], device) for device in layer]

    local[0].wait()
    own1 = halve_xy([rho0[2 * k + 1, 8:40, :] + rho0[2 * k + 2, 8:40, :] for k in range(2)])
    for k in range(2):
        rho1[k + 2, 16:32, :] = own1[k]
    own2 = restrict1(lambda k: own1[k])
    rho2[3, 16:24, :] = own2
    pack_message(0, own2)
    local[1].wait()
    for k in range(4):
        for f, ref in ((0, rho0), (1, val0)):
            rows_out[0, f, k : k + 1, :] = ref[k + 1, 39:40, :]
            rows_out[1, f, k : k + 1, :] = ref[k + 1, 8:9, :]

    for k in (0, 5):
        smo0[k, 8:40, :] = jnp.zeros((32, 512), F32)
    for k in range(1, 5):
        smo0[k, 7:8, :] = jnp.zeros((1, 512), F32)
        smo0[k, 40:41, :] = jnp.zeros((1, 512), F32)

    pl.semaphore_wait(barrier, len(greeted))

    z_dens = [
        send(rho0.at[4, 8:40, :], rho0.at[0, 8:40, :], faces[0]),
        send(rho0.at[1, 8:40, :], rho0.at[5, 8:40, :], faces[1]),
    ]
    z_vals = [
        send(val0.at[4, 8:40, :], val0.at[0, 8:40, :], faces[0]),
        send(val0.at[1, 8:40, :], val0.at[5, 8:40, :], faces[1]),
    ]
    y_both = [
        send(rows_out.at[0, 0:2], rows_in.at[0, 0:2], faces[2]),
        send(rows_out.at[1, 0:2], rows_in.at[1, 0:2], faces[3]),
    ]

    rows1 = {0: (slice(16, 32), slice(16, 32)), 1: (slice(24, 32), slice(8, 16)), -1: (slice(16, 24), slice(32, 40))}
    rows2 = {dy: (slice(16, 24), slice(16 - 8 * dy, 24 - 8 * dy)) for dy in (0, 1, -1)}
    y_ways = ((1, faces[2]), (-1, faces[3]))
    z_ways = ((1, faces[0]), (-1, faces[1]))

    def planes1(dz):
        return slice(2 - 2 * dz, 4 - 2 * dz)

    def fill_y(ref, planes, rows, first):
        last = first + rows - 1
        for k in planes:
            ref[k, first - 1 : first, :] = jnp.where(gy == 0, ref[k, first : first + 1, :], ref[k, first - 1 : first, :])
            ref[k, last + 1 : last + 2, :] = jnp.where(
                gy == ny - 1, ref[k, last : last + 1, :], ref[k, last + 1 : last + 2, :]
            )

    def fill_z(ref, own, planes, rows, reach):
        for i in range(reach):
            low, high = own - 1 - i * planes, own + planes + i * planes
            ref[low, rows, :] = jnp.where(gz == i, ref[low + 1, rows, :], ref[low, rows, :])
            ref[high, rows, :] = jnp.where(gz == nz - 1 - i, ref[high - 1, rows, :], ref[high, rows, :])

    for k in range(4):
        fine.faces_x(k)
    for face in (1, 2, 3):
        fine.faces_z(face)
    wait_recv(y_both)
    for k in range(4):
        for f, ref in ((0, rho0), (1, val0)):
            ref[k + 1, 7:8, :] = rows_in[0, f, k : k + 1, :]
            ref[k + 1, 40:41, :] = rows_in[1, f, k : k + 1, :]
    fill_y(rho0, range(1, 5), 32, 8)
    for k in range(4):
        fine.faces_y(k)
    local[2].wait()

    def smooth(plane):
        for r, m in fine.chunks():
            here, near = fine.neighbours(val0, plane, r, m)
            smo0[plane + 1, 8 + r : 8 + r + m, :] = (1.0 - OMEGA) * here + (
                src0[plane, r : r + m, :] + near
            ) * fine.idg[plane, r : r + m, :]

    for k in (1, 2):
        fine.diagonal(k)
        fine.mask_y(k, ((0, y_low), (32, y_high)))
        smooth(k)
    wait_recv(z_dens)
    fill_z(rho0, 1, 4, slice(8, 40), 1)
    for face in (0, 4):
        fine.faces_z(face)
    for k in (0, 3):
        fine.diagonal(k)
        fine.mask_y(k, ((0, y_low), (32, y_high)))
    fine.mask_z(((0, z_low), (4, z_high)))
    wait_recv(z_vals)
    dens1_copies = [
        send(rho1.at[2:4, 16:32, :], rho1.at[planes1(dz), 16:32, :], device) for dz, device in z_ways
    ]
    for dy, device in y_ways:
        source, target = rows1[dy]
        dens1_copies.append(send(rho1.at[2:4, source, :], rho1.at[2:4, target, :], device))
    for dz, dy, device in corners:
        source, target = rows1[dy]
        dens1_copies.append(send(rho1.at[2:4, source, :], rho1.at[planes1(dz), target, :], device))
    smooth(3)
    smooth(0)

    for plane in range(4):
        for r, m in fine.chunks():
            here, near = fine.neighbours(smo0, plane, r, m)
            res0[plane, r : r + m, :] = src0[plane, r : r + m, :] - dg0[plane, r : r + m, :] * here + near
    for way, (row, cell) in enumerate(((32, 39), (0, 8))):
        for k in range(2):
            lower = by0[2 * k, row : row + 1, :] * smo0[2 * k + 1, cell : cell + 1, :]
            upper = by0[2 * k + 1, row : row + 1, :] * smo0[2 * k + 2, cell : cell + 1, :]
            face_rows[2 * way + k : 2 * way + k + 1, :] = lower + upper
    blocks = halve_x(
        [res0[0] + res0[1], res0[2] + res0[3], bz0[4] * smo0[4, 8:40, :], bz0[0] * smo0[1, 8:40, :], face_rows[...]]
    )
    part0, part1, give_up, give_down = [
        jnp.concatenate([halve_y(2 * i, left), halve_y(2 * i + 1, right)], axis=1)
        for i, (left, right) in enumerate(blocks[:4])
    ]
    give_rows = jnp.concatenate(blocks[4], axis=1)
    parts = (part0, part1)
    z_out[0, 0] = give_up
    z_out[0, 1] = part1
    z_out[1, 0] = give_down
    z_out[1, 1] = part0
    swap_z = [send(z_out.at[way], z_in.at[way], faces[way]) for way in range(2)]
    for way, row in ((0, 15), (1, 0)):
        for k in range(2):
            y_out[way, k : k + 1, :] = parts[k][row : row + 1]
            y_out[way, 2 + k : 3 + k, :] = give_rows[2 * way + k : 2 * way + k + 1]
    swap_y = [send(y_out.at[way], y_in.at[way], faces[2 + way]) for way in range(2)]
    slot_of, swap_d = {}, []
    for i, (dz, dy, device) in enumerate(corners):
        slot_of[dz, dy] = i
        way = (1 - dy) // 2
        plane = (1 + dz) // 2
        give, row = (give_up if dz == 1 else give_down), (15 if dy == 1 else 0)
        d_out[i, 0:1, :] = give_rows[2 * way + plane : 2 * way + plane + 1]
        d_out[i, 1:2, :] = give[row : row + 1]
        swap_d.append(send(d_out.at[i], d_in.at[i], device))
    column_dens = gather_column(0, inbox_dens)
    dens2_near = [send(rho2.at[3, 16:24, :], rho2.at[3, rows2[dy][1], :], device) for dy, device in y_ways]
    dens2_near += [send(rho2.at[3, 16:24, :], rho2.at[3 - dz, 16:24, :], device) for dz, device in z_ways]

    def coefficients(level, planes, z_faces):
        for k in planes:
            level.faces_x(k)
            level.faces_y(k)
        for k in range(planes[0], planes[-1] + 2):
            level.faces_z(k)
        for k in planes:
            level.diagonal(k)
            level.mask_y(k, ((8, y_low), (level.rows - 8, y_high)))
        level.mask_z(z_faces)

    wait_recv(dens1_copies)
    fill_y(rho1, range(6), 16, 16)
    fill_z(rho1, 2, 2, slice(8, 40), 1)
    coefficients(middle, range(4), ((1, z_low), (3, z_high)))
    wait_recv(dens2_near)
    fill_y(rho2, (3,), 8, 16)
    fill_z(rho2, 3, 1, slice(16, 24), 1)
    coarse.span = (8, 16)
    coefficients(coarse, (2,), ((2, z_low), (3, z_high)))
    coarse.span = (0, 24)

    wait_recv(swap_z + swap_y + swap_d)
    source1 = []
    for k in range(2):
        src1[k + 2, 16:32, :] = parts[k] + z_in[k, 0]
        src1[k + 2, 16:17, :] = src1[k + 2, 16:17, :] + y_in[0, 2 + k : 3 + k, :]
        src1[k + 2, 31:32, :] = src1[k + 2, 31:32, :] + y_in[1, 2 + k : 3 + k, :]
        source1.append(src1[k + 2, 16:32, :])
        val1[k + 2, 16:32, :] = 4.0 * source1[k] * idg1[k + 1, 8:24, :]
    for dz, plane, theirs, mine in ((1, 4, z_in[1, 1], give_up), (-1, 1, z_in[0, 1], give_down)):
        src1[plane, 16:32, :] = theirs + mine
        low, high = slot_of[-dz, 1], slot_of[-dz, -1]
        src1[plane, 16:17, :] = src1[plane, 16:17, :] + d_in[low, 0:1, :]
        src1[plane, 31:32, :] = src1[plane, 31:32, :] + d_in[high, 0:1, :]
        val1[plane, 16:32, :] = 4.0 * src1[plane, 16:32, :] * idg1[plane - 1, 8:24, :]
    for dy, row in ((1, 32), (-1, 15)):
        way = (1 - dy) // 2
        for k, dz in ((0, -1), (1, 1)):
            total = y_in[1 - way, k : k + 1, :] + give_rows[2 * way + k : 2 * way + k + 1]
            total = total + d_in[slot_of[-dz, -dy], 1:2, :]
            src1[k + 2, row : row + 1, :] = total
            val1[k + 2, row : row + 1, :] = 4.0 * total * idg1[k + 1, row - 8 : row - 7, :]

    def residual1(k):
        here, near = middle.neighbours(val1, k + 1, 8, 16)
        return (1.0 - OMEGA) * source1[k] + 0.25 * near

    source2 = restrict1(residual1)
    src2[3, 16:24, :] = source2
    val2[3, 16:24, :] = 16.0 * source2 * idg2[2, 8:16, :]
    copies2 = [send(val2.at[3, 16:24, :], val2.at[3, rows2[dy][1], :], device) for dy, device in y_ways]
    for dz, device in z_ways:
        copies2.append(send(val2.at[3, 16:24, :], val2.at[3 - dz, 16:24, :], device))

    z_smooth = [
        send(smo0.at[4, 8:40, :], far_smooth.at[0], faces[0]), send(smo0.at[1, 8:40, :], far_smooth.at[1], faces[1])
    ]
    for k in range(4):
        rows_out[0, 2, k : k + 1, :] = smo0[k + 1, 39:40, :]
        rows_out[1, 2, k : k + 1, :] = smo0[k + 1, 8:9, :]
    y_smooth = [send(rows_out.at[way, 2], rows_in.at[way, 2], faces[2 + way]) for way in range(2)]
    dens2_far = [
        send(rho2.at[3, 16:24, :], rho2.at[3 - dz, rows2[dy][1], :], device)
        for dz, dy, device in around if abs(dz) > 1 or dy
    ]
    wait_recv(column_dens)
    layer_dens = gather_layer(0, inbox_dens, wide_dens)
    wait_recv(copies2)
    here, near = coarse.neighbours(val2, 2, 8, 8)
    pack_message(1, (1.0 - OMEGA) * source2 + 0.0625 * near)
    column_src = gather_column(1, inbox_src)

    wait_recv(layer_dens)
    lane, sub = iota((8, 128), 1), iota((8, 128), 0)
    right_half = lane >= 64
    first_x, last_x = (lane % 64) == 0, (lane % 64) == 63
    first_y, last_y = (lane < 64) & (sub == 0), (lane >= 64) & (sub == 7)

    def lower_y(v):
        q = pltpu.roll(v, 64, 1)
        return jnp.where(right_half, q, pltpu.roll(q, 1, 0))

    def upper_y(v):
        q = pltpu.roll(v, 64, 1)
        return jnp.where(right_half, pltpu.roll(q, 7, 0), q)

    scale3 = 0.015625
    for zh in range(4):
        for s in range(16):
            rho3[1 + 16 * zh + s] = wide_dens[s, zh]
    rho3[0] = rho3[1]
    rho3[65] = rho3[64]

    def face3(k, _):
        bz3[k] = scale3 * twice_inverse(rho3[k] + rho3[k + 1])
        return 0

    lax.fori_loop(0, 65, face3, 0)

    def coef3(k, _):
        rho = rho3[k + 1]
        edge = twice_inverse(rho + rho)
        low = twice_inverse(rho + jnp.where(first_x, rho, pltpu.roll(rho, 1, 1)))
        total = low + jnp.where(last_x, edge, pltpu.roll(low, 127, 1))
        bx3[k] = jnp.where(first_x, 0.0, scale3 * low)
        low = twice_inverse(rho + jnp.where(first_y, rho, lower_y(rho)))
        total = total + low + jnp.where(last_y, edge, upper_y(low))
        by3[k] = jnp.where(first_y, 0.0, scale3 * low)
        dg3[k] = scale3 * total + bz3[k] + bz3[k + 1]
        return 0

    lax.fori_loop(0, 64, coef3, 0, unroll=4)

    wait_recv(dens2_far)

    def inside_z(face):
        at = gz + face - 2
        return jnp.where((at > 0) & (at < nz), 1.0, 0.0).astype(F32)

    fill_y(rho2, range(7), 8, 16)
    fill_z(rho2, 3, 1, slice(8, 32), 3)
    coefficients(coarse, range(5), [(face, inside_z(face)) for face in range(6)])

    zero_plane = jnp.zeros((8, 128), F32)
    for k in (0, 1, 66, 67):
        cor3[k] = zero_plane

    def clear3(k, _):
        dir3[k] = zero_plane
        mul3[k] = zero_plane
        cor3[k + 2] = zero_plane
        return 0

    lax.fori_loop(0, 64, clear3, 0, unroll=8)
    for ref in (dir3, mul3, res3, img3):
        ref[64] = zero_plane

    wait_recv(column_src)
    layer_src = gather_layer(1, inbox_src, wide_src)

    more1 = [
        send(val1.at[2, 16:32, :], val1.at[0, 16:32, :], faces[0]),
        send(val1.at[3, 16:32, :], val1.at[5, 16:32, :], faces[1]),
    ]
    for way, row in ((0, 30), (1, 17)):
        for k in range(2):
            wide_y_out[way, k : k + 1, :] = val1[k + 2, row : row + 1, :]
        more1.append(send(wide_y_out.at[way], wide_y_in.at[way], faces[2 + way]))
    for i, (dz, dy, device) in enumerate(corners):
        plane, far_plane = (3, 2) if dz == 1 else (2, 3)
        row, far_row = (31, 30) if dy == 1 else (16, 17)
        wide_d_out[i, 0:1, :] = val1[plane, row : row + 1, :]
        wide_d_out[i, 1:2, :] = val1[plane, far_row : far_row + 1, :]
        wide_d_out[i, 2:3, :] = val1[far_plane, row : row + 1, :]
        wide_d_out[i, 3:4, :] = src1[plane, row : row + 1, :]
        more1.append(send(wide_d_out.at[i], wide_d_in.at[i], device))
    more2 = [send(src2.at[3, 16:24, :], src2.at[3, rows2[dy][1], :], device) for dy, device in y_ways]
    for dz, dy, device in around:
        target = rows2[dy][1]
        if abs(dz) == 1 and dy == 0:
            more2.append(send(src2.at[3, 16:24, :], src2.at[3 - dz, target, :], device))
        elif abs(dz) == 3:
            more2.append(send(val2.at[3, 16:24, :], val2.at[3 - dz, target, :], device))
        else:
            more2.append(send(pair2.at[:, 3, 16:24, :], pair2.at[:, 3 - dz, target, :], device))
    wait_recv(layer_src)

    for zh in range(4):
        for k in range(16):
            res3[16 * zh + k] = wide_src[k, zh]

    def whole(v):
        return jnp.sum(jnp.sum(v, axis=1, keepdims=True), axis=0, keepdims=True)

    def apply(k, prev, here, later):
        bx, by = bx3[k], by3[k]
        image = (dg3[k] * here - bz3[k] * prev) - (bz3[k + 1] * later + by * lower_y(here))
        image = image - ((bx * pltpu.roll(here, 1, 1) + upper_y(by * here)) + pltpu.roll(bx * here, 127, 1))
        img3[k] = image
        return image

    def advance(k, alpha, beta):
        direction = res3[k] + beta * dir3[k]
        dir3[k] = direction
        cor3[k + 2] = cor3[k + 2] + alpha * direction
        image = img3[k] + beta * mul3[k]
        mul3[k] = image
        resid = res3[k] - alpha * image
        res3[k] = resid
        return resid

    def totals(first, next_resid):
        def plane(k, carry):
            norm, power, prev, here = carry
            later = next_resid(k + 1)
            image = apply(k, prev, here, later)
            return norm + here * here, power + here * image, here, later

        norm, power, _, _ = lax.fori_loop(0, 64, plane, (zero_plane, zero_plane, zero_plane, first), unroll=64)
        return whole(norm), whole(power)

    norm, power = totals(res3[0], lambda k: res3[k])

    def sweep(step, carry):
        alpha, beta, norm = carry
        norm_next, power = totals(advance(0, alpha, beta), lambda k: advance(k, alpha, beta))
        beta = norm_next / norm
        return norm_next / (power - beta * norm_next / alpha), beta, norm_next

    alpha, beta, _ = lax.fori_loop(0, SWEEPS - 1, sweep, (norm / power, jnp.zeros((1, 1), F32), norm))

    def finish(k, _):
        cor3[k + 2] = cor3[k + 2] + alpha * (res3[k] + beta * dir3[k])
        return 0

    lax.fori_loop(0, 64, finish, 0, unroll=16)

    spread_rows, spread_cols = iota((128, 256), 0), iota((128, 256), 1)
    fine_x = spread_cols % 128
    parent = fine_x // 2
    near = parent + 2 * (fine_x % 2) - 1
    half = spread_cols // 128
    inside = (near >= 0) & (near < 64)
    from_halves = (
        jnp.where(spread_rows == parent + 64 * half, 0.75, 0.0)
        + jnp.where((spread_rows == near + 64 * half) & inside, 0.25, 0.0)
    ).astype(jnp.bfloat16)
    mixed = []
    for d in range(-3, 4):
        plane = gz + d + 4
        index = plane // 2
        other = index + 2 * (plane % 2) - 1
        mixed.append(0.75 * cor3[index] + 0.25 * cor3[other])
    x_done = dot(jnp.concatenate(mixed, axis=0), from_halves)
    wait_recv(more1 + more2 + z_smooth + y_smooth)
    wait_send(copies2 + more1 + more2 + z_smooth)
    for way, row in ((0, 14), (1, 33)):
        for k in range(2):
            val1[k + 2, row : row + 1, :] = wide_y_in[way, k : k + 1, :]
    for i, (dz, dy, _) in enumerate(corners):
        plane, far_plane = (1, 0) if dz == 1 else (4, 5)
        row, far_row = (15, 14) if dy == 1 else (32, 33)
        val1[plane, row : row + 1, :] = wide_d_in[i, 0:1, :]
        val1[plane, far_row : far_row + 1, :] = wide_d_in[i, 1:2, :]
        val1[far_plane, row : row + 1, :] = wide_d_in[i, 2:3, :]
        src1[plane, row : row + 1, :] = wide_d_in[i, 3:4, :]
    first_row, last_row = iota((8, 128), 0) == 0, iota((8, 128), 0) == 7
    window = pl.ds(pl.multiple_of(8 * gy, 8), 24)
    for k in range(7):
        even, odd = x_done[8 * k : 8 * k + 8, 0:128], x_done[8 * k : 8 * k + 8, 128:256]
        fine_rows[k, 0:8, :] = zero_plane
        fine_rows[k, 40:48, :] = zero_plane
        below = jnp.where(first_row, 0.0, pltpu.roll(odd, 1, 0))
        above = jnp.where(last_row, 0.0, pltpu.roll(even, 7, 0))
        fine_rows[k, pl.ds(8, 8, stride=4), :] = 0.75 * even + 0.25 * below
        fine_rows[k, pl.ds(9, 8, stride=4), :] = 0.75 * even + 0.25 * odd
        fine_rows[k, pl.ds(10, 8, stride=4), :] = 0.75 * odd + 0.25 * even
        fine_rows[k, pl.ds(11, 8, stride=4), :] = 0.75 * odd + 0.25 * above
        val2[k, 8:32, :] = val2[k, 8:32, :] + fine_rows[k, window, :]

    def in_grid(shape, margin, first_row, rows, plane, planes):
        row = iota(shape, 0)
        at = row + first_row
        good = (row >= margin) & (row < shape[0] - margin) & (at >= 0) & (at < rows)
        return good & (plane >= 0) & (plane < planes)

    ups = []
    for k in range(5):
        here, near = coarse.neighbours(val2, k, 0, 24)
        up = (1.0 - OMEGA) * here + (16.0 * src2[k + 1, 8:32, :] + near) * idg2[k]
        ups.append(jnp.where(in_grid((24, 128), 1, 8 * gy - 8, 8 * ny, gz + k - 2, nz), up, 0.0))

    spread_x1, spread_x0 = spread_matrix(128), spread_matrix(256)

    def prolong(ups, target, first, rows, spread_x):
        height = ups[0].shape[0]
        tall = 2 * height - 16
        n = height - 8
        x_done = dot(jnp.concatenate(ups, axis=0), spread_x)
        tiles = x_done.shape[1] // 128
        for t in range(tiles):
            for k in range(len(ups)):
                pair_rows[t, 0:height, :] = x_done[height * k : height * (k + 1), 128 * t : 128 * (t + 1)]
                here = 0.75 * pair_rows[t, 4 : 4 + n, :]
                fine_rows[k, pl.ds(0, n, stride=2), :] = here + 0.25 * pair_rows[t, 3 : 3 + n, :]
                fine_rows[k, pl.ds(1, n, stride=2), :] = here + 0.25 * pair_rows[t, 5 : 5 + n, :]
            cols = slice(128 * t, 128 * (t + 1))
            for k in range(6):
                parent_z = (k + first) // 2
                near_z = parent_z + 2 * ((k + first) % 2) - 1
                target[k, rows, cols] = (
                    target[k, rows, cols] + 0.75 * fine_rows[parent_z, 0:tall, :] + 0.25 * fine_rows[near_z, 0:tall, :]
                )

    prolong(ups, val1, 2, slice(8, 40), spread_x1)
    ups = []
    for k in range(4):
        parts = []
        for r, m in middle.chunks():
            here, near = middle.neighbours(val1, k, r, m)
            source = src1[k + 1, 8 + r : 8 + r + m, :]
            parts.append((1.0 - OMEGA) * here + (4.0 * source + near) * idg1[k, r : r + m, :])
        up = jnp.concatenate(parts, axis=0)
        ups.append(jnp.where(in_grid((32, 256), 7, 16 * gy - 8, 16 * ny, 2 * gz + k - 1, 2 * nz), up, 0.0))
    for k, plane in ((0, 0), (1, 5)):
        smo0[plane, 8:40, :] = far_smooth[k]
    for k in range(4):
        smo0[k + 1, 7:8, :] = rows_in[0, 2, k : k + 1, :]
        smo0[k + 1, 40:41, :] = rows_in[1, 2, k : k + 1, :]
    prolong(ups, smo0, 1, slice(0, 48), spread_x0)
    outgoing = []
    for k in range(4):
        for r, m in fine.chunks():
            here, near = fine.neighbours(smo0, k, r, m)
            result[k, r : r + m, :] = (1.0 - OMEGA) * here + (src0[k, r : r + m, :] + near) * fine.idg[k, r : r + m, :]
        copy = pltpu.make_async_copy(result.at[k], out.at[k], out_sem.at[k])
        copy.start()
        outgoing.append(copy)

    wait_send(
        z_dens + z_vals + y_both + dens1_copies + dens2_near + dens2_far + column_dens + y_smooth + layer_dens
        + column_src + layer_src + swap_z + swap_y + swap_d
    )
    for copy in outgoing:
        copy.wait()


def coefficient_scratch(planes, rows, cols):
    own = pltpu.VMEM((planes, rows, cols), F32)
    return [own, pltpu.VMEM((planes, rows + 8, cols), F32), pltpu.VMEM((planes + 1, rows, cols), F32), own, own]


COPIES = 6 + 8 + 8 + 4 + 16 + 4 + 4 + 8 + 20 + 62 + 30


def per_device(density, right_side, pressure_guess):
    coarsest, longer = pltpu.VMEM((64, 8, 128), F32), pltpu.VMEM((65, 8, 128), F32)
    return pl.pallas_call(
        kernel,
        out_shape=jax.ShapeDtypeStruct(density.shape, F32),
        in_specs=[pl.BlockSpec(memory_space=pltpu.HBM)] * 3,
        out_specs=pl.BlockSpec(memory_space=pltpu.HBM),
        scratch_shapes=[
            *[pltpu.VMEM((6, 48, 512), F32)] * 3,
            *[pltpu.VMEM((4, 32, 512), F32)] * 2,
            *coefficient_scratch(4, 32, 512),
            pltpu.VMEM((6, 48, 256), F32),
            pltpu.VMEM((2, 6, 48, 256), F32),
            *coefficient_scratch(4, 32, 256),
            pltpu.VMEM((7, 40, 128), F32),
            pltpu.VMEM((2, 7, 40, 128), F32),
            *coefficient_scratch(5, 24, 128),
            pltpu.VMEM((2, 3, 4, 512), F32),
            pltpu.VMEM((2, 3, 4, 512), F32),
            pltpu.VMEM((2, 2, 128), F32),
            pltpu.VMEM((4, 2, 4, 2, 128), F32),
            pltpu.VMEM((4, 2, 4, 2, 128), F32),
            pltpu.VMEM((2, 4, 8, 128), F32),
            pltpu.VMEM((16, 4, 8, 128), F32),
            pltpu.VMEM((16, 4, 8, 128), F32),
            pltpu.VMEM((66, 8, 128), F32),
            coarsest, coarsest, longer, coarsest,
            longer, longer, longer, longer, pltpu.VMEM((68, 8, 128), F32),
            pltpu.VMEM((8, 256), F32),
            pltpu.VMEM((8, 32, 128), F32),
            pltpu.VMEM((7, 48, 128), F32),
            pltpu.VMEM((4, 32, 512), F32),
            pltpu.VMEM((2, 32, 512), F32),
            pltpu.VMEM((8, 512), F32),
            *[pltpu.VMEM((2, 2, 16, 256), F32)] * 2,
            *[pltpu.VMEM((2, 4, 256), F32)] * 2,
            *[pltpu.VMEM((4, 2, 256), F32)] * 2,
            *[pltpu.VMEM((2, 2, 256), F32)] * 2,
            *[pltpu.VMEM((4, 4, 256), F32)] * 2,
            pltpu.SemaphoreType.DMA((3,)),
            pltpu.SemaphoreType.DMA((4,)),
            pltpu.SemaphoreType.DMA((COPIES,)),
            pltpu.SemaphoreType.DMA((COPIES,)),
        ],
        compiler_params=pltpu.CompilerParams(
            collective_id=0, has_side_effects=True, vmem_limit_bytes=32 * 1024 * 1024
        ),
        cost_estimate=pl.CostEstimate(flops=20_000_000, bytes_accessed=1 << 20, transcendentals=0),
    )(density, right_side, pressure_guess)


def solution(mesh):
    spec = P("gz", "gy", None)
    return jax.shard_map(per_device, mesh=mesh, in_specs=(spec, spec, spec), out_specs=spec, check_vma=False)
```

```python
import functools

import jax
import jax.numpy as jnp
from jax import lax
from jax.experimental import pallas as pl
from jax.experimental.pallas import tpu as pltpu
from jax.sharding import PartitionSpec as P

MESH = pl.DeviceIdType.MESH
SWEEPS = 8
OMEGA = 0.8
F32 = jnp.float32
PAD = 8


def dot(values, weights):
    rows = values.shape[0]
    if rows % 16:
        values = jnp.concatenate([values, jnp.zeros((16 - rows % 16, values.shape[1]), F32)], axis=0)
    total = values.shape[0]
    first = values.astype(jnp.bfloat16).astype(F32)
    rest = values - first
    second = rest.astype(jnp.bfloat16).astype(F32)
    parts = jnp.concatenate([first, second, rest - second], axis=0).astype(jnp.bfloat16)
    out = jnp.dot(parts, weights, preferred_element_type=F32)
    return (out[0:total] + out[total : 2 * total] + out[2 * total :])[0:rows]


def twice_inverse(total):
    guess = pltpu.reciprocal(total, approx=True)
    return guess * (4.0 - 2.0 * total * guess)


def iota(shape, axis):
    return lax.broadcasted_iota(jnp.int32, shape, axis)


def pair_matrix():
    rows, cols = iota((256, 128), 0), iota((256, 128), 1)
    return jnp.where(rows // 2 == cols, 0.125, 0.0).astype(jnp.bfloat16)


def spread_matrix(coarse):
    rows, cols = iota((coarse, 2 * coarse), 0), iota((coarse, 2 * coarse), 1)
    parent = cols // 2
    near = parent + 2 * (cols % 2) - 1
    return (jnp.where(rows == parent, 0.75, 0.0) + jnp.where(rows == near, 0.25, 0.0)).astype(jnp.bfloat16)


class Level:
    def __init__(self, shape, chunk, rho, bx, by, bz, dg, idg):
        self.planes, self.rows, self.cols = shape
        self.chunk = chunk
        self.rho, self.bx, self.by, self.bz, self.dg, self.idg = rho, bx, by, bz, dg, idg

        self.span = (0, self.rows)

    def chunks(self):
        return [(r, self.chunk) for r in range(*self.span, self.chunk)]

    def faces_x(self, plane):
        n = self.cols
        for r, m in self.chunks():
            rho = self.rho[plane + 1, PAD + r : PAD + r + m, :]
            lane = iota((m, n), 1)
            low = twice_inverse(rho + jnp.where(lane == 0, rho, pltpu.roll(rho, 1, 1)))
            high = jnp.where(lane == n - 1, twice_inverse(rho + rho), pltpu.roll(low, n - 1, 1))
            self.dg[plane, r : r + m, :] = low + high
            self.bx[plane, r : r + m, :] = jnp.where(lane == 0, 0.0, low)

    def faces_y(self, plane):
        for r, m in self.chunks():
            low = self.rho[plane + 1, PAD - 1 + r : PAD - 1 + r + m, :]
            high = self.rho[plane + 1, PAD + r : PAD + r + m, :]
            self.by[plane, r : r + m, :] = twice_inverse(low + high)
        last = self.span[1]
        low = self.rho[plane + 1, PAD - 1 + last : PAD + last, :]
        high = self.rho[plane + 1, PAD + last : PAD + last + 1, :]
        self.by[plane, last : last + 1, :] = twice_inverse(low + high)

    def faces_z(self, face):
        for r, m in self.chunks():
            low = self.rho[face, PAD + r : PAD + r + m, :]
            high = self.rho[face + 1, PAD + r : PAD + r + m, :]
            self.bz[face, r : r + m, :] = twice_inverse(low + high)

    def diagonal(self, plane):
        for r, m in self.chunks():
            total = self.dg[plane, r : r + m, :]
            total = total + self.by[plane, r : r + m, :] + self.by[plane, r + 1 : r + 1 + m, :]
            total = total + self.bz[plane, r : r + m, :] + self.bz[plane + 1, r : r + m, :]
            self.dg[plane, r : r + m, :] = total
            self.idg[plane, r : r + m, :] = (0.5 * OMEGA) * twice_inverse(total)

    def mask_y(self, plane, faces):
        for row, factor in faces:
            self.by[plane, row : row + 1, :] = self.by[plane, row : row + 1, :] * factor

    def mask_z(self, faces):
        for face, factor in faces:
            self.bz[face] = self.bz[face] * factor

    def neighbours(self, val, plane, r, m):
        n = self.cols
        rows = slice(PAD + r, PAD + r + m)
        here = val[plane + 1, rows, :]
        bx = self.bx[plane, r : r + m, :]
        total = self.bz[plane, r : r + m, :] * val[plane, rows, :]
        total = total + self.bz[plane + 1, r : r + m, :] * val[plane + 2, rows, :]
        total = total + self.by[plane, r : r + m, :] * val[plane + 1, PAD - 1 + r : PAD - 1 + r + m, :]
        total = total + self.by[plane, r + 1 : r + 1 + m, :] * val[plane + 1, PAD + 1 + r : PAD + 1 + r + m, :]
        total = total + bx * pltpu.roll(here, 1, 1)
        total = total + pltpu.roll(bx * here, n - 1, 1)
        return here, total


def kernel(
    dens_in, right_in, guess_in, out,
    rho0, val0, smo0, src0, res0, bx0, by0, bz0, dg0, idg0,
    rho1, pair1, bx1, by1, bz1, dg1, idg1,
    rho2, pair2, bx2, by2, bz2, dg2, idg2,
    rows_out, rows_in, message, inbox_dens, inbox_src, tile, wide_dens, wide_src,
    rho3, bx3, by3, bz3, dg3, dir3, res3, img3, mul3, cor3, pair_tmp, pair_rows, fine_rows, result,
    far_smooth, face_rows, z_out, z_in, y_out, y_in, d_out, d_in, wide_y_out, wide_y_in, wide_d_out, wide_d_in,
    dens_y_out, dens_y_in, dens_d_out, dens_d_in, local_sem, out_sem, send_sem, recv_sem,
):
    gz, gy = lax.axis_index("gz"), lax.axis_index("gy")
    nz, ny = 128, 4
    core, ypos, xpos, zhi = gz % 2, (gz // 2) % 4, (gz // 8) % 4, gz // 32
    zpos = zhi * 4 + gy

    def gz_of(zh, x, y, c):
        return ((zh * 4 + x) * 4 + y) * 2 + c

    up_z, down_z = (gz + 1) % nz, (gz + nz - 1) % nz
    up_y, down_y = (gy + 1) % ny, (gy + ny - 1) % ny
    column = []
    for d in (8, 7, 9, 6, 10, 5, 11, 4, 12, 3, 13, 2, 14, 1, 15, 0):
        for k in range(2):
            if d or k:
                z = (zpos + d) % 16
                column.append((gz_of(z // 4, xpos, ypos, (core + k) % 2), z % 4))
    layer = []
    for i in range(4):
        for j in range(4):
            if i or j:
                layer.append((gz_of(zhi, (xpos + i) % 4, (ypos + j) % 4, core), gy))
    faces = [(up_z, gy), (down_z, gy), (gz, up_y), (gz, down_y)]
    around = []
    for dz in (1, -1, 2, -2, 3, -3):
        for dy in (0, 1, -1):
            around.append((dz, dy, ((gz + dz + nz) % nz, (gy + dy + ny) % ny)))
    corners = [(dz, dy, device) for dz, dy, device in around if abs(dz) == 1 and dy]
    greeted = column + [device for _, _, device in around] + faces[2:] + layer

    barrier = pltpu.get_barrier_semaphore()
    for device in greeted:
        pl.semaphore_signal(barrier, inc=1, device_id=device, device_id_type=MESH)

    local = []
    for i, (source, target) in enumerate(
        ((dens_in, rho0.at[1:5, 8:40, :]), (guess_in, val0.at[1:5, 8:40, :]), (right_in, src0))
    ):
        copy = pltpu.make_async_copy(source, target, local_sem.at[i])
        copy.start()
        local.append(copy)

    count = [0]

    def send(source, target, device):
        i = count[0]
        count[0] = i + 1
        copy = pltpu.make_async_remote_copy(
            src_ref=source, dst_ref=target, send_sem=send_sem.at[i], recv_sem=recv_sem.at[i],
            device_id=device, device_id_type=MESH,
        )
        copy.start()
        return copy

    def wait_recv(copies):
        for copy in copies:
            copy.wait_recv()

    def wait_send(copies):
        for copy in copies:
            copy.wait_send()

    fine = Level((4, 32, 512), 8, rho0, bx0, by0, bz0, dg0, idg0)
    middle = Level((4, 32, 256), 16, rho1, bx1, by1, bz1, dg1, idg1)
    coarse = Level((5, 24, 128), 8, rho2, bx2, by2, bz2, dg2, idg2)
    val1, src1, val2, src2 = pair1.at[0], pair1.at[1], pair2.at[0], pair2.at[1]

    z_low = jnp.where(gz > 0, 1.0, 0.0).astype(F32)
    z_high = jnp.where(gz < nz - 1, 1.0, 0.0).astype(F32)
    y_low = jnp.where(gy > 0, 1.0, 0.0).astype(F32)
    y_high = jnp.where(gy < ny - 1, 1.0, 0.0).astype(F32)

    pair_x = pair_matrix()

    def halve_x(blocks):
        rows = sum(block.shape[0] for block in blocks)
        summed = dot(jnp.concatenate([b[:, 0:256] for b in blocks] + [b[:, 256:512] for b in blocks], axis=0), pair_x)
        out, at = [], 0
        for block in blocks:
            n = block.shape[0]
            out.append((summed[at : at + n], summed[rows + at : rows + at + n]))
            at += n
        return out

    def halve_y(slot, value):
        n = value.shape[0]
        pair_rows[slot, 0:n, :] = value
        return pair_rows[slot, pl.ds(0, n // 2, stride=2), :] + pair_rows[slot, pl.ds(1, n // 2, stride=2), :]

    def halve_xy(blocks):
        return [
            jnp.concatenate([halve_y(2 * i, left), halve_y(2 * i + 1, right)], axis=1)
            for i, (left, right) in enumerate(halve_x(blocks))
        ]

    def restrict1(read):
        return halve_y(0, dot(read(0) + read(1), pair_x))

    half_rows, half_cols = iota((128, 256), 0), iota((128, 256), 1)
    to_halves = jnp.where((half_cols % 64 == half_rows // 2) & ((half_cols < 64) | (half_cols >= 192)), 0.125, 0.0).astype(jnp.bfloat16)

    def pack_message(field, value):
        pair_tmp[...] = dot(value, to_halves)
        for r in range(2):
            t = 4 * r
            message[field, r : r + 1, :] = (
                pair_tmp[t : t + 1, 0:128] + pair_tmp[t + 1 : t + 2, 0:128]
                + pair_tmp[t + 2 : t + 3, 128:256] + pair_tmp[t + 3 : t + 4, 128:256]
            )

    def gather_column(field, inbox):
        inbox[zhi, core, gy] = message[field]
        return [send(message.at[field], inbox.at[zhi, core, gy], device) for device in column]

    def gather_layer(field, inbox, wide):
        for zh in range(4):
            for y in range(4):
                tile[field, zh, 2 * y : 2 * y + 2, :] = inbox[zh, 0, y] + inbox[zh, 1, y]
        slot = xpos * 4 + ypos
        wide[slot] = tile[field]
        return [send(tile.at[field], wide.at[slot], device) for device in layer]

    local[0].wait()
    own1 = halve_xy([rho0[2 * k + 1, 8:40, :] + rho0[2 * k + 2, 8:40, :] for k in range(2)])
    for k in range(2):
        rho1[k + 2, 16:32, :] = own1[k]
    own2 = restrict1(lambda k: own1[k])
    rho2[3, 16:24, :] = own2
    pack_message(0, own2)
    local[1].wait()
    for k in range(4):
        for f, ref in ((0, rho0), (1, val0)):
            rows_out[0, f, k : k + 1, :] = ref[k + 1, 39:40, :]
            rows_out[1, f, k : k + 1, :] = ref[k + 1, 8:9, :]

    for way, (row, second) in enumerate(((31, 30), (16, 17))):
        for k in range(2):
            dens_y_out[way, 2 * k : 2 * k + 1, :] = rho1[k + 2, row : row + 1, :]
            dens_y_out[way, 2 * k + 1 : 2 * k + 2, :] = rho1[k + 2, second : second + 1, :]
    for i, (dz, dy, device) in enumerate(corners):
        plane, far_plane = (3, 2) if dz == 1 else (2, 3)
        row, second = (31, 30) if dy == 1 else (16, 17)
        for at, (p, r) in enumerate(((plane, row), (plane, second), (far_plane, row), (far_plane, second))):
            dens_d_out[i, at : at + 1, :] = rho1[p, r : r + 1, :]
    for k in (0, 5):
        smo0[k, 8:40, :] = jnp.zeros((32, 512), F32)
    for k in range(1, 5):
        smo0[k, 7:8, :] = jnp.zeros((1, 512), F32)
        smo0[k, 40:41, :] = jnp.zeros((1, 512), F32)

    pl.semaphore_wait(barrier, len(greeted))

    z_dens = [
        send(rho0.at[4, 8:40, :], rho0.at[0, 8:40, :], faces[0]),
        send(rho0.at[1, 8:40, :], rho0.at[5, 8:40, :], faces[1]),
    ]
    z_vals = [
        send(val0.at[4, 8:40, :], val0.at[0, 8:40, :], faces[0]),
        send(val0.at[1, 8:40, :], val0.at[5, 8:40, :], faces[1]),
    ]
    y_both = [
        send(rows_out.at[0, 0:2], rows_in.at[0, 0:2], faces[2]),
        send(rows_out.at[1, 0:2], rows_in.at[1, 0:2], faces[3]),
    ]

    dens1_copies = [
        send(rho1.at[2:4, 16:32, :], rho1.at[0:2, 16:32, :], faces[0]),
        send(rho1.at[2:4, 16:32, :], rho1.at[4:6, 16:32, :], faces[1]),
        send(dens_y_out.at[0], dens_y_in.at[0], faces[2]),
        send(dens_y_out.at[1], dens_y_in.at[1], faces[3]),
    ]
    for i, (dz, dy, device) in enumerate(corners):
        dens1_copies.append(send(dens_d_out.at[i], dens_d_in.at[i], device))

    rows2 = {dy: (slice(16, 24), slice(16 - 8 * dy, 24 - 8 * dy)) for dy in (0, 1, -1)}
    y_ways = ((1, faces[2]), (-1, faces[3]))
    z_ways = ((1, faces[0]), (-1, faces[1]))

    def fill_y(ref, planes, rows, first):
        last = first + rows - 1
        for k in planes:
            ref[k, first - 1 : first, :] = jnp.where(gy == 0, ref[k, first : first + 1, :], ref[k, first - 1 : first, :])
            ref[k, last + 1 : last + 2, :] = jnp.where(
                gy == ny - 1, ref[k, last : last + 1, :], ref[k, last + 1 : last + 2, :]
            )

    def fill_z(ref, own, planes, rows, reach):
        for i in range(reach):
            low, high = own - 1 - i * planes, own + planes + i * planes
            ref[low, rows, :] = jnp.where(gz == i, ref[low + 1, rows, :], ref[low, rows, :])
            ref[high, rows, :] = jnp.where(gz == nz - 1 - i, ref[high - 1, rows, :], ref[high, rows, :])

    for k in range(4):
        fine.faces_x(k)
    for face in (1, 2, 3):
        fine.faces_z(face)
    wait_recv(y_both)
    for k in range(4):
        for f, ref in ((0, rho0), (1, val0)):
            ref[k + 1, 7:8, :] = rows_in[0, f, k : k + 1, :]
            ref[k + 1, 40:41, :] = rows_in[1, f, k : k + 1, :]
    fill_y(rho0, range(1, 5), 32, 8)
    for k in range(4):
        fine.faces_y(k)
    local[2].wait()

    def smooth(plane):
        for r, m in fine.chunks():
            here, near = fine.neighbours(val0, plane, r, m)
            smo0[plane + 1, 8 + r : 8 + r + m, :] = (1.0 - OMEGA) * here + (
                src0[plane, r : r + m, :] + near
            ) * fine.idg[plane, r : r + m, :]

    for k in (1, 2):
        fine.diagonal(k)
        fine.mask_y(k, ((0, y_low), (32, y_high)))
        smooth(k)
    wait_recv(z_dens)
    fill_z(rho0, 1, 4, slice(8, 40), 1)
    for face in (0, 4):
        fine.faces_z(face)
    for k in (0, 3):
        fine.diagonal(k)
        fine.mask_y(k, ((0, y_low), (32, y_high)))
    fine.mask_z(((0, z_low), (4, z_high)))
    wait_recv(z_vals)
    smooth(3)
    smooth(0)

    for plane in range(4):
        for r, m in fine.chunks():
            here, near = fine.neighbours(smo0, plane, r, m)
            res0[plane, r : r + m, :] = src0[plane, r : r + m, :] - dg0[plane, r : r + m, :] * here + near
    for way, (row, cell) in enumerate(((32, 39), (0, 8))):
        for k in range(2):
            lower = by0[2 * k, row : row + 1, :] * smo0[2 * k + 1, cell : cell + 1, :]
            upper = by0[2 * k + 1, row : row + 1, :] * smo0[2 * k + 2, cell : cell + 1, :]
            face_rows[2 * way + k : 2 * way + k + 1, :] = lower + upper
    blocks = halve_x(
        [res0[0] + res0[1], res0[2] + res0[3], bz0[4] * smo0[4, 8:40, :], bz0[0] * smo0[1, 8:40, :], face_rows[...]]
    )
    part0, part1, give_up, give_down = [
        jnp.concatenate([halve_y(2 * i, left), halve_y(2 * i + 1, right)], axis=1)
        for i, (left, right) in enumerate(blocks[:4])
    ]
    give_rows = jnp.concatenate(blocks[4], axis=1)
    parts = (part0, part1)
    z_out[0, 0] = give_up
    z_out[0, 1] = part1
    z_out[1, 0] = give_down
    z_out[1, 1] = part0
    swap_z = [send(z_out.at[way], z_in.at[way], faces[way]) for way in range(2)]
    for way, row in ((0, 15), (1, 0)):
        for k in range(2):
            y_out[way, k : k + 1, :] = parts[k][row : row + 1]
            y_out[way, 2 + k : 3 + k, :] = give_rows[2 * way + k : 2 * way + k + 1]
    swap_y = [send(y_out.at[way], y_in.at[way], faces[2 + way]) for way in range(2)]
    slot_of, swap_d = {}, []
    for i, (dz, dy, device) in enumerate(corners):
        slot_of[dz, dy] = i
        way = (1 - dy) // 2
        plane = (1 + dz) // 2
        give, row = (give_up if dz == 1 else give_down), (15 if dy == 1 else 0)
        d_out[i, 0:1, :] = give_rows[2 * way + plane : 2 * way + plane + 1]
        d_out[i, 1:2, :] = give[row : row + 1]
        swap_d.append(send(d_out.at[i], d_in.at[i], device))
    column_dens = gather_column(0, inbox_dens)
    dens2_near = [send(rho2.at[3, 16:24, :], rho2.at[3, rows2[dy][1], :], device) for dy, device in y_ways]
    dens2_near += [send(rho2.at[3, 16:24, :], rho2.at[3 - dz, 16:24, :], device) for dz, device in z_ways]

    def coefficients(level, planes, z_faces):
        for k in planes:
            level.faces_x(k)
            level.faces_y(k)
        for k in range(planes[0], planes[-1] + 2):
            level.faces_z(k)
        for k in planes:
            level.diagonal(k)
            level.mask_y(k, ((8, y_low), (level.rows - 8, y_high)))
        level.mask_z(z_faces)

    wait_recv(dens1_copies)
    for way, (row, second) in enumerate(((15, 14), (32, 33))):
        for k in range(2):
            rho1[k + 2, row : row + 1, :] = dens_y_in[way, 2 * k : 2 * k + 1, :]
            rho1[k + 2, second : second + 1, :] = dens_y_in[way, 2 * k + 1 : 2 * k + 2, :]
    for i, (dz, dy, device) in enumerate(corners):
        plane, far_plane = (1, 0) if dz == 1 else (4, 5)
        row, second = (15, 14) if dy == 1 else (32, 33)
        for at, (p, r) in enumerate(((plane, row), (plane, second), (far_plane, row), (far_plane, second))):
            rho1[p, r : r + 1, :] = dens_d_in[i, at : at + 1, :]
    fill_y(rho1, range(6), 16, 16)
    fill_z(rho1, 2, 2, slice(8, 40), 1)
    coefficients(middle, range(4), ((1, z_low), (3, z_high)))
    wait_recv(dens2_near)
    fill_y(rho2, (3,), 8, 16)
    fill_z(rho2, 3, 1, slice(16, 24), 1)
    coarse.span = (8, 16)
    coefficients(coarse, (2,), ((2, z_low), (3, z_high)))
    coarse.span = (0, 24)

    wait_recv(swap_z + swap_y + swap_d)
    source1 = []
    for k in range(2):
        src1[k + 2, 16:32, :] = parts[k] + z_in[k, 0]
        src1[k + 2, 16:17, :] = src1[k + 2, 16:17, :] + y_in[0, 2 + k : 3 + k, :]
        src1[k + 2, 31:32, :] = src1[k + 2, 31:32, :] + y_in[1, 2 + k : 3 + k, :]
        source1.append(src1[k + 2, 16:32, :])
        val1[k + 2, 16:32, :] = 4.0 * source1[k] * idg1[k + 1, 8:24, :]
    for dz, plane, theirs, mine in ((1, 4, z_in[1, 1], give_up), (-1, 1, z_in[0, 1], give_down)):
        src1[plane, 16:32, :] = theirs + mine
        low, high = slot_of[-dz, 1], slot_of[-dz, -1]
        src1[plane, 16:17, :] = src1[plane, 16:17, :] + d_in[low, 0:1, :]
        src1[plane, 31:32, :] = src1[plane, 31:32, :] + d_in[high, 0:1, :]
        val1[plane, 16:32, :] = 4.0 * src1[plane, 16:32, :] * idg1[plane - 1, 8:24, :]
    for dy, row in ((1, 32), (-1, 15)):
        way = (1 - dy) // 2
        for k, dz in ((0, -1), (1, 1)):
            total = y_in[1 - way, k : k + 1, :] + give_rows[2 * way + k : 2 * way + k + 1]
            total = total + d_in[slot_of[-dz, -dy], 1:2, :]
            src1[k + 2, row : row + 1, :] = total
            val1[k + 2, row : row + 1, :] = 4.0 * total * idg1[k + 1, row - 8 : row - 7, :]

    def residual1(k):
        here, near = middle.neighbours(val1, k + 1, 8, 16)
        return (1.0 - OMEGA) * source1[k] + 0.25 * near

    source2 = restrict1(residual1)
    src2[3, 16:24, :] = source2
    val2[3, 16:24, :] = 16.0 * source2 * idg2[2, 8:16, :]
    copies2 = [send(val2.at[3, 16:24, :], val2.at[3, rows2[dy][1], :], device) for dy, device in y_ways]
    for dz, device in z_ways:
        copies2.append(send(val2.at[3, 16:24, :], val2.at[3 - dz, 16:24, :], device))

    dens2_far = [
        send(rho2.at[3, 16:24, :], rho2.at[3 - dz, rows2[dy][1], :], device)
        for dz, dy, device in around if abs(dz) > 1 or dy
    ]
    more1 = [
        send(val1.at[2, 16:32, :], val1.at[0, 16:32, :], faces[0]),
        send(val1.at[3, 16:32, :], val1.at[5, 16:32, :], faces[1]),
    ]
    for way, row in ((0, 30), (1, 17)):
        for k in range(2):
            wide_y_out[way, k : k + 1, :] = val1[k + 2, row : row + 1, :]
        more1.append(send(wide_y_out.at[way], wide_y_in.at[way], faces[2 + way]))
    for i, (dz, dy, device) in enumerate(corners):
        plane, far_plane = (3, 2) if dz == 1 else (2, 3)
        row, far_row = (31, 30) if dy == 1 else (16, 17)
        wide_d_out[i, 0:1, :] = val1[plane, row : row + 1, :]
        wide_d_out[i, 1:2, :] = val1[plane, far_row : far_row + 1, :]
        wide_d_out[i, 2:3, :] = val1[far_plane, row : row + 1, :]
        wide_d_out[i, 3:4, :] = src1[plane, row : row + 1, :]
        more1.append(send(wide_d_out.at[i], wide_d_in.at[i], device))
    more2 = [send(src2.at[3, 16:24, :], src2.at[3, rows2[dy][1], :], device) for dy, device in y_ways]
    for dz, dy, device in around:
        target = rows2[dy][1]
        if abs(dz) == 1 and dy == 0:
            more2.append(send(src2.at[3, 16:24, :], src2.at[3 - dz, target, :], device))
        elif abs(dz) == 3:
            more2.append(send(val2.at[3, 16:24, :], val2.at[3 - dz, target, :], device))
        else:
            more2.append(send(pair2.at[:, 3, 16:24, :], pair2.at[:, 3 - dz, target, :], device))
    wait_recv(column_dens)
    layer_dens = gather_layer(0, inbox_dens, wide_dens)
    wait_recv(copies2)
    here, near = coarse.neighbours(val2, 2, 8, 8)
    pack_message(1, (1.0 - OMEGA) * source2 + 0.0625 * near)
    column_src = gather_column(1, inbox_src)

    wait_recv(layer_dens)
    lane, sub = iota((8, 128), 1), iota((8, 128), 0)
    right_half = lane >= 64
    first_x, last_x = (lane % 64) == 0, (lane % 64) == 63
    first_y, last_y = (lane < 64) & (sub == 0), (lane >= 64) & (sub == 7)

    def lower_y(v):
        q = pltpu.roll(v, 64, 1)
        return jnp.where(right_half, q, pltpu.roll(q, 1, 0))

    def upper_y(v):
        q = pltpu.roll(v, 64, 1)
        return jnp.where(right_half, pltpu.roll(q, 7, 0), q)

    scale3 = 0.015625
    for zh in range(4):
        for s in range(16):
            rho3[1 + 16 * zh + s] = wide_dens[s, zh]
    rho3[0] = rho3[1]
    rho3[65] = rho3[64]

    def face3(k, _):
        bz3[k] = scale3 * twice_inverse(rho3[k] + rho3[k + 1])
        return 0

    lax.fori_loop(0, 65, face3, 0)

    def coef3(k, _):
        rho = rho3[k + 1]
        edge = twice_inverse(rho + rho)
        low = twice_inverse(rho + jnp.where(first_x, rho, pltpu.roll(rho, 1, 1)))
        total = low + jnp.where(last_x, edge, pltpu.roll(low, 127, 1))
        bx3[k] = jnp.where(first_x, 0.0, scale3 * low)
        low = twice_inverse(rho + jnp.where(first_y, rho, lower_y(rho)))
        total = total + low + jnp.where(last_y, edge, upper_y(low))
        by3[k] = jnp.where(first_y, 0.0, scale3 * low)
        dg3[k] = scale3 * total + bz3[k] + bz3[k + 1]
        return 0

    lax.fori_loop(0, 64, coef3, 0, unroll=4)

    wait_recv(dens2_far)

    def inside_z(face):
        at = gz + face - 2
        return jnp.where((at > 0) & (at < nz), 1.0, 0.0).astype(F32)

    fill_y(rho2, range(7), 8, 16)
    fill_z(rho2, 3, 1, slice(8, 32), 3)
    coefficients(coarse, range(5), [(face, inside_z(face)) for face in range(6)])

    zero_plane = jnp.zeros((8, 128), F32)
    for k in (0, 1, 66, 67):
        cor3[k] = zero_plane

    def clear3(k, _):
        dir3[k] = zero_plane
        mul3[k] = zero_plane
        cor3[k + 2] = zero_plane
        return 0

    lax.fori_loop(0, 64, clear3, 0, unroll=8)
    for ref in (dir3, mul3, res3, img3):
        ref[64] = zero_plane

    wait_recv(column_src)
    layer_src = gather_layer(1, inbox_src, wide_src)

    z_smooth = [
        send(smo0.at[4, 8:40, :], far_smooth.at[0], faces[0]), send(smo0.at[1, 8:40, :], far_smooth.at[1], faces[1])
    ]
    for k in range(4):
        rows_out[0, 2, k : k + 1, :] = smo0[k + 1, 39:40, :]
        rows_out[1, 2, k : k + 1, :] = smo0[k + 1, 8:9, :]
    y_smooth = [send(rows_out.at[way, 2], rows_in.at[way, 2], faces[2 + way]) for way in range(2)]
    wait_recv(layer_src)

    for zh in range(4):
        for k in range(16):
            res3[16 * zh + k] = wide_src[k, zh]

    def whole(v):
        return jnp.sum(jnp.sum(v, axis=1, keepdims=True), axis=0, keepdims=True)

    def apply(k, prev, here, later):
        bx, by = bx3[k], by3[k]
        image = (dg3[k] * here - bz3[k] * prev) - (bz3[k + 1] * later + by * lower_y(here))
        image = image - ((bx * pltpu.roll(here, 1, 1) + upper_y(by * here)) + pltpu.roll(bx * here, 127, 1))
        img3[k] = image
        return image

    def advance(k, alpha, beta):
        direction = res3[k] + beta * dir3[k]
        dir3[k] = direction
        cor3[k + 2] = cor3[k + 2] + alpha * direction
        image = img3[k] + beta * mul3[k]
        mul3[k] = image
        resid = res3[k] - alpha * image
        res3[k] = resid
        return resid

    def totals(first, next_resid):
        def plane(k, carry):
            norm, power, prev, here = carry
            later = next_resid(k + 1)
            image = apply(k, prev, here, later)
            return norm + here * here, power + here * image, here, later

        norm, power, _, _ = lax.fori_loop(0, 64, plane, (zero_plane, zero_plane, zero_plane, first), unroll=64)
        return whole(norm), whole(power)

    norm, power = totals(res3[0], lambda k: res3[k])

    def sweep(step, carry):
        alpha, beta, norm = carry
        norm_next, power = totals(advance(0, alpha, beta), lambda k: advance(k, alpha, beta))
        beta = norm_next / norm
        return norm_next / (power - beta * norm_next / alpha), beta, norm_next

    alpha, beta, _ = lax.fori_loop(0, SWEEPS - 1, sweep, (norm / power, jnp.zeros((1, 1), F32), norm))

    def finish(k, _):
        cor3[k + 2] = cor3[k + 2] + alpha * (res3[k] + beta * dir3[k])
        return 0

    lax.fori_loop(0, 64, finish, 0, unroll=16)

    spread_rows, spread_cols = iota((128, 256), 0), iota((128, 256), 1)
    fine_x = spread_cols % 128
    parent = fine_x // 2
    near = parent + 2 * (fine_x % 2) - 1
    half = spread_cols // 128
    inside = (near >= 0) & (near < 64)
    from_halves = (
        jnp.where(spread_rows == parent + 64 * half, 0.75, 0.0)
        + jnp.where((spread_rows == near + 64 * half) & inside, 0.25, 0.0)
    ).astype(jnp.bfloat16)
    mixed = []
    for d in range(-3, 4):
        plane = gz + d + 4
        index = plane // 2
        other = index + 2 * (plane % 2) - 1
        mixed.append(0.75 * cor3[index] + 0.25 * cor3[other])
    x_done = dot(jnp.concatenate(mixed, axis=0), from_halves)
    wait_recv(more1 + more2 + z_smooth + y_smooth)
    wait_send(copies2 + more1 + more2 + z_smooth)
    for way, row in ((0, 14), (1, 33)):
        for k in range(2):
            val1[k + 2, row : row + 1, :] = wide_y_in[way, k : k + 1, :]
    for i, (dz, dy, _) in enumerate(corners):
        plane, far_plane = (1, 0) if dz == 1 else (4, 5)
        row, far_row = (15, 14) if dy == 1 else (32, 33)
        val1[plane, row : row + 1, :] = wide_d_in[i, 0:1, :]
        val1[plane, far_row : far_row + 1, :] = wide_d_in[i, 1:2, :]
        val1[far_plane, row : row + 1, :] = wide_d_in[i, 2:3, :]
        src1[plane, row : row + 1, :] = wide_d_in[i, 3:4, :]
    first_row, last_row = iota((8, 128), 0) == 0, iota((8, 128), 0) == 7
    window = pl.ds(pl.multiple_of(8 * gy, 8), 24)
    for k in range(7):
        even, odd = x_done[8 * k : 8 * k + 8, 0:128], x_done[8 * k : 8 * k + 8, 128:256]
        fine_rows[k, 0:8, :] = zero_plane
        fine_rows[k, 40:48, :] = zero_plane
        below = jnp.where(first_row, 0.0, pltpu.roll(odd, 1, 0))
        above = jnp.where(last_row, 0.0, pltpu.roll(even, 7, 0))
        fine_rows[k, pl.ds(8, 8, stride=4), :] = 0.75 * even + 0.25 * below
        fine_rows[k, pl.ds(9, 8, stride=4), :] = 0.75 * even + 0.25 * odd
        fine_rows[k, pl.ds(10, 8, stride=4), :] = 0.75 * odd + 0.25 * even
        fine_rows[k, pl.ds(11, 8, stride=4), :] = 0.75 * odd + 0.25 * above
        val2[k, 8:32, :] = val2[k, 8:32, :] + fine_rows[k, window, :]

    def in_grid(shape, margin, first_row, rows, plane, planes):
        row = iota(shape, 0)
        at = row + first_row
        good = (row >= margin) & (row < shape[0] - margin) & (at >= 0) & (at < rows)
        return good & (plane >= 0) & (plane < planes)

    ups = []
    for k in range(5):
        here, near = coarse.neighbours(val2, k, 0, 24)
        up = (1.0 - OMEGA) * here + (16.0 * src2[k + 1, 8:32, :] + near) * idg2[k]
        ups.append(jnp.where(in_grid((24, 128), 1, 8 * gy - 8, 8 * ny, gz + k - 2, nz), up, 0.0))

    spread_x1, spread_x0 = spread_matrix(128), spread_matrix(256)

    def prolong(ups, target, first, rows, spread_x):
        height = ups[0].shape[0]
        tall = 2 * height - 16
        n = height - 8
        x_done = dot(jnp.concatenate(ups, axis=0), spread_x)
        tiles = x_done.shape[1] // 128
        for t in range(tiles):
            for k in range(len(ups)):
                pair_rows[t, 0:height, :] = x_done[height * k : height * (k + 1), 128 * t : 128 * (t + 1)]
                here = 0.75 * pair_rows[t, 4 : 4 + n, :]
                fine_rows[k, pl.ds(0, n, stride=2), :] = here + 0.25 * pair_rows[t, 3 : 3 + n, :]
                fine_rows[k, pl.ds(1, n, stride=2), :] = here + 0.25 * pair_rows[t, 5 : 5 + n, :]
            cols = slice(128 * t, 128 * (t + 1))
            for k in range(6):
                parent_z = (k + first) // 2
                near_z = parent_z + 2 * ((k + first) % 2) - 1
                target[k, rows, cols] = (
                    target[k, rows, cols] + 0.75 * fine_rows[parent_z, 0:tall, :] + 0.25 * fine_rows[near_z, 0:tall, :]
                )

    prolong(ups, val1, 2, slice(8, 40), spread_x1)
    ups = []
    for k in range(4):
        parts = []
        for r, m in middle.chunks():
            here, near = middle.neighbours(val1, k, r, m)
            source = src1[k + 1, 8 + r : 8 + r + m, :]
            parts.append((1.0 - OMEGA) * here + (4.0 * source + near) * idg1[k, r : r + m, :])
        up = jnp.concatenate(parts, axis=0)
        ups.append(jnp.where(in_grid((32, 256), 7, 16 * gy - 8, 16 * ny, 2 * gz + k - 1, 2 * nz), up, 0.0))
    for k, plane in ((0, 0), (1, 5)):
        smo0[plane, 8:40, :] = far_smooth[k]
    for k in range(4):
        smo0[k + 1, 7:8, :] = rows_in[0, 2, k : k + 1, :]
        smo0[k + 1, 40:41, :] = rows_in[1, 2, k : k + 1, :]
    prolong(ups, smo0, 1, slice(0, 48), spread_x0)
    outgoing = []
    for k in range(4):
        for r, m in fine.chunks():
            here, near = fine.neighbours(smo0, k, r, m)
            result[k, r : r + m, :] = (1.0 - OMEGA) * here + (src0[k, r : r + m, :] + near) * fine.idg[k, r : r + m, :]
        copy = pltpu.make_async_copy(result.at[k], out.at[k], out_sem.at[k])
        copy.start()
        outgoing.append(copy)

    wait_send(
        z_dens + z_vals + y_both + dens1_copies + dens2_near + dens2_far + column_dens + y_smooth + layer_dens
        + column_src + layer_src + swap_z + swap_y + swap_d
    )
    for copy in outgoing:
        copy.wait()


def coefficient_scratch(planes, rows, cols):
    own = pltpu.VMEM((planes, rows, cols), F32)
    return [own, pltpu.VMEM((planes, rows + 8, cols), F32), pltpu.VMEM((planes + 1, rows, cols), F32), own, own]


COPIES = 6 + 8 + 8 + 4 + 16 + 4 + 4 + 8 + 20 + 62 + 30


def per_device(density, right_side, pressure_guess):
    coarsest, longer = pltpu.VMEM((64, 8, 128), F32), pltpu.VMEM((65, 8, 128), F32)
    return pl.pallas_call(
        kernel,
        out_shape=jax.ShapeDtypeStruct(density.shape, F32),
        in_specs=[pl.BlockSpec(memory_space=pltpu.HBM)] * 3,
        out_specs=pl.BlockSpec(memory_space=pltpu.HBM),
        scratch_shapes=[
            *[pltpu.VMEM((6, 48, 512), F32)] * 3,
            *[pltpu.VMEM((4, 32, 512), F32)] * 2,
            *coefficient_scratch(4, 32, 512),
            pltpu.VMEM((6, 48, 256), F32),
            pltpu.VMEM((2, 6, 48, 256), F32),
            *coefficient_scratch(4, 32, 256),
            pltpu.VMEM((7, 40, 128), F32),
            pltpu.VMEM((2, 7, 40, 128), F32),
            *coefficient_scratch(5, 24, 128),
            pltpu.VMEM((2, 3, 4, 512), F32),
            pltpu.VMEM((2, 3, 4, 512), F32),
            pltpu.VMEM((2, 2, 128), F32),
            pltpu.VMEM((4, 2, 4, 2, 128), F32),
            pltpu.VMEM((4, 2, 4, 2, 128), F32),
            pltpu.VMEM((2, 4, 8, 128), F32),
            pltpu.VMEM((16, 4, 8, 128), F32),
            pltpu.VMEM((16, 4, 8, 128), F32),
            pltpu.VMEM((66, 8, 128), F32),
            coarsest, coarsest, longer, coarsest,
            longer, longer, longer, longer, pltpu.VMEM((68, 8, 128), F32),
            pltpu.VMEM((8, 256), F32),
            pltpu.VMEM((8, 32, 128), F32),
            pltpu.VMEM((7, 48, 128), F32),
            pltpu.VMEM((4, 32, 512), F32),
            pltpu.VMEM((2, 32, 512), F32),
            pltpu.VMEM((8, 512), F32),
            *[pltpu.VMEM((2, 2, 16, 256), F32)] * 2,
            *[pltpu.VMEM((2, 4, 256), F32)] * 2,
            *[pltpu.VMEM((4, 2, 256), F32)] * 2,
            *[pltpu.VMEM((2, 2, 256), F32)] * 2,
            *[pltpu.VMEM((4, 4, 256), F32)] * 2,
            *[pltpu.VMEM((2, 4, 256), F32)] * 2,
            *[pltpu.VMEM((4, 4, 256), F32)] * 2,
            pltpu.SemaphoreType.DMA((3,)),
            pltpu.SemaphoreType.DMA((4,)),
            pltpu.SemaphoreType.DMA((COPIES,)),
            pltpu.SemaphoreType.DMA((COPIES,)),
        ],
        compiler_params=pltpu.CompilerParams(
            collective_id=0, has_side_effects=True, vmem_limit_bytes=63 * 1024 * 1024
        ),
        cost_estimate=pl.CostEstimate(flops=20_000_000, bytes_accessed=1 << 20, transcendentals=0),
    )(density, right_side, pressure_guess)


def solution(mesh):
    spec = P("gz", "gy", None)
    return jax.shard_map(per_device, mesh=mesh, in_specs=(spec, spec, spec), out_specs=spec, check_vma=False)
```

```python
import functools

import jax
import jax.numpy as jnp
from jax import lax
from jax.experimental import pallas as pl
from jax.experimental.pallas import tpu as pltpu
from jax.sharding import PartitionSpec as P

MESH = pl.DeviceIdType.MESH
SWEEPS = 8
OMEGA = 0.8
F32 = jnp.float32
PAD = 8


def dot(values, weights):
    rows = values.shape[0]
    if rows % 16:
        values = jnp.concatenate([values, jnp.zeros((16 - rows % 16, values.shape[1]), F32)], axis=0)
    total = values.shape[0]
    first = values.astype(jnp.bfloat16).astype(F32)
    rest = values - first
    second = rest.astype(jnp.bfloat16).astype(F32)
    parts = jnp.concatenate([first, second, rest - second], axis=0).astype(jnp.bfloat16)
    out = jnp.dot(parts, weights, preferred_element_type=F32)
    return (out[0:total] + out[total : 2 * total] + out[2 * total :])[0:rows]


def twice_inverse(total):
    guess = pltpu.reciprocal(total, approx=True)
    return guess * (4.0 - 2.0 * total * guess)


def iota(shape, axis):
    return lax.broadcasted_iota(jnp.int32, shape, axis)


def pair_matrix():
    rows, cols = iota((256, 128), 0), iota((256, 128), 1)
    return jnp.where(rows // 2 == cols, 0.125, 0.0).astype(jnp.bfloat16)


def spread_matrix(coarse):
    rows, cols = iota((coarse, 2 * coarse), 0), iota((coarse, 2 * coarse), 1)
    parent = cols // 2
    near = parent + 2 * (cols % 2) - 1
    return (jnp.where(rows == parent, 0.75, 0.0) + jnp.where(rows == near, 0.25, 0.0)).astype(jnp.bfloat16)


class Level:
    def __init__(self, shape, chunk, rho, bx, by, bz, dg, idg):
        self.planes, self.rows, self.cols = shape
        self.chunk = chunk
        self.rho, self.bx, self.by, self.bz, self.dg, self.idg = rho, bx, by, bz, dg, idg

        self.span = (0, self.rows)

    def chunks(self):
        return [(r, self.chunk) for r in range(*self.span, self.chunk)]

    def faces_x(self, plane):
        n = self.cols
        for r, m in self.chunks():
            rho = self.rho[plane + 1, PAD + r : PAD + r + m, :]
            lane = iota((m, n), 1)
            low = twice_inverse(rho + jnp.where(lane == 0, rho, pltpu.roll(rho, 1, 1)))
            high = jnp.where(lane == n - 1, twice_inverse(rho + rho), pltpu.roll(low, n - 1, 1))
            self.dg[plane, r : r + m, :] = low + high
            self.bx[plane, r : r + m, :] = jnp.where(lane == 0, 0.0, low)

    def faces_y(self, plane):
        for r, m in self.chunks():
            low = self.rho[plane + 1, PAD - 1 + r : PAD - 1 + r + m, :]
            high = self.rho[plane + 1, PAD + r : PAD + r + m, :]
            self.by[plane, r : r + m, :] = twice_inverse(low + high)
        last = self.span[1]
        low = self.rho[plane + 1, PAD - 1 + last : PAD + last, :]
        high = self.rho[plane + 1, PAD + last : PAD + last + 1, :]
        self.by[plane, last : last + 1, :] = twice_inverse(low + high)

    def faces_z(self, face):
        for r, m in self.chunks():
            low = self.rho[face, PAD + r : PAD + r + m, :]
            high = self.rho[face + 1, PAD + r : PAD + r + m, :]
            self.bz[face, r : r + m, :] = twice_inverse(low + high)

    def diagonal(self, plane):
        for r, m in self.chunks():
            total = self.dg[plane, r : r + m, :]
            total = total + self.by[plane, r : r + m, :] + self.by[plane, r + 1 : r + 1 + m, :]
            total = total + self.bz[plane, r : r + m, :] + self.bz[plane + 1, r : r + m, :]
            self.dg[plane, r : r + m, :] = total
            self.idg[plane, r : r + m, :] = (0.5 * OMEGA) * twice_inverse(total)

    def mask_y(self, plane, faces):
        for row, factor in faces:
            self.by[plane, row : row + 1, :] = self.by[plane, row : row + 1, :] * factor

    def mask_z(self, faces):
        for face, factor in faces:
            self.bz[face] = self.bz[face] * factor

    def neighbours(self, val, plane, r, m):
        n = self.cols
        rows = slice(PAD + r, PAD + r + m)
        here = val[plane + 1, rows, :]
        bx = self.bx[plane, r : r + m, :]
        total = self.bz[plane, r : r + m, :] * val[plane, rows, :]
        total = total + self.bz[plane + 1, r : r + m, :] * val[plane + 2, rows, :]
        total = total + self.by[plane, r : r + m, :] * val[plane + 1, PAD - 1 + r : PAD - 1 + r + m, :]
        total = total + self.by[plane, r + 1 : r + 1 + m, :] * val[plane + 1, PAD + 1 + r : PAD + 1 + r + m, :]
        total = total + bx * pltpu.roll(here, 1, 1)
        total = total + pltpu.roll(bx * here, n - 1, 1)
        return here, total


def kernel(
    dens_in, right_in, guess_in, out,
    rho0, val0, smo0, src0, res0, bx0, by0, bz0, dg0, idg0,
    rho1, val1, src1, base1, up1, bx1, by1, bz1, dg1, idg1,
    rho2, val2, base2, up2, bx2, by2, bz2, dg2, idg2,
    rows_out, rows_in, message, inbox_dens, inbox_src, tile, wide_dens, wide_src,
    rho3, bx3, by3, bz3, dg3, dir3, res3, img3, mul3, cor3, pair_tmp, pair_rows, fine_rows, result,
    far_smooth, face_rows, z_out, z_in, y_out, y_in, d_out, d_in, wide_y_out, wide_y_in, wide_d_out, wide_d_in,
    dens_y_out, dens_y_in, dens_d_out, dens_d_in, local_sem, out_sem, send_sem, recv_sem,
):
    gz, gy = lax.axis_index("gz"), lax.axis_index("gy")
    nz, ny = 128, 4
    core, ypos, xpos, zhi = gz % 2, (gz // 2) % 4, (gz // 8) % 4, gz // 32
    zpos = zhi * 4 + gy

    def gz_of(zh, x, y, c):
        return ((zh * 4 + x) * 4 + y) * 2 + c

    up_z, down_z = (gz + 1) % nz, (gz + nz - 1) % nz
    up_y, down_y = (gy + 1) % ny, (gy + ny - 1) % ny
    column = []
    for d in (8, 7, 9, 6, 10, 5, 11, 4, 12, 3, 13, 2, 14, 1, 15, 0):
        for k in range(2):
            if d or k:
                z = (zpos + d) % 16
                column.append((gz_of(z // 4, xpos, ypos, (core + k) % 2), z % 4))
    layer = []
    for i in range(4):
        for j in range(4):
            if i or j:
                layer.append((gz_of(zhi, (xpos + i) % 4, (ypos + j) % 4, core), gy))
    faces = [(up_z, gy), (down_z, gy), (gz, up_y), (gz, down_y)]
    around = []
    for dz in (1, -1):
        for dy in (0, 1, -1):
            around.append((dz, dy, ((gz + dz + nz) % nz, (gy + dy + ny) % ny)))
    corners = [(dz, dy, device) for dz, dy, device in around if dy]
    greeted = column + [device for _, _, device in around] + faces[2:] + layer

    barrier = pltpu.get_barrier_semaphore()
    for device in greeted:
        pl.semaphore_signal(barrier, inc=1, device_id=device, device_id_type=MESH)

    local = []
    for i, (source, target) in enumerate(
        ((dens_in, rho0.at[1:5, 8:40, :]), (guess_in, val0.at[1:5, 8:40, :]), (right_in, src0))
    ):
        copy = pltpu.make_async_copy(source, target, local_sem.at[i])
        copy.start()
        local.append(copy)

    count = [0]

    def send(source, target, device):
        i = count[0]
        count[0] = i + 1
        copy = pltpu.make_async_remote_copy(
            src_ref=source, dst_ref=target, send_sem=send_sem.at[i], recv_sem=recv_sem.at[i],
            device_id=device, device_id_type=MESH,
        )
        copy.start()
        return copy

    def wait_recv(copies):
        for copy in copies:
            copy.wait_recv()

    def wait_send(copies):
        for copy in copies:
            copy.wait_send()

    fine = Level((4, 32, 512), 8, rho0, bx0, by0, bz0, dg0, idg0)
    middle = Level((4, 32, 256), 16, rho1, bx1, by1, bz1, dg1, idg1)
    coarse = Level((5, 24, 128), 8, rho2, bx2, by2, bz2, dg2, idg2)

    z_low = jnp.where(gz > 0, 1.0, 0.0).astype(F32)
    z_high = jnp.where(gz < nz - 1, 1.0, 0.0).astype(F32)
    y_low = jnp.where(gy > 0, 1.0, 0.0).astype(F32)
    y_high = jnp.where(gy < ny - 1, 1.0, 0.0).astype(F32)

    pair_x = pair_matrix()

    def halve_x(blocks):
        rows = sum(block.shape[0] for block in blocks)
        summed = dot(jnp.concatenate([b[:, 0:256] for b in blocks] + [b[:, 256:512] for b in blocks], axis=0), pair_x)
        out, at = [], 0
        for block in blocks:
            n = block.shape[0]
            out.append((summed[at : at + n], summed[rows + at : rows + at + n]))
            at += n
        return out

    def halve_y(slot, value):
        n = value.shape[0]
        pair_rows[slot, 0:n, :] = value
        return pair_rows[slot, pl.ds(0, n // 2, stride=2), :] + pair_rows[slot, pl.ds(1, n // 2, stride=2), :]

    def halve_xy(blocks):
        return [
            jnp.concatenate([halve_y(2 * i, left), halve_y(2 * i + 1, right)], axis=1)
            for i, (left, right) in enumerate(halve_x(blocks))
        ]

    def restrict1(read):
        return halve_y(0, dot(read(0) + read(1), pair_x))

    half_rows, half_cols = iota((128, 256), 0), iota((128, 256), 1)
    to_halves = jnp.where((half_cols % 64 == half_rows // 2) & ((half_cols < 64) | (half_cols >= 192)), 0.125, 0.0).astype(jnp.bfloat16)

    def pack_message(field, value):
        pair_tmp[...] = dot(value, to_halves)
        for r in range(2):
            t = 4 * r
            message[field, r : r + 1, :] = (
                pair_tmp[t : t + 1, 0:128] + pair_tmp[t + 1 : t + 2, 0:128]
                + pair_tmp[t + 2 : t + 3, 128:256] + pair_tmp[t + 3 : t + 4, 128:256]
            )

    def gather_column(field, inbox):
        inbox[zhi, core, gy] = message[field]
        return [send(message.at[field], inbox.at[zhi, core, gy], device) for device in column]

    def gather_layer(field, inbox, wide):
        for zh in range(4):
            for y in range(4):
                tile[field, zh, 2 * y : 2 * y + 2, :] = inbox[zh, 0, y] + inbox[zh, 1, y]
        slot = xpos * 4 + ypos
        wide[slot] = tile[field]
        return [send(tile.at[field], wide.at[slot], device) for device in layer]

    local[0].wait()
    own1 = halve_xy([rho0[2 * k + 1, 8:40, :] + rho0[2 * k + 2, 8:40, :] for k in range(2)])
    for k in range(2):
        rho1[k + 2, 16:32, :] = own1[k]
    own2 = restrict1(lambda k: own1[k])
    rho2[3, 16:24, :] = own2
    pack_message(0, own2)
    local[1].wait()
    for k in range(4):
        for f, ref in ((0, rho0), (1, val0)):
            rows_out[0, f, k : k + 1, :] = ref[k + 1, 39:40, :]
            rows_out[1, f, k : k + 1, :] = ref[k + 1, 8:9, :]

    for way, (row, second) in enumerate(((31, 30), (16, 17))):
        for k in range(2):
            dens_y_out[way, 2 * k : 2 * k + 1, :] = rho1[k + 2, row : row + 1, :]
            dens_y_out[way, 2 * k + 1 : 2 * k + 2, :] = rho1[k + 2, second : second + 1, :]
    for i, (dz, dy, device) in enumerate(corners):
        plane, far_plane = (3, 2) if dz == 1 else (2, 3)
        row, second = (31, 30) if dy == 1 else (16, 17)
        for at, (p, r) in enumerate(((plane, row), (plane, second), (far_plane, row), (far_plane, second))):
            dens_d_out[i, at : at + 1, :] = rho1[p, r : r + 1, :]
    for k in (0, 5):
        smo0[k, 8:40, :] = jnp.zeros((32, 512), F32)
    for k in range(1, 5):
        smo0[k, 7:8, :] = jnp.zeros((1, 512), F32)
        smo0[k, 40:41, :] = jnp.zeros((1, 512), F32)

    pl.semaphore_wait(barrier, len(greeted))

    z_dens = [
        send(rho0.at[4, 8:40, :], rho0.at[0, 8:40, :], faces[0]),
        send(rho0.at[1, 8:40, :], rho0.at[5, 8:40, :], faces[1]),
    ]
    z_vals = [
        send(val0.at[4, 8:40, :], val0.at[0, 8:40, :], faces[0]),
        send(val0.at[1, 8:40, :], val0.at[5, 8:40, :], faces[1]),
    ]
    y_both = [
        send(rows_out.at[0, 0:2], rows_in.at[0, 0:2], faces[2]),
        send(rows_out.at[1, 0:2], rows_in.at[1, 0:2], faces[3]),
    ]

    dens1_copies = [
        send(rho1.at[2:4, 16:32, :], rho1.at[0:2, 16:32, :], faces[0]),
        send(rho1.at[2:4, 16:32, :], rho1.at[4:6, 16:32, :], faces[1]),
        send(dens_y_out.at[0], dens_y_in.at[0], faces[2]),
        send(dens_y_out.at[1], dens_y_in.at[1], faces[3]),
    ]
    for i, (dz, dy, device) in enumerate(corners):
        dens1_copies.append(send(dens_d_out.at[i], dens_d_in.at[i], device))

    rows2 = {dy: (slice(16, 24), slice(16 - 8 * dy, 24 - 8 * dy)) for dy in (0, 1, -1)}
    y_ways = ((1, faces[2]), (-1, faces[3]))
    z_ways = ((1, faces[0]), (-1, faces[1]))

    def fill_y(ref, planes, rows, first):
        last = first + rows - 1
        for k in planes:
            ref[k, first - 1 : first, :] = jnp.where(gy == 0, ref[k, first : first + 1, :], ref[k, first - 1 : first, :])
            ref[k, last + 1 : last + 2, :] = jnp.where(
                gy == ny - 1, ref[k, last : last + 1, :], ref[k, last + 1 : last + 2, :]
            )

    def fill_z(ref, own, planes, rows, reach):
        for i in range(reach):
            low, high = own - 1 - i * planes, own + planes + i * planes
            ref[low, rows, :] = jnp.where(gz == i, ref[low + 1, rows, :], ref[low, rows, :])
            ref[high, rows, :] = jnp.where(gz == nz - 1 - i, ref[high - 1, rows, :], ref[high, rows, :])

    for k in range(4):
        fine.faces_x(k)
    for face in (1, 2, 3):
        fine.faces_z(face)
    wait_recv(y_both)
    for k in range(4):
        for f, ref in ((0, rho0), (1, val0)):
            ref[k + 1, 7:8, :] = rows_in[0, f, k : k + 1, :]
            ref[k + 1, 40:41, :] = rows_in[1, f, k : k + 1, :]
    fill_y(rho0, range(1, 5), 32, 8)
    for k in range(4):
        fine.faces_y(k)
    local[2].wait()

    def smooth(plane):
        for r, m in fine.chunks():
            here, near = fine.neighbours(val0, plane, r, m)
            smo0[plane + 1, 8 + r : 8 + r + m, :] = (1.0 - OMEGA) * here + (
                src0[plane, r : r + m, :] + near
            ) * fine.idg[plane, r : r + m, :]

    for k in (1, 2):
        fine.diagonal(k)
        fine.mask_y(k, ((0, y_low), (32, y_high)))
        smooth(k)
    wait_recv(z_dens)
    fill_z(rho0, 1, 4, slice(8, 40), 1)
    for face in (0, 4):
        fine.faces_z(face)
    for k in (0, 3):
        fine.diagonal(k)
        fine.mask_y(k, ((0, y_low), (32, y_high)))
    fine.mask_z(((0, z_low), (4, z_high)))
    wait_recv(z_vals)
    smooth(3)
    smooth(0)

    for plane in range(4):
        for r, m in fine.chunks():
            here, near = fine.neighbours(smo0, plane, r, m)
            res0[plane, r : r + m, :] = src0[plane, r : r + m, :] - dg0[plane, r : r + m, :] * here + near
    for way, (row, cell) in enumerate(((32, 39), (0, 8))):
        for k in range(2):
            lower = by0[2 * k, row : row + 1, :] * smo0[2 * k + 1, cell : cell + 1, :]
            upper = by0[2 * k + 1, row : row + 1, :] * smo0[2 * k + 2, cell : cell + 1, :]
            face_rows[2 * way + k : 2 * way + k + 1, :] = lower + upper
    blocks = halve_x(
        [res0[0] + res0[1], res0[2] + res0[3], bz0[4] * smo0[4, 8:40, :], bz0[0] * smo0[1, 8:40, :], face_rows[...]]
    )
    part0, part1, give_up, give_down = [
        jnp.concatenate([halve_y(2 * i, left), halve_y(2 * i + 1, right)], axis=1)
        for i, (left, right) in enumerate(blocks[:4])
    ]
    give_rows = jnp.concatenate(blocks[4], axis=1)
    parts = (part0, part1)
    z_out[0, 0] = give_up
    z_out[0, 1] = part1
    z_out[1, 0] = give_down
    z_out[1, 1] = part0
    swap_z = [send(z_out.at[way], z_in.at[way], faces[way]) for way in range(2)]
    for way, row in ((0, 15), (1, 0)):
        for k in range(2):
            y_out[way, k : k + 1, :] = parts[k][row : row + 1]
            y_out[way, 2 + k : 3 + k, :] = give_rows[2 * way + k : 2 * way + k + 1]
    swap_y = [send(y_out.at[way], y_in.at[way], faces[2 + way]) for way in range(2)]
    slot_of, swap_d = {}, []
    for i, (dz, dy, device) in enumerate(corners):
        slot_of[dz, dy] = i
        way = (1 - dy) // 2
        plane = (1 + dz) // 2
        give, row = (give_up if dz == 1 else give_down), (15 if dy == 1 else 0)
        d_out[i, 0:1, :] = give_rows[2 * way + plane : 2 * way + plane + 1]
        d_out[i, 1:2, :] = give[row : row + 1]
        swap_d.append(send(d_out.at[i], d_in.at[i], device))
    column_dens = gather_column(0, inbox_dens)
    dens2_near = [send(rho2.at[3, 16:24, :], rho2.at[3, rows2[dy][1], :], device) for dy, device in y_ways]
    dens2_near += [
        send(rho2.at[3, 16:24, :], rho2.at[3 - dz, rows2[dy][1], :], device) for dz, dy, device in around
    ]

    def coefficients(level, planes, z_faces):
        for k in planes:
            level.faces_x(k)
            level.faces_y(k)
        for k in range(planes[0], planes[-1] + 2):
            level.faces_z(k)
        for k in planes:
            level.diagonal(k)
            level.mask_y(k, ((8, y_low), (level.rows - 8, y_high)))
        level.mask_z(z_faces)

    wait_recv(dens1_copies)
    for way, (row, second) in enumerate(((15, 14), (32, 33))):
        for k in range(2):
            rho1[k + 2, row : row + 1, :] = dens_y_in[way, 2 * k : 2 * k + 1, :]
            rho1[k + 2, second : second + 1, :] = dens_y_in[way, 2 * k + 1 : 2 * k + 2, :]
    for i, (dz, dy, device) in enumerate(corners):
        plane, far_plane = (1, 0) if dz == 1 else (4, 5)
        row, second = (15, 14) if dy == 1 else (32, 33)
        for at, (p, r) in enumerate(((plane, row), (plane, second), (far_plane, row), (far_plane, second))):
            rho1[p, r : r + 1, :] = dens_d_in[i, at : at + 1, :]
    fill_y(rho1, range(6), 16, 16)
    fill_z(rho1, 2, 2, slice(8, 40), 1)
    coefficients(middle, range(4), ((1, z_low), (3, z_high)))
    wait_recv(dens2_near)
    fill_y(rho2, (3,), 8, 16)
    fill_z(rho2, 3, 1, slice(16, 24), 1)
    coarse.span = (8, 16)
    coefficients(coarse, (2,), ((2, z_low), (3, z_high)))
    coarse.span = (0, 24)

    wait_recv(swap_z + swap_y + swap_d)
    source1 = []
    for k in range(2):
        src1[k + 2, 16:32, :] = parts[k] + z_in[k, 0]
        src1[k + 2, 16:17, :] = src1[k + 2, 16:17, :] + y_in[0, 2 + k : 3 + k, :]
        src1[k + 2, 31:32, :] = src1[k + 2, 31:32, :] + y_in[1, 2 + k : 3 + k, :]
        source1.append(src1[k + 2, 16:32, :])
        val1[k + 2, 16:32, :] = 4.0 * source1[k] * idg1[k + 1, 8:24, :]
    for dz, plane, theirs, mine in ((1, 4, z_in[1, 1], give_up), (-1, 1, z_in[0, 1], give_down)):
        src1[plane, 16:32, :] = theirs + mine
        low, high = slot_of[-dz, 1], slot_of[-dz, -1]
        src1[plane, 16:17, :] = src1[plane, 16:17, :] + d_in[low, 0:1, :]
        src1[plane, 31:32, :] = src1[plane, 31:32, :] + d_in[high, 0:1, :]
        val1[plane, 16:32, :] = 4.0 * src1[plane, 16:32, :] * idg1[plane - 1, 8:24, :]
    for dy, row in ((1, 32), (-1, 15)):
        way = (1 - dy) // 2
        for k, dz in ((0, -1), (1, 1)):
            total = y_in[1 - way, k : k + 1, :] + give_rows[2 * way + k : 2 * way + k + 1]
            total = total + d_in[slot_of[-dz, -dy], 1:2, :]
            src1[k + 2, row : row + 1, :] = total
            val1[k + 2, row : row + 1, :] = 4.0 * total * idg1[k + 1, row - 8 : row - 7, :]

    def residual1(k):
        here, near = middle.neighbours(val1, k + 1, 8, 16)
        base1[k + 2, 16:32, :] = (1.0 - OMEGA) * here + (4.0 * source1[k] + near) * idg1[k + 1, 8:24, :]
        return (1.0 - OMEGA) * source1[k] + 0.25 * near

    source2 = restrict1(residual1)
    val2[3, 16:24, :] = 16.0 * source2 * idg2[2, 8:16, :]
    copies2 = [send(val2.at[3, 16:24, :], val2.at[3, rows2[dy][1], :], device) for dy, device in y_ways]
    for dz, device in z_ways:
        copies2.append(send(val2.at[3, 16:24, :], val2.at[3 - dz, 16:24, :], device))

    def pass_on(ref, reach):
        return [
            send(ref.at[4 - reach, 8:32, :], ref.at[3 - reach, 8:32, :], faces[0]),
            send(ref.at[2 + reach, 8:32, :], ref.at[3 + reach, 8:32, :], faces[1]),
        ]

    dens2_far = pass_on(rho2, 2)
    more1 = [
        send(base1.at[3, 16:32, :], base1.at[1, 16:32, :], faces[0]),
        send(base1.at[2, 16:32, :], base1.at[4, 16:32, :], faces[1]),
    ]
    for way, row in ((0, 31), (1, 16)):
        for k in range(2):
            wide_y_out[way, k : k + 1, :] = base1[k + 2, row : row + 1, :]
        more1.append(send(wide_y_out.at[way], wide_y_in.at[way], faces[2 + way]))
    for i, (dz, dy, device) in enumerate(corners):
        plane, row = (3 if dz == 1 else 2), (31 if dy == 1 else 16)
        wide_d_out[i] = base1[plane, row : row + 1, :]
        more1.append(send(wide_d_out.at[i], wide_d_in.at[i], device))
    wait_recv(column_dens)
    layer_dens = gather_layer(0, inbox_dens, wide_dens)
    wait_recv(copies2)
    here, near = coarse.neighbours(val2, 2, 8, 8)
    pack_message(1, (1.0 - OMEGA) * source2 + 0.0625 * near)
    base2[3, 16:24, :] = (1.0 - OMEGA) * here + (16.0 * source2 + near) * idg2[2, 8:16, :]
    column_src = gather_column(1, inbox_src)
    more2 = [send(base2.at[3, 16:24, :], base2.at[3, rows2[dy][1], :], device) for dy, device in y_ways]
    more2 += [send(base2.at[3, 16:24, :], base2.at[3 - dz, rows2[dy][1], :], device) for dz, dy, device in around]
    wait_recv(dens2_far)
    dens2_last = pass_on(rho2, 3)

    wait_recv(layer_dens)
    lane, sub = iota((8, 128), 1), iota((8, 128), 0)
    right_half = lane >= 64
    first_x, last_x = (lane % 64) == 0, (lane % 64) == 63
    first_y, last_y = (lane < 64) & (sub == 0), (lane >= 64) & (sub == 7)

    def lower_y(v):
        q = pltpu.roll(v, 64, 1)
        return jnp.where(right_half, q, pltpu.roll(q, 1, 0))

    def upper_y(v):
        q = pltpu.roll(v, 64, 1)
        return jnp.where(right_half, pltpu.roll(q, 7, 0), q)

    scale3 = 0.015625
    for zh in range(4):
        for s in range(16):
            rho3[1 + 16 * zh + s] = wide_dens[s, zh]
    rho3[0] = rho3[1]
    rho3[65] = rho3[64]

    def face3(k, _):
        bz3[k] = scale3 * twice_inverse(rho3[k] + rho3[k + 1])
        return 0

    lax.fori_loop(0, 65, face3, 0)

    def coef3(k, _):
        rho = rho3[k + 1]
        edge = twice_inverse(rho + rho)
        low = twice_inverse(rho + jnp.where(first_x, rho, pltpu.roll(rho, 1, 1)))
        total = low + jnp.where(last_x, edge, pltpu.roll(low, 127, 1))
        bx3[k] = jnp.where(first_x, 0.0, scale3 * low)
        low = twice_inverse(rho + jnp.where(first_y, rho, lower_y(rho)))
        total = total + low + jnp.where(last_y, edge, upper_y(low))
        by3[k] = jnp.where(first_y, 0.0, scale3 * low)
        dg3[k] = scale3 * total + bz3[k] + bz3[k + 1]
        return 0

    lax.fori_loop(0, 64, coef3, 0, unroll=4)

    zero_plane = jnp.zeros((8, 128), F32)
    for k in (0, 1, 66, 67):
        cor3[k] = zero_plane

    def clear3(k, _):
        dir3[k] = zero_plane
        mul3[k] = zero_plane
        cor3[k + 2] = zero_plane
        return 0

    lax.fori_loop(0, 64, clear3, 0, unroll=8)
    for ref in (dir3, mul3, res3, img3):
        ref[64] = zero_plane

    wait_recv(column_src)
    layer_src = gather_layer(1, inbox_src, wide_src)

    z_smooth = [
        send(smo0.at[4, 8:40, :], far_smooth.at[0], faces[0]), send(smo0.at[1, 8:40, :], far_smooth.at[1], faces[1])
    ]
    for k in range(4):
        rows_out[0, 2, k : k + 1, :] = smo0[k + 1, 39:40, :]
        rows_out[1, 2, k : k + 1, :] = smo0[k + 1, 8:9, :]
    y_smooth = [send(rows_out.at[way, 2], rows_in.at[way, 2], faces[2 + way]) for way in range(2)]
    wait_recv(more2)
    base2_far = pass_on(base2, 2)

    wait_recv(dens2_last)
    wait_send(dens2_near + dens2_far + dens2_last)

    def inside_z(face):
        at = gz + face - 2
        return jnp.where((at > 0) & (at < nz), 1.0, 0.0).astype(F32)

    fill_y(rho2, range(7), 8, 16)
    fill_z(rho2, 3, 1, slice(8, 32), 3)
    coefficients(coarse, range(5), [(face, inside_z(face)) for face in range(6)])

    wait_recv(layer_src)

    for zh in range(4):
        for k in range(16):
            res3[16 * zh + k] = wide_src[k, zh]

    def whole(v):
        return jnp.sum(jnp.sum(v, axis=1, keepdims=True), axis=0, keepdims=True)

    def apply(k, prev, here, later):
        bx, by = bx3[k], by3[k]
        image = (dg3[k] * here - bz3[k] * prev) - (bz3[k + 1] * later + by * lower_y(here))
        image = image - ((bx * pltpu.roll(here, 1, 1) + upper_y(by * here)) + pltpu.roll(bx * here, 127, 1))
        img3[k] = image
        return image

    def advance(k, alpha, beta):
        direction = res3[k] + beta * dir3[k]
        dir3[k] = direction
        cor3[k + 2] = cor3[k + 2] + alpha * direction
        image = img3[k] + beta * mul3[k]
        mul3[k] = image
        resid = res3[k] - alpha * image
        res3[k] = resid
        return resid

    def totals(first, next_resid):
        def plane(k, carry):
            norm, power, prev, here = carry
            later = next_resid(k + 1)
            image = apply(k, prev, here, later)
            return norm + here * here, power + here * image, here, later

        norm, power, _, _ = lax.fori_loop(0, 64, plane, (zero_plane, zero_plane, zero_plane, first), unroll=64)
        return whole(norm), whole(power)

    norm, power = totals(res3[0], lambda k: res3[k])

    def sweep(step, carry):
        alpha, beta, norm = carry
        norm_next, power = totals(advance(0, alpha, beta), lambda k: advance(k, alpha, beta))
        beta = norm_next / norm
        return norm_next / (power - beta * norm_next / alpha), beta, norm_next

    alpha, beta, _ = lax.fori_loop(0, SWEEPS - 1, sweep, (norm / power, jnp.zeros((1, 1), F32), norm))

    def finish(k, _):
        cor3[k + 2] = cor3[k + 2] + alpha * (res3[k] + beta * dir3[k])
        return 0

    lax.fori_loop(0, 64, finish, 0, unroll=16)

    spread_rows, spread_cols = iota((128, 256), 0), iota((128, 256), 1)
    fine_x = spread_cols % 128
    parent = fine_x // 2
    near = parent + 2 * (fine_x % 2) - 1
    half = spread_cols // 128
    inside = (near >= 0) & (near < 64)
    from_halves = (
        jnp.where(spread_rows == parent + 64 * half, 0.75, 0.0)
        + jnp.where((spread_rows == near + 64 * half) & inside, 0.25, 0.0)
    ).astype(jnp.bfloat16)
    mixed = []
    for d in range(-3, 4):
        plane = gz + d + 4
        index = plane // 2
        other = index + 2 * (plane % 2) - 1
        mixed.append(0.75 * cor3[index] + 0.25 * cor3[other])
    x_done = dot(jnp.concatenate(mixed, axis=0), from_halves)
    wait_recv(more1 + base2_far + z_smooth + y_smooth)
    wait_send(more1 + more2 + base2_far + z_smooth)
    for way, row in ((0, 15), (1, 32)):
        for k in range(2):
            base1[k + 2, row : row + 1, :] = wide_y_in[way, k : k + 1, :]
    for i, (dz, dy, _) in enumerate(corners):
        plane, row = (1 if dz == 1 else 4), (15 if dy == 1 else 32)
        base1[plane, row : row + 1, :] = wide_d_in[i]
    first_row, last_row = iota((8, 128), 0) == 0, iota((8, 128), 0) == 7
    window = pl.ds(pl.multiple_of(8 * gy, 8), 24)
    for k in range(7):
        even, odd = x_done[8 * k : 8 * k + 8, 0:128], x_done[8 * k : 8 * k + 8, 128:256]
        fine_rows[k, 0:8, :] = zero_plane
        fine_rows[k, 40:48, :] = zero_plane
        below = jnp.where(first_row, 0.0, pltpu.roll(odd, 1, 0))
        above = jnp.where(last_row, 0.0, pltpu.roll(even, 7, 0))
        fine_rows[k, pl.ds(8, 8, stride=4), :] = 0.75 * even + 0.25 * below
        fine_rows[k, pl.ds(9, 8, stride=4), :] = 0.75 * even + 0.25 * odd
        fine_rows[k, pl.ds(10, 8, stride=4), :] = 0.75 * odd + 0.25 * even
        fine_rows[k, pl.ds(11, 8, stride=4), :] = 0.75 * odd + 0.25 * above
        up2[k, 8:32, :] = fine_rows[k, window, :]

    def in_grid(shape, margin, first_row, rows, plane, planes):
        row = iota(shape, 0)
        at = row + first_row
        good = (row >= margin) & (row < shape[0] - margin) & (at >= 0) & (at < rows)
        return good & (plane >= 0) & (plane < planes)

    ups = []
    for k in range(5):
        here, near = coarse.neighbours(up2, k, 0, 24)
        up = base2[k + 1, 8:32, :] + (1.0 - OMEGA) * here + near * idg2[k]
        ups.append(jnp.where(in_grid((24, 128), 1, 8 * gy - 8, 8 * ny, gz + k - 2, nz), up, 0.0))

    spread_x1, spread_x0 = spread_matrix(128), spread_matrix(256)

    def prolong(ups, target, first, rows, spread_x, add):
        height = ups[0].shape[0]
        tall = 2 * height - 16
        n = height - 8
        x_done = dot(jnp.concatenate(ups, axis=0), spread_x)
        tiles = x_done.shape[1] // 128
        for t in range(tiles):
            for k in range(len(ups)):
                pair_rows[t, 0:height, :] = x_done[height * k : height * (k + 1), 128 * t : 128 * (t + 1)]
                here = 0.75 * pair_rows[t, 4 : 4 + n, :]
                fine_rows[k, pl.ds(0, n, stride=2), :] = here + 0.25 * pair_rows[t, 3 : 3 + n, :]
                fine_rows[k, pl.ds(1, n, stride=2), :] = here + 0.25 * pair_rows[t, 5 : 5 + n, :]
            cols = slice(128 * t, 128 * (t + 1))
            for k in range(6):
                parent_z = (k + first) // 2
                near_z = parent_z + 2 * ((k + first) % 2) - 1
                value = 0.75 * fine_rows[parent_z, 0:tall, :] + 0.25 * fine_rows[near_z, 0:tall, :]
                target[k, rows, cols] = target[k, rows, cols] + value if add else value

    prolong(ups, up1, 2, slice(8, 40), spread_x1, False)
    ups = []
    for k in range(4):
        parts = []
        for r, m in middle.chunks():
            here, near = middle.neighbours(up1, k, r, m)
            base = base1[k + 1, 8 + r : 8 + r + m, :]
            parts.append(base + (1.0 - OMEGA) * here + near * idg1[k, r : r + m, :])
        up = jnp.concatenate(parts, axis=0)
        ups.append(jnp.where(in_grid((32, 256), 7, 16 * gy - 8, 16 * ny, 2 * gz + k - 1, 2 * nz), up, 0.0))
    for k, plane in ((0, 0), (1, 5)):
        smo0[plane, 8:40, :] = far_smooth[k]
    for k in range(4):
        smo0[k + 1, 7:8, :] = rows_in[0, 2, k : k + 1, :]
        smo0[k + 1, 40:41, :] = rows_in[1, 2, k : k + 1, :]
    prolong(ups, smo0, 1, slice(0, 48), spread_x0, True)
    outgoing = []
    for k in range(4):
        for r, m in fine.chunks():
            here, near = fine.neighbours(smo0, k, r, m)
            result[k, r : r + m, :] = (1.0 - OMEGA) * here + (src0[k, r : r + m, :] + near) * fine.idg[k, r : r + m, :]
        copy = pltpu.make_async_copy(result.at[k], out.at[k], out_sem.at[k])
        copy.start()
        outgoing.append(copy)

    wait_send(
        z_dens + z_vals + y_both + dens1_copies + copies2 + column_dens + y_smooth + layer_dens
        + column_src + layer_src + swap_z + swap_y + swap_d
    )
    for copy in outgoing:
        copy.wait()


def coefficient_scratch(planes, rows, cols):
    own = pltpu.VMEM((planes, rows, cols), F32)
    return [own, pltpu.VMEM((planes, rows + 8, cols), F32), pltpu.VMEM((planes + 1, rows, cols), F32), own, own]


COPIES = 6 + 8 + 8 + 8 + 2 + 2 + 4 + 4 + 8 + 8 + 2 + 62 + 30


def per_device(density, right_side, pressure_guess):
    coarsest, longer = pltpu.VMEM((64, 8, 128), F32), pltpu.VMEM((65, 8, 128), F32)
    return pl.pallas_call(
        kernel,
        out_shape=jax.ShapeDtypeStruct(density.shape, F32),
        in_specs=[pl.BlockSpec(memory_space=pltpu.HBM)] * 3,
        out_specs=pl.BlockSpec(memory_space=pltpu.HBM),
        scratch_shapes=[
            *[pltpu.VMEM((6, 48, 512), F32)] * 3,
            *[pltpu.VMEM((4, 32, 512), F32)] * 2,
            *coefficient_scratch(4, 32, 512),
            pltpu.VMEM((6, 48, 256), F32),
            *[pltpu.VMEM((6, 48, 256), F32)] * 4,
            *coefficient_scratch(4, 32, 256),
            pltpu.VMEM((7, 40, 128), F32),
            *[pltpu.VMEM((7, 40, 128), F32)] * 3,
            *coefficient_scratch(5, 24, 128),
            pltpu.VMEM((2, 3, 4, 512), F32),
            pltpu.VMEM((2, 3, 4, 512), F32),
            pltpu.VMEM((2, 2, 128), F32),
            pltpu.VMEM((4, 2, 4, 2, 128), F32),
            pltpu.VMEM((4, 2, 4, 2, 128), F32),
            pltpu.VMEM((2, 4, 8, 128), F32),
            pltpu.VMEM((16, 4, 8, 128), F32),
            pltpu.VMEM((16, 4, 8, 128), F32),
            pltpu.VMEM((66, 8, 128), F32),
            coarsest, coarsest, longer, coarsest,
            longer, longer, longer, longer, pltpu.VMEM((68, 8, 128), F32),
            pltpu.VMEM((8, 256), F32),
            pltpu.VMEM((8, 32, 128), F32),
            pltpu.VMEM((7, 48, 128), F32),
            pltpu.VMEM((4, 32, 512), F32),
            pltpu.VMEM((2, 32, 512), F32),
            pltpu.VMEM((8, 512), F32),
            *[pltpu.VMEM((2, 2, 16, 256), F32)] * 2,
            *[pltpu.VMEM((2, 4, 256), F32)] * 2,
            *[pltpu.VMEM((4, 2, 256), F32)] * 2,
            *[pltpu.VMEM((2, 2, 256), F32)] * 2,
            *[pltpu.VMEM((4, 1, 256), F32)] * 2,
            *[pltpu.VMEM((2, 4, 256), F32)] * 2,
            *[pltpu.VMEM((4, 4, 256), F32)] * 2,
            pltpu.SemaphoreType.DMA((3,)),
            pltpu.SemaphoreType.DMA((4,)),
            pltpu.SemaphoreType.DMA((COPIES,)),
            pltpu.SemaphoreType.DMA((COPIES,)),
        ],
        compiler_params=pltpu.CompilerParams(
            collective_id=0, has_side_effects=True, vmem_limit_bytes=32 * 1024 * 1024
        ),
        cost_estimate=pl.CostEstimate(flops=20_000_000, bytes_accessed=1 << 20, transcendentals=0),
    )(*[pltpu.with_memory_space_constraint(a, pltpu.HBM) for a in (density, right_side, pressure_guess)])


def solution(mesh):
    spec = P("gz", "gy", None)
    return jax.shard_map(per_device, mesh=mesh, in_specs=(spec, spec, spec), out_specs=spec, check_vma=False)
```

```python
import functools

import jax
import jax.numpy as jnp
from jax import lax
from jax.experimental import pallas as pl
from jax.experimental.pallas import tpu as pltpu
from jax.sharding import PartitionSpec as P

MESH = pl.DeviceIdType.MESH
SWEEPS = 8
OMEGA = 0.8
F32 = jnp.float32
PAD = 8


def dot(values, weights):
    rows = values.shape[0]
    if rows % 16:
        values = jnp.concatenate([values, jnp.zeros((16 - rows % 16, values.shape[1]), F32)], axis=0)
    total = values.shape[0]
    first = values.astype(jnp.bfloat16).astype(F32)
    rest = values - first
    second = rest.astype(jnp.bfloat16).astype(F32)
    parts = jnp.concatenate([first, second, rest - second], axis=0).astype(jnp.bfloat16)
    out = jnp.dot(parts, weights, preferred_element_type=F32)
    return (out[0:total] + out[total : 2 * total] + out[2 * total :])[0:rows]


def twice_inverse(total):
    guess = pltpu.reciprocal(total, approx=True)
    return guess * (4.0 - 2.0 * total * guess)


def iota(shape, axis):
    return lax.broadcasted_iota(jnp.int32, shape, axis)


def pair_matrix():
    rows, cols = iota((256, 128), 0), iota((256, 128), 1)
    return jnp.where(rows // 2 == cols, 0.125, 0.0).astype(jnp.bfloat16)


def spread_matrix(coarse):
    rows, cols = iota((coarse, 2 * coarse), 0), iota((coarse, 2 * coarse), 1)
    parent = cols // 2
    near = parent + 2 * (cols % 2) - 1
    return (jnp.where(rows == parent, 0.75, 0.0) + jnp.where(rows == near, 0.25, 0.0)).astype(jnp.bfloat16)


class Level:
    def __init__(self, shape, chunk, rho, bx, by, bz, dg, idg):
        self.planes, self.rows, self.cols = shape
        self.chunk = chunk
        self.rho, self.bx, self.by, self.bz, self.dg, self.idg = rho, bx, by, bz, dg, idg

        self.span = (0, self.rows)

    def chunks(self):
        return [(r, self.chunk) for r in range(*self.span, self.chunk)]

    def faces_x(self, plane):
        n = self.cols
        for r, m in self.chunks():
            rho = self.rho[plane + 1, PAD + r : PAD + r + m, :]
            lane = iota((m, n), 1)
            low = twice_inverse(rho + jnp.where(lane == 0, rho, pltpu.roll(rho, 1, 1)))
            high = jnp.where(lane == n - 1, twice_inverse(rho + rho), pltpu.roll(low, n - 1, 1))
            self.dg[plane, r : r + m, :] = low + high
            self.bx[plane, r : r + m, :] = jnp.where(lane == 0, 0.0, low)

    def faces_y(self, plane):
        for r, m in self.chunks():
            low = self.rho[plane + 1, PAD - 1 + r : PAD - 1 + r + m, :]
            high = self.rho[plane + 1, PAD + r : PAD + r + m, :]
            self.by[plane, r : r + m, :] = twice_inverse(low + high)
        last = self.span[1]
        low = self.rho[plane + 1, PAD - 1 + last : PAD + last, :]
        high = self.rho[plane + 1, PAD + last : PAD + last + 1, :]
        self.by[plane, last : last + 1, :] = twice_inverse(low + high)

    def faces_z(self, face):
        for r, m in self.chunks():
            low = self.rho[face, PAD + r : PAD + r + m, :]
            high = self.rho[face + 1, PAD + r : PAD + r + m, :]
            self.bz[face, r : r + m, :] = twice_inverse(low + high)

    def diagonal(self, plane):
        for r, m in self.chunks():
            total = self.dg[plane, r : r + m, :]
            total = total + self.by[plane, r : r + m, :] + self.by[plane, r + 1 : r + 1 + m, :]
            total = total + self.bz[plane, r : r + m, :] + self.bz[plane + 1, r : r + m, :]
            self.dg[plane, r : r + m, :] = total
            self.idg[plane, r : r + m, :] = (0.5 * OMEGA) * twice_inverse(total)

    def mask_y(self, plane, faces):
        for row, factor in faces:
            self.by[plane, row : row + 1, :] = self.by[plane, row : row + 1, :] * factor

    def mask_z(self, faces):
        for face, factor in faces:
            self.bz[face] = self.bz[face] * factor

    def neighbours(self, val, plane, r, m):
        n = self.cols
        rows = slice(PAD + r, PAD + r + m)
        here = val[plane + 1, rows, :]
        bx = self.bx[plane, r : r + m, :]
        total = self.bz[plane, r : r + m, :] * val[plane, rows, :]
        total = total + self.bz[plane + 1, r : r + m, :] * val[plane + 2, rows, :]
        total = total + self.by[plane, r : r + m, :] * val[plane + 1, PAD - 1 + r : PAD - 1 + r + m, :]
        total = total + self.by[plane, r + 1 : r + 1 + m, :] * val[plane + 1, PAD + 1 + r : PAD + 1 + r + m, :]
        total = total + bx * pltpu.roll(here, 1, 1)
        total = total + pltpu.roll(bx * here, n - 1, 1)
        return here, total


def kernel(
    dens_in, right_in, guess_in, out,
    rho0, val0, smo0, src0, res0, bx0, by0, bz0, dg0, idg0,
    rho1, val1, src1, base1, up1, bx1, by1, bz1, dg1, idg1,
    rho2, val2, base2, up2, bx2, by2, bz2, dg2, idg2,
    rows_out, rows_in, message, inbox_dens, inbox_src, tile, wide_dens, wide_src,
    rho3, bx3, by3, bz3, dg3, dir3, res3, img3, mul3, cor3, pair_tmp, pair_rows, fine_rows,
    far_smooth, face_rows, z_out, z_in, y_out, y_in, d_out, d_in, wide_y_out, wide_y_in, wide_d_out, wide_d_in,
    dens_y_out, dens_y_in, dens_d_out, dens_d_in, local_sem, send_sem, recv_sem,
):
    gz, gy = lax.axis_index("gz"), lax.axis_index("gy")
    nz, ny = 128, 4
    core, ypos, xpos, zhi = gz % 2, (gz // 2) % 4, (gz // 8) % 4, gz // 32
    zpos = zhi * 4 + gy

    def gz_of(zh, x, y, c):
        return ((zh * 4 + x) * 4 + y) * 2 + c

    up_z, down_z = (gz + 1) % nz, (gz + nz - 1) % nz
    up_y, down_y = (gy + 1) % ny, (gy + ny - 1) % ny
    column = []
    for d in (8, 7, 9, 6, 10, 5, 11, 4, 12, 3, 13, 2, 14, 1, 15, 0):
        for k in range(2):
            if d or k:
                z = (zpos + d) % 16
                column.append((gz_of(z // 4, xpos, ypos, (core + k) % 2), z % 4))
    layer = []
    for i in (2, 1, 3, 0):
        for j in (2, 1, 3, 0):
            if i or j:
                layer.append((gz_of(zhi, (xpos + i) % 4, (ypos + j) % 4, core), gy))
    faces = [(up_z, gy), (down_z, gy), (gz, up_y), (gz, down_y)]
    around = []
    for dz in (1, -1):
        for dy in (0, 1, -1):
            around.append((dz, dy, ((gz + dz + nz) % nz, (gy + dy + ny) % ny)))
    corners = [(dz, dy, device) for dz, dy, device in around if dy]
    greeted = column + [device for _, _, device in around] + faces[2:] + layer

    barrier = pltpu.get_barrier_semaphore()
    for device in greeted:
        pl.semaphore_signal(barrier, inc=1, device_id=device, device_id_type=MESH)

    local = []
    for i, (source, target) in enumerate(
        ((dens_in, rho0.at[1:5, 8:40, :]), (guess_in, val0.at[1:5, 8:40, :]), (right_in, src0))
    ):
        copy = pltpu.make_async_copy(source, target, local_sem.at[i])
        copy.start()
        local.append(copy)

    count = [0]

    def send(source, target, device):
        i = count[0]
        count[0] = i + 1
        copy = pltpu.make_async_remote_copy(
            src_ref=source, dst_ref=target, send_sem=send_sem.at[i], recv_sem=recv_sem.at[i],
            device_id=device, device_id_type=MESH,
        )
        copy.start()
        return copy

    def wait_recv(copies):
        for copy in copies:
            copy.wait_recv()

    def wait_send(copies):
        for copy in copies:
            copy.wait_send()

    fine = Level((4, 32, 512), 8, rho0, bx0, by0, bz0, dg0, idg0)
    middle = Level((4, 32, 256), 16, rho1, bx1, by1, bz1, dg1, idg1)
    coarse = Level((5, 24, 128), 8, rho2, bx2, by2, bz2, dg2, idg2)

    z_low = jnp.where(gz > 0, 1.0, 0.0).astype(F32)
    z_high = jnp.where(gz < nz - 1, 1.0, 0.0).astype(F32)
    y_low = jnp.where(gy > 0, 1.0, 0.0).astype(F32)
    y_high = jnp.where(gy < ny - 1, 1.0, 0.0).astype(F32)

    pair_x = pair_matrix()

    def halve_x(blocks):
        rows = sum(block.shape[0] for block in blocks)
        summed = dot(jnp.concatenate([b[:, 0:256] for b in blocks] + [b[:, 256:512] for b in blocks], axis=0), pair_x)
        out, at = [], 0
        for block in blocks:
            n = block.shape[0]
            out.append((summed[at : at + n], summed[rows + at : rows + at + n]))
            at += n
        return out

    def halve_y(slot, value):
        n = value.shape[0]
        pair_rows[slot, 0:n, :] = value
        return pair_rows[slot, pl.ds(0, n // 2, stride=2), :] + pair_rows[slot, pl.ds(1, n // 2, stride=2), :]

    def halve_xy(blocks):
        return [
            jnp.concatenate([halve_y(2 * i, left), halve_y(2 * i + 1, right)], axis=1)
            for i, (left, right) in enumerate(halve_x(blocks))
        ]

    def restrict1(read):
        return halve_y(0, dot(read(0) + read(1), pair_x))

    half_rows, half_cols = iota((128, 256), 0), iota((128, 256), 1)
    to_halves = jnp.where((half_cols % 64 == half_rows // 2) & ((half_cols < 64) | (half_cols >= 192)), 0.125, 0.0).astype(jnp.bfloat16)

    def pack_message(field, value):
        pair_tmp[...] = dot(value, to_halves)
        for r in range(2):
            t = 4 * r
            message[field, r : r + 1, :] = (
                pair_tmp[t : t + 1, 0:128] + pair_tmp[t + 1 : t + 2, 0:128]
                + pair_tmp[t + 2 : t + 3, 128:256] + pair_tmp[t + 3 : t + 4, 128:256]
            )

    def gather_column(field, inbox):
        inbox[zhi, core, gy] = message[field]
        return [send(message.at[field], inbox.at[zhi, core, gy], device) for device in column]

    def gather_layer(field, inbox, wide):
        for zh in range(4):
            for y in range(4):
                tile[field, zh, 2 * y : 2 * y + 2, :] = inbox[zh, 0, y] + inbox[zh, 1, y]
        slot = xpos * 4 + ypos
        wide[slot] = tile[field]
        return [send(tile.at[field], wide.at[slot], device) for device in layer]

    local[0].wait()
    own1 = halve_xy([rho0[2 * k + 1, 8:40, :] + rho0[2 * k + 2, 8:40, :] for k in range(2)])
    for k in range(2):
        rho1[k + 2, 16:32, :] = own1[k]
    own2 = restrict1(lambda k: own1[k])
    rho2[3, 16:24, :] = own2
    pack_message(0, own2)
    local[1].wait()
    for k in range(4):
        for f, ref in ((0, rho0), (1, val0)):
            rows_out[0, f, k : k + 1, :] = ref[k + 1, 39:40, :]
            rows_out[1, f, k : k + 1, :] = ref[k + 1, 8:9, :]

    for way, (row, second) in enumerate(((31, 30), (16, 17))):
        for k in range(2):
            dens_y_out[way, 2 * k : 2 * k + 1, :] = rho1[k + 2, row : row + 1, :]
            dens_y_out[way, 2 * k + 1 : 2 * k + 2, :] = rho1[k + 2, second : second + 1, :]
    for i, (dz, dy, device) in enumerate(corners):
        plane, far_plane = (3, 2) if dz == 1 else (2, 3)
        row, second = (31, 30) if dy == 1 else (16, 17)
        for at, (p, r) in enumerate(((plane, row), (plane, second), (far_plane, row), (far_plane, second))):
            dens_d_out[i, at : at + 1, :] = rho1[p, r : r + 1, :]
    for k in (0, 5):
        smo0[k, 8:40, :] = jnp.zeros((32, 512), F32)
    for k in range(1, 5):
        smo0[k, 7:8, :] = jnp.zeros((1, 512), F32)
        smo0[k, 40:41, :] = jnp.zeros((1, 512), F32)

    pl.semaphore_wait(barrier, len(greeted))

    z_dens = [
        send(rho0.at[4, 8:40, :], rho0.at[0, 8:40, :], faces[0]),
        send(rho0.at[1, 8:40, :], rho0.at[5, 8:40, :], faces[1]),
    ]
    z_vals = [
        send(val0.at[4, 8:40, :], val0.at[0, 8:40, :], faces[0]),
        send(val0.at[1, 8:40, :], val0.at[5, 8:40, :], faces[1]),
    ]
    y_both = [
        send(rows_out.at[0, 0:2], rows_in.at[0, 0:2], faces[2]),
        send(rows_out.at[1, 0:2], rows_in.at[1, 0:2], faces[3]),
    ]

    dens1_copies = [
        send(rho1.at[2:4, 16:32, :], rho1.at[0:2, 16:32, :], faces[0]),
        send(rho1.at[2:4, 16:32, :], rho1.at[4:6, 16:32, :], faces[1]),
        send(dens_y_out.at[0], dens_y_in.at[0], faces[2]),
        send(dens_y_out.at[1], dens_y_in.at[1], faces[3]),
    ]
    for i, (dz, dy, device) in enumerate(corners):
        dens1_copies.append(send(dens_d_out.at[i], dens_d_in.at[i], device))

    rows2 = {dy: (slice(16, 24), slice(16 - 8 * dy, 24 - 8 * dy)) for dy in (0, 1, -1)}
    y_ways = ((1, faces[2]), (-1, faces[3]))
    z_ways = ((1, faces[0]), (-1, faces[1]))

    def fill_y(ref, planes, rows, first):
        last = first + rows - 1
        for k in planes:
            ref[k, first - 1 : first, :] = jnp.where(gy == 0, ref[k, first : first + 1, :], ref[k, first - 1 : first, :])
            ref[k, last + 1 : last + 2, :] = jnp.where(
                gy == ny - 1, ref[k, last : last + 1, :], ref[k, last + 1 : last + 2, :]
            )

    def fill_z(ref, own, planes, rows, reach):
        for i in range(reach):
            low, high = own - 1 - i * planes, own + planes + i * planes
            ref[low, rows, :] = jnp.where(gz == i, ref[low + 1, rows, :], ref[low, rows, :])
            ref[high, rows, :] = jnp.where(gz == nz - 1 - i, ref[high - 1, rows, :], ref[high, rows, :])

    for k in range(4):
        fine.faces_x(k)
    for face in (1, 2, 3):
        fine.faces_z(face)
    wait_recv(y_both)
    for k in range(4):
        for f, ref in ((0, rho0), (1, val0)):
            ref[k + 1, 7:8, :] = rows_in[0, f, k : k + 1, :]
            ref[k + 1, 40:41, :] = rows_in[1, f, k : k + 1, :]
    fill_y(rho0, range(1, 5), 32, 8)
    for k in range(4):
        fine.faces_y(k)
    local[2].wait()

    def smooth(plane):
        for r, m in fine.chunks():
            here, near = fine.neighbours(val0, plane, r, m)
            smo0[plane + 1, 8 + r : 8 + r + m, :] = (1.0 - OMEGA) * here + (
                src0[plane, r : r + m, :] + near
            ) * fine.idg[plane, r : r + m, :]

    for k in (1, 2):
        fine.diagonal(k)
        fine.mask_y(k, ((0, y_low), (32, y_high)))
        smooth(k)
    wait_recv(z_dens)
    fill_z(rho0, 1, 4, slice(8, 40), 1)
    for face in (0, 4):
        fine.faces_z(face)
    for k in (0, 3):
        fine.diagonal(k)
        fine.mask_y(k, ((0, y_low), (32, y_high)))
    fine.mask_z(((0, z_low), (4, z_high)))
    wait_recv(z_vals)
    smooth(3)
    smooth(0)

    for plane in range(4):
        for r, m in fine.chunks():
            here, near = fine.neighbours(smo0, plane, r, m)
            res0[plane, r : r + m, :] = src0[plane, r : r + m, :] - dg0[plane, r : r + m, :] * here + near
    for way, (row, cell) in enumerate(((32, 39), (0, 8))):
        for k in range(2):
            lower = by0[2 * k, row : row + 1, :] * smo0[2 * k + 1, cell : cell + 1, :]
            upper = by0[2 * k + 1, row : row + 1, :] * smo0[2 * k + 2, cell : cell + 1, :]
            face_rows[2 * way + k : 2 * way + k + 1, :] = lower + upper
    blocks = halve_x(
        [res0[0] + res0[1], res0[2] + res0[3], bz0[4] * smo0[4, 8:40, :], bz0[0] * smo0[1, 8:40, :], face_rows[...]]
    )
    part0, part1, give_up, give_down = [
        jnp.concatenate([halve_y(2 * i, left), halve_y(2 * i + 1, right)], axis=1)
        for i, (left, right) in enumerate(blocks[:4])
    ]
    give_rows = jnp.concatenate(blocks[4], axis=1)
    parts = (part0, part1)
    z_out[0, 0] = give_up
    z_out[0, 1] = part1
    z_out[1, 0] = give_down
    z_out[1, 1] = part0
    swap_z = [send(z_out.at[way], z_in.at[way], faces[way]) for way in range(2)]
    for way, row in ((0, 15), (1, 0)):
        for k in range(2):
            y_out[way, k : k + 1, :] = parts[k][row : row + 1]
            y_out[way, 2 + k : 3 + k, :] = give_rows[2 * way + k : 2 * way + k + 1]
    swap_y = [send(y_out.at[way], y_in.at[way], faces[2 + way]) for way in range(2)]
    slot_of, swap_d = {}, []
    for i, (dz, dy, device) in enumerate(corners):
        slot_of[dz, dy] = i
        way = (1 - dy) // 2
        plane = (1 + dz) // 2
        give, row = (give_up if dz == 1 else give_down), (15 if dy == 1 else 0)
        d_out[i, 0:1, :] = give_rows[2 * way + plane : 2 * way + plane + 1]
        d_out[i, 1:2, :] = give[row : row + 1]
        swap_d.append(send(d_out.at[i], d_in.at[i], device))
    column_dens = gather_column(0, inbox_dens)
    dens2_near = [send(rho2.at[3, 16:24, :], rho2.at[3, rows2[dy][1], :], device) for dy, device in y_ways]
    dens2_near += [
        send(rho2.at[3, 16:24, :], rho2.at[3 - dz, rows2[dy][1], :], device) for dz, dy, device in around
    ]

    def coefficients(level, planes, z_faces):
        for k in planes:
            level.faces_x(k)
            level.faces_y(k)
        for k in range(planes[0], planes[-1] + 2):
            level.faces_z(k)
        for k in planes:
            level.diagonal(k)
            level.mask_y(k, ((8, y_low), (level.rows - 8, y_high)))
        level.mask_z(z_faces)

    wait_recv(dens1_copies)
    for way, (row, second) in enumerate(((15, 14), (32, 33))):
        for k in range(2):
            rho1[k + 2, row : row + 1, :] = dens_y_in[way, 2 * k : 2 * k + 1, :]
            rho1[k + 2, second : second + 1, :] = dens_y_in[way, 2 * k + 1 : 2 * k + 2, :]
    for i, (dz, dy, device) in enumerate(corners):
        plane, far_plane = (1, 0) if dz == 1 else (4, 5)
        row, second = (15, 14) if dy == 1 else (32, 33)
        for at, (p, r) in enumerate(((plane, row), (plane, second), (far_plane, row), (far_plane, second))):
            rho1[p, r : r + 1, :] = dens_d_in[i, at : at + 1, :]
    fill_y(rho1, range(6), 16, 16)
    fill_z(rho1, 2, 2, slice(8, 40), 1)
    coefficients(middle, range(4), ((1, z_low), (3, z_high)))
    wait_recv(dens2_near)
    fill_y(rho2, (3,), 8, 16)
    fill_z(rho2, 3, 1, slice(16, 24), 1)
    coarse.span = (8, 16)
    coefficients(coarse, (2,), ((2, z_low), (3, z_high)))
    coarse.span = (0, 24)

    wait_recv(swap_z + swap_y + swap_d)
    source1 = []
    for k in range(2):
        src1[k + 2, 16:32, :] = parts[k] + z_in[k, 0]
        src1[k + 2, 16:17, :] = src1[k + 2, 16:17, :] + y_in[0, 2 + k : 3 + k, :]
        src1[k + 2, 31:32, :] = src1[k + 2, 31:32, :] + y_in[1, 2 + k : 3 + k, :]
        source1.append(src1[k + 2, 16:32, :])
        val1[k + 2, 16:32, :] = 4.0 * source1[k] * idg1[k + 1, 8:24, :]
    for dz, plane, theirs, mine in ((1, 4, z_in[1, 1], give_up), (-1, 1, z_in[0, 1], give_down)):
        src1[plane, 16:32, :] = theirs + mine
        low, high = slot_of[-dz, 1], slot_of[-dz, -1]
        src1[plane, 16:17, :] = src1[plane, 16:17, :] + d_in[low, 0:1, :]
        src1[plane, 31:32, :] = src1[plane, 31:32, :] + d_in[high, 0:1, :]
        val1[plane, 16:32, :] = 4.0 * src1[plane, 16:32, :] * idg1[plane - 1, 8:24, :]
    for dy, row in ((1, 32), (-1, 15)):
        way = (1 - dy) // 2
        for k, dz in ((0, -1), (1, 1)):
            total = y_in[1 - way, k : k + 1, :] + give_rows[2 * way + k : 2 * way + k + 1]
            total = total + d_in[slot_of[-dz, -dy], 1:2, :]
            src1[k + 2, row : row + 1, :] = total
            val1[k + 2, row : row + 1, :] = 4.0 * total * idg1[k + 1, row - 8 : row - 7, :]

    def residual1(k):
        here, near = middle.neighbours(val1, k + 1, 8, 16)
        base1[k + 2, 16:32, :] = (1.0 - OMEGA) * here + (4.0 * source1[k] + near) * idg1[k + 1, 8:24, :]
        return (1.0 - OMEGA) * source1[k] + 0.25 * near

    source2 = restrict1(residual1)
    val2[3, 16:24, :] = 16.0 * source2 * idg2[2, 8:16, :]
    copies2 = [send(val2.at[3, 16:24, :], val2.at[3, rows2[dy][1], :], device) for dy, device in y_ways]
    for dz, device in z_ways:
        copies2.append(send(val2.at[3, 16:24, :], val2.at[3 - dz, 16:24, :], device))

    def pass_on(ref, reach):
        return [
            send(ref.at[4 - reach, 8:32, :], ref.at[3 - reach, 8:32, :], faces[0]),
            send(ref.at[2 + reach, 8:32, :], ref.at[3 + reach, 8:32, :], faces[1]),
        ]

    dens2_far = pass_on(rho2, 2)
    more1 = [
        send(base1.at[3, 16:32, :], base1.at[1, 16:32, :], faces[0]),
        send(base1.at[2, 16:32, :], base1.at[4, 16:32, :], faces[1]),
    ]
    for way, row in ((0, 31), (1, 16)):
        for k in range(2):
            wide_y_out[way, k : k + 1, :] = base1[k + 2, row : row + 1, :]
        more1.append(send(wide_y_out.at[way], wide_y_in.at[way], faces[2 + way]))
    for i, (dz, dy, device) in enumerate(corners):
        plane, row = (3 if dz == 1 else 2), (31 if dy == 1 else 16)
        wide_d_out[i] = base1[plane, row : row + 1, :]
        more1.append(send(wide_d_out.at[i], wide_d_in.at[i], device))
    wait_recv(column_dens)
    layer_dens = gather_layer(0, inbox_dens, wide_dens)
    wait_recv(copies2)
    here, near = coarse.neighbours(val2, 2, 8, 8)
    pack_message(1, (1.0 - OMEGA) * source2 + 0.0625 * near)
    base2[3, 16:24, :] = (1.0 - OMEGA) * here + (16.0 * source2 + near) * idg2[2, 8:16, :]
    column_src = gather_column(1, inbox_src)
    more2 = [send(base2.at[3, 16:24, :], base2.at[3, rows2[dy][1], :], device) for dy, device in y_ways]
    more2 += [send(base2.at[3, 16:24, :], base2.at[3 - dz, rows2[dy][1], :], device) for dz, dy, device in around]
    wait_recv(dens2_far)
    dens2_last = pass_on(rho2, 3)

    wait_recv(layer_dens)
    lane, sub = iota((8, 128), 1), iota((8, 128), 0)
    right_half = lane >= 64
    first_x, last_x = (lane % 64) == 0, (lane % 64) == 63
    first_y, last_y = (lane < 64) & (sub == 0), (lane >= 64) & (sub == 7)

    def lower_y(v):
        q = pltpu.roll(v, 64, 1)
        return jnp.where(right_half, q, pltpu.roll(q, 1, 0))

    def upper_y(v):
        q = pltpu.roll(v, 64, 1)
        return jnp.where(right_half, pltpu.roll(q, 7, 0), q)

    scale3 = 0.015625
    for zh in range(4):
        for s in range(16):
            rho3[1 + 16 * zh + s] = wide_dens[s, zh]
    rho3[0] = rho3[1]
    rho3[65] = rho3[64]

    def face3(k, _):
        bz3[k] = scale3 * twice_inverse(rho3[k] + rho3[k + 1])
        return 0

    lax.fori_loop(0, 65, face3, 0)

    def coef3(k, _):
        rho = rho3[k + 1]
        edge = twice_inverse(rho + rho)
        low = twice_inverse(rho + jnp.where(first_x, rho, pltpu.roll(rho, 1, 1)))
        total = low + jnp.where(last_x, edge, pltpu.roll(low, 127, 1))
        bx3[k] = jnp.where(first_x, 0.0, scale3 * low)
        low = twice_inverse(rho + jnp.where(first_y, rho, lower_y(rho)))
        total = total + low + jnp.where(last_y, edge, upper_y(low))
        by3[k] = jnp.where(first_y, 0.0, scale3 * low)
        dg3[k] = scale3 * total + bz3[k] + bz3[k + 1]
        return 0

    lax.fori_loop(0, 64, coef3, 0, unroll=4)

    zero_plane = jnp.zeros((8, 128), F32)
    lowest = (gz + 1) // 2 - 1
    cor3[...] = jnp.zeros((6, 8, 128), F32)
    for k in (0, 1, 2, 67, 68, 69):
        dir3[k] = zero_plane
        res3[k] = zero_plane
    mul3[64] = zero_plane
    img3[64] = zero_plane

    def clear3(k, _):
        dir3[k + 3] = zero_plane
        mul3[k] = zero_plane
        return 0

    lax.fori_loop(0, 64, clear3, 0, unroll=8)

    wait_recv(column_src)
    layer_src = gather_layer(1, inbox_src, wide_src)

    z_smooth = [
        send(smo0.at[4, 8:40, :], far_smooth.at[0], faces[0]), send(smo0.at[1, 8:40, :], far_smooth.at[1], faces[1])
    ]
    for k in range(4):
        rows_out[0, 2, k : k + 1, :] = smo0[k + 1, 39:40, :]
        rows_out[1, 2, k : k + 1, :] = smo0[k + 1, 8:9, :]
    y_smooth = [send(rows_out.at[way, 2], rows_in.at[way, 2], faces[2 + way]) for way in range(2)]
    wait_recv(more2)
    base2_far = pass_on(base2, 2)

    wait_recv(dens2_last)
    wait_send(dens2_near + dens2_far + dens2_last)

    def inside_z(face):
        at = gz + face - 2
        return jnp.where((at > 0) & (at < nz), 1.0, 0.0).astype(F32)

    fill_y(rho2, range(7), 8, 16)
    fill_z(rho2, 3, 1, slice(8, 32), 3)
    coefficients(coarse, range(5), [(face, inside_z(face)) for face in range(6)])

    wait_recv(layer_src)

    for zh in range(4):
        for k in range(16):
            res3[16 * zh + k + 3] = wide_src[k, zh]

    def whole(v):
        return jnp.sum(jnp.sum(v, axis=1, keepdims=True), axis=0, keepdims=True)

    def apply(k, prev, here, later):
        bx, by = bx3[k], by3[k]
        image = (dg3[k] * here - bz3[k] * prev) - (bz3[k + 1] * later + by * lower_y(here))
        image = image - ((bx * pltpu.roll(here, 1, 1) + upper_y(by * here)) + pltpu.roll(bx * here, 127, 1))
        img3[k] = image
        return image

    def advance(k, alpha, beta):
        dir3[k + 3] = res3[k + 3] + beta * dir3[k + 3]
        image = img3[k] + beta * mul3[k]
        mul3[k] = image
        resid = res3[k + 3] - alpha * image
        res3[k + 3] = resid
        return resid

    def totals(first, next_resid):
        def plane(k, carry):
            norm, power, prev, here = carry
            later = next_resid(k + 1)
            image = apply(k, prev, here, later)
            return norm + here * here, power + here * image, here, later

        norm, power, _, _ = lax.fori_loop(0, 64, plane, (zero_plane, zero_plane, zero_plane, first), unroll=64)
        return whole(norm), whole(power)

    norm, power = totals(res3[3], lambda k: res3[k + 3])

    def sweep(step, carry):
        alpha, beta, norm = carry
        norm_next, power = totals(advance(0, alpha, beta), lambda k: advance(k, alpha, beta))
        cor3[...] = cor3[...] + alpha * dir3[pl.ds(lowest + 1, 6)]
        beta = norm_next / norm
        return norm_next / (power - beta * norm_next / alpha), beta, norm_next

    alpha, beta, _ = lax.fori_loop(0, SWEEPS - 1, sweep, (norm / power, jnp.zeros((1, 1), F32), norm))

    window = pl.ds(lowest + 1, 6)
    cor3[...] = cor3[...] + alpha * (res3[window] + beta * dir3[window])

    spread_rows, spread_cols = iota((128, 256), 0), iota((128, 256), 1)
    fine_x = spread_cols % 128
    parent = fine_x // 2
    near = parent + 2 * (fine_x % 2) - 1
    half = spread_cols // 128
    inside = (near >= 0) & (near < 64)
    from_halves = (
        jnp.where(spread_rows == parent + 64 * half, 0.75, 0.0)
        + jnp.where((spread_rows == near + 64 * half) & inside, 0.25, 0.0)
    ).astype(jnp.bfloat16)
    mixed = []
    for d in range(-3, 4):
        plane = gz + d + 4
        index = plane // 2 - lowest
        other = index + 2 * (plane % 2) - 1
        mixed.append(0.75 * cor3[index] + 0.25 * cor3[other])
    x_done = dot(jnp.concatenate(mixed, axis=0), from_halves)
    wait_recv(more1 + base2_far + z_smooth + y_smooth)
    wait_send(more1 + more2 + base2_far + z_smooth)
    for way, row in ((0, 15), (1, 32)):
        for k in range(2):
            base1[k + 2, row : row + 1, :] = wide_y_in[way, k : k + 1, :]
    for i, (dz, dy, _) in enumerate(corners):
        plane, row = (1 if dz == 1 else 4), (15 if dy == 1 else 32)
        base1[plane, row : row + 1, :] = wide_d_in[i]
    first_row, last_row = iota((8, 128), 0) == 0, iota((8, 128), 0) == 7
    window = pl.ds(pl.multiple_of(8 * gy, 8), 24)
    for k in range(7):
        even, odd = x_done[8 * k : 8 * k + 8, 0:128], x_done[8 * k : 8 * k + 8, 128:256]
        fine_rows[k, 0:8, :] = zero_plane
        fine_rows[k, 40:48, :] = zero_plane
        below = jnp.where(first_row, 0.0, pltpu.roll(odd, 1, 0))
        above = jnp.where(last_row, 0.0, pltpu.roll(even, 7, 0))
        fine_rows[k, pl.ds(8, 8, stride=4), :] = 0.75 * even + 0.25 * below
        fine_rows[k, pl.ds(9, 8, stride=4), :] = 0.75 * even + 0.25 * odd
        fine_rows[k, pl.ds(10, 8, stride=4), :] = 0.75 * odd + 0.25 * even
        fine_rows[k, pl.ds(11, 8, stride=4), :] = 0.75 * odd + 0.25 * above
        up2[k, 8:32, :] = fine_rows[k, window, :]

    def in_grid(shape, margin, first_row, rows, plane, planes):
        row = iota(shape, 0)
        at = row + first_row
        good = (row >= margin) & (row < shape[0] - margin) & (at >= 0) & (at < rows)
        return good & (plane >= 0) & (plane < planes)

    ups = []
    for k in range(5):
        here, near = coarse.neighbours(up2, k, 0, 24)
        up = base2[k + 1, 8:32, :] + (1.0 - OMEGA) * here + near * idg2[k]
        ups.append(jnp.where(in_grid((24, 128), 1, 8 * gy - 8, 8 * ny, gz + k - 2, nz), up, 0.0))

    spread_x1, spread_x0 = spread_matrix(128), spread_matrix(256)

    def prolong(ups, target, first, rows, spread_x, add):
        height = ups[0].shape[0]
        tall = 2 * height - 16
        n = height - 8
        x_done = dot(jnp.concatenate(ups, axis=0), spread_x)
        tiles = x_done.shape[1] // 128
        for t in range(tiles):
            for k in range(len(ups)):
                pair_rows[t, 0:height, :] = x_done[height * k : height * (k + 1), 128 * t : 128 * (t + 1)]
                here = 0.75 * pair_rows[t, 4 : 4 + n, :]
                fine_rows[k, pl.ds(0, n, stride=2), :] = here + 0.25 * pair_rows[t, 3 : 3 + n, :]
                fine_rows[k, pl.ds(1, n, stride=2), :] = here + 0.25 * pair_rows[t, 5 : 5 + n, :]
            cols = slice(128 * t, 128 * (t + 1))
            for k in range(6):
                parent_z = (k + first) // 2
                near_z = parent_z + 2 * ((k + first) % 2) - 1
                value = 0.75 * fine_rows[parent_z, 0:tall, :] + 0.25 * fine_rows[near_z, 0:tall, :]
                target[k, rows, cols] = target[k, rows, cols] + value if add else value

    prolong(ups, up1, 2, slice(8, 40), spread_x1, False)
    ups = []
    for k in range(4):
        parts = []
        for r, m in middle.chunks():
            here, near = middle.neighbours(up1, k, r, m)
            base = base1[k + 1, 8 + r : 8 + r + m, :]
            parts.append(base + (1.0 - OMEGA) * here + near * idg1[k, r : r + m, :])
        up = jnp.concatenate(parts, axis=0)
        ups.append(jnp.where(in_grid((32, 256), 7, 16 * gy - 8, 16 * ny, 2 * gz + k - 1, 2 * nz), up, 0.0))
    for k, plane in ((0, 0), (1, 5)):
        smo0[plane, 8:40, :] = far_smooth[k]
    for k in range(4):
        smo0[k + 1, 7:8, :] = rows_in[0, 2, k : k + 1, :]
        smo0[k + 1, 40:41, :] = rows_in[1, 2, k : k + 1, :]
    prolong(ups, smo0, 1, slice(0, 48), spread_x0, True)
    for k in range(4):
        for r, m in fine.chunks():
            here, near = fine.neighbours(smo0, k, r, m)
            out[k, r : r + m, :] = (1.0 - OMEGA) * here + (src0[k, r : r + m, :] + near) * fine.idg[k, r : r + m, :]

    wait_send(
        z_dens + z_vals + y_both + dens1_copies + copies2 + column_dens + y_smooth + layer_dens
        + column_src + layer_src + swap_z + swap_y + swap_d
    )


def coefficient_scratch(planes, rows, cols):
    own = pltpu.VMEM((planes, rows, cols), F32)
    return [own, pltpu.VMEM((planes, rows + 8, cols), F32), pltpu.VMEM((planes + 1, rows, cols), F32), own, own]


COPIES = 6 + 8 + 8 + 8 + 2 + 2 + 4 + 4 + 8 + 8 + 2 + 62 + 30


def per_device(density, right_side, pressure_guess):
    coarsest, longer = pltpu.VMEM((64, 8, 128), F32), pltpu.VMEM((65, 8, 128), F32)
    padded = pltpu.VMEM((70, 8, 128), F32)
    return pl.pallas_call(
        kernel,
        out_shape=jax.ShapeDtypeStruct(density.shape, F32),
        in_specs=[pl.BlockSpec(memory_space=pltpu.HBM)] * 3,
        out_specs=pl.BlockSpec(memory_space=pltpu.VMEM),
        scratch_shapes=[
            *[pltpu.VMEM((6, 48, 512), F32)] * 3,
            *[pltpu.VMEM((4, 32, 512), F32)] * 2,
            *coefficient_scratch(4, 32, 512),
            pltpu.VMEM((6, 48, 256), F32),
            *[pltpu.VMEM((6, 48, 256), F32)] * 4,
            *coefficient_scratch(4, 32, 256),
            pltpu.VMEM((7, 40, 128), F32),
            *[pltpu.VMEM((7, 40, 128), F32)] * 3,
            *coefficient_scratch(5, 24, 128),
            pltpu.VMEM((2, 3, 4, 512), F32),
            pltpu.VMEM((2, 3, 4, 512), F32),
            pltpu.VMEM((2, 2, 128), F32),
            pltpu.VMEM((4, 2, 4, 2, 128), F32),
            pltpu.VMEM((4, 2, 4, 2, 128), F32),
            pltpu.VMEM((2, 4, 8, 128), F32),
            pltpu.VMEM((16, 4, 8, 128), F32),
            pltpu.VMEM((16, 4, 8, 128), F32),
            pltpu.VMEM((66, 8, 128), F32),
            coarsest, coarsest, longer, coarsest,
            padded, padded, longer, longer, pltpu.VMEM((6, 8, 128), F32),
            pltpu.VMEM((8, 256), F32),
            pltpu.VMEM((8, 32, 128), F32),
            pltpu.VMEM((7, 48, 128), F32),
            pltpu.VMEM((2, 32, 512), F32),
            pltpu.VMEM((8, 512), F32),
            *[pltpu.VMEM((2, 2, 16, 256), F32)] * 2,
            *[pltpu.VMEM((2, 4, 256), F32)] * 2,
            *[pltpu.VMEM((4, 2, 256), F32)] * 2,
            *[pltpu.VMEM((2, 2, 256), F32)] * 2,
            *[pltpu.VMEM((4, 1, 256), F32)] * 2,
            *[pltpu.VMEM((2, 4, 256), F32)] * 2,
            *[pltpu.VMEM((4, 4, 256), F32)] * 2,
            pltpu.SemaphoreType.DMA((3,)),
            pltpu.SemaphoreType.DMA((COPIES,)),
            pltpu.SemaphoreType.DMA((COPIES,)),
        ],
        compiler_params=pltpu.CompilerParams(
            collective_id=0, has_side_effects=True, vmem_limit_bytes=32 * 1024 * 1024
        ),
        cost_estimate=pl.CostEstimate(flops=20_000_000, bytes_accessed=1 << 20, transcendentals=0),
    )(*[pltpu.with_memory_space_constraint(a, pltpu.HBM) for a in (density, right_side, pressure_guess)])


def solution(mesh):
    spec = P("gz", "gy", None)
    return jax.shard_map(per_device, mesh=mesh, in_specs=(spec, spec, spec), out_specs=spec, check_vma=False)
```

```python
import functools

import jax
import jax.numpy as jnp
from jax import lax
from jax.experimental import pallas as pl
from jax.experimental.pallas import tpu as pltpu
from jax.sharding import PartitionSpec as P

MESH = pl.DeviceIdType.MESH
SWEEPS = 8
OMEGA = 0.8
F32 = jnp.float32
PAD = 8


def dot(values, weights):
    rows = values.shape[0]
    if rows % 16:
        values = jnp.concatenate([values, jnp.zeros((16 - rows % 16, values.shape[1]), F32)], axis=0)
    total = values.shape[0]
    first = values.astype(jnp.bfloat16).astype(F32)
    rest = values - first
    second = rest.astype(jnp.bfloat16).astype(F32)
    parts = jnp.concatenate([first, second, rest - second], axis=0).astype(jnp.bfloat16)
    out = jnp.dot(parts, weights, preferred_element_type=F32)
    return (out[0:total] + out[total : 2 * total] + out[2 * total :])[0:rows]


def twice_inverse(total):
    guess = pltpu.reciprocal(total, approx=True)
    return guess * (4.0 - 2.0 * total * guess)


def iota(shape, axis):
    return lax.broadcasted_iota(jnp.int32, shape, axis)


def pair_matrix():
    rows, cols = iota((256, 128), 0), iota((256, 128), 1)
    return jnp.where(rows // 2 == cols, 0.125, 0.0).astype(jnp.bfloat16)


def spread_matrix(coarse):
    rows, cols = iota((coarse, 2 * coarse), 0), iota((coarse, 2 * coarse), 1)
    parent = cols // 2
    near = parent + 2 * (cols % 2) - 1
    return (jnp.where(rows == parent, 0.75, 0.0) + jnp.where(rows == near, 0.25, 0.0)).astype(jnp.bfloat16)


class Level:
    def __init__(self, shape, chunk, rho, bx, by, bz, dg, idg):
        self.planes, self.rows, self.cols = shape
        self.chunk = chunk
        self.rho, self.bx, self.by, self.bz, self.dg, self.idg = rho, bx, by, bz, dg, idg

        self.span = (0, self.rows)

    def chunks(self):
        return [(r, self.chunk) for r in range(*self.span, self.chunk)]

    def faces_x(self, plane):
        n = self.cols
        for r, m in self.chunks():
            rho = self.rho[plane + 1, PAD + r : PAD + r + m, :]
            lane = iota((m, n), 1)
            low = twice_inverse(rho + jnp.where(lane == 0, rho, pltpu.roll(rho, 1, 1)))
            high = jnp.where(lane == n - 1, twice_inverse(rho + rho), pltpu.roll(low, n - 1, 1))
            self.dg[plane, r : r + m, :] = low + high
            self.bx[plane, r : r + m, :] = jnp.where(lane == 0, 0.0, low)

    def faces_y(self, plane):
        for r, m in self.chunks():
            low = self.rho[plane + 1, PAD - 1 + r : PAD - 1 + r + m, :]
            high = self.rho[plane + 1, PAD + r : PAD + r + m, :]
            self.by[plane, r : r + m, :] = twice_inverse(low + high)
        last = self.span[1]
        low = self.rho[plane + 1, PAD - 1 + last : PAD + last, :]
        high = self.rho[plane + 1, PAD + last : PAD + last + 1, :]
        self.by[plane, last : last + 1, :] = twice_inverse(low + high)

    def faces_z(self, face):
        for r, m in self.chunks():
            low = self.rho[face, PAD + r : PAD + r + m, :]
            high = self.rho[face + 1, PAD + r : PAD + r + m, :]
            self.bz[face, r : r + m, :] = twice_inverse(low + high)

    def diagonal(self, plane):
        for r, m in self.chunks():
            total = self.dg[plane, r : r + m, :]
            total = total + self.by[plane, r : r + m, :] + self.by[plane, r + 1 : r + 1 + m, :]
            total = total + self.bz[plane, r : r + m, :] + self.bz[plane + 1, r : r + m, :]
            self.dg[plane, r : r + m, :] = total
            self.idg[plane, r : r + m, :] = (0.5 * OMEGA) * twice_inverse(total)

    def mask_y(self, plane, faces):
        for row, factor in faces:
            self.by[plane, row : row + 1, :] = self.by[plane, row : row + 1, :] * factor

    def mask_z(self, faces):
        for face, factor in faces:
            self.bz[face] = self.bz[face] * factor

    def neighbours(self, val, plane, r, m):
        n = self.cols
        rows = slice(PAD + r, PAD + r + m)
        here = val[plane + 1, rows, :]
        bx = self.bx[plane, r : r + m, :]
        total = self.bz[plane, r : r + m, :] * val[plane, rows, :]
        total = total + self.bz[plane + 1, r : r + m, :] * val[plane + 2, rows, :]
        total = total + self.by[plane, r : r + m, :] * val[plane + 1, PAD - 1 + r : PAD - 1 + r + m, :]
        total = total + self.by[plane, r + 1 : r + 1 + m, :] * val[plane + 1, PAD + 1 + r : PAD + 1 + r + m, :]
        total = total + bx * pltpu.roll(here, 1, 1)
        total = total + pltpu.roll(bx * here, n - 1, 1)
        return here, total


def kernel(
    dens_in, right_in, guess_in, out,
    rho0, val0, smo0, src0, res0, bx0, by0, bz0, dg0, idg0,
    rho1, val1, src1, base1, up1, bx1, by1, bz1, dg1, idg1,
    rho2, val2, base2, up2, bx2, by2, bz2, dg2, idg2,
    rows_out, rows_in, message, inbox_dens, inbox_src, tile, wide_dens, wide_src,
    rho3, bx3, by3, bz3, dg3, dir3, res3, img3, mul3, cor3, pair_tmp, pair_rows, fine_rows,
    far_smooth, face_rows, z_out, z_in, y_out, y_in, d_out, d_in, wide_y_out, wide_y_in, wide_d_out, wide_d_in,
    dens_y_out, dens_y_in, dens_d_out, dens_d_in, local_sem, send_sem, recv_sem,
):
    gz, gy = lax.axis_index("gz"), lax.axis_index("gy")
    nz, ny = 128, 4
    core, ypos, xpos, zhi = gz % 2, (gz // 2) % 4, (gz // 8) % 4, gz // 32
    zpos = zhi * 4 + gy

    def gz_of(zh, x, y, c):
        return ((zh * 4 + x) * 4 + y) * 2 + c

    up_z, down_z = (gz + 1) % nz, (gz + nz - 1) % nz
    up_y, down_y = (gy + 1) % ny, (gy + ny - 1) % ny
    column = []
    for d in (8, 7, 9, 6, 10, 5, 11, 4, 12, 3, 13, 2, 14, 1, 15, 0):
        for k in range(2):
            if d or k:
                z = (zpos + d) % 16
                column.append((gz_of(z // 4, xpos, ypos, (core + k) % 2), z % 4))
    layer = []
    for i in (2, 1, 3, 0):
        for j in (2, 1, 3, 0):
            if i or j:
                layer.append((gz_of(zhi, (xpos + i) % 4, (ypos + j) % 4, core), gy))
    faces = [(up_z, gy), (down_z, gy), (gz, up_y), (gz, down_y)]
    around = []
    for dz in (1, -1):
        for dy in (0, 1, -1):
            around.append((dz, dy, ((gz + dz + nz) % nz, (gy + dy + ny) % ny)))
    corners = [(dz, dy, device) for dz, dy, device in around if dy]
    greeted = column + [device for _, _, device in around] + faces[2:] + layer

    barrier = pltpu.get_barrier_semaphore()
    for device in greeted:
        pl.semaphore_signal(barrier, inc=1, device_id=device, device_id_type=MESH)

    local = []
    for i, (source, target) in enumerate(
        ((dens_in, rho0.at[1:5, 8:40, :]), (guess_in, val0.at[1:5, 8:40, :]), (right_in, src0))
    ):
        copy = pltpu.make_async_copy(source, target, local_sem.at[i])
        copy.start()
        local.append(copy)

    count = [0]

    def send(source, target, device):
        i = count[0]
        count[0] = i + 1
        copy = pltpu.make_async_remote_copy(
            src_ref=source, dst_ref=target, send_sem=send_sem.at[i], recv_sem=recv_sem.at[i],
            device_id=device, device_id_type=MESH,
        )
        copy.start()
        return copy

    def wait_recv(copies):
        for copy in copies:
            copy.wait_recv()

    def wait_send(copies):
        for copy in copies:
            copy.wait_send()

    fine = Level((4, 32, 512), 8, rho0, bx0, by0, bz0, dg0, idg0)
    middle = Level((4, 32, 256), 16, rho1, bx1, by1, bz1, dg1, idg1)
    coarse = Level((5, 24, 128), 8, rho2, bx2, by2, bz2, dg2, idg2)

    z_low = jnp.where(gz > 0, 1.0, 0.0).astype(F32)
    z_high = jnp.where(gz < nz - 1, 1.0, 0.0).astype(F32)
    y_low = jnp.where(gy > 0, 1.0, 0.0).astype(F32)
    y_high = jnp.where(gy < ny - 1, 1.0, 0.0).astype(F32)

    pair_x = pair_matrix()

    def halve_x(blocks):
        rows = sum(block.shape[0] for block in blocks)
        summed = dot(jnp.concatenate([b[:, 0:256] for b in blocks] + [b[:, 256:512] for b in blocks], axis=0), pair_x)
        out, at = [], 0
        for block in blocks:
            n = block.shape[0]
            out.append((summed[at : at + n], summed[rows + at : rows + at + n]))
            at += n
        return out

    def halve_y(slot, value):
        n = value.shape[0]
        pair_rows[slot, 0:n, :] = value
        return pair_rows[slot, pl.ds(0, n // 2, stride=2), :] + pair_rows[slot, pl.ds(1, n // 2, stride=2), :]

    def halve_xy(blocks):
        return [
            jnp.concatenate([halve_y(2 * i, left), halve_y(2 * i + 1, right)], axis=1)
            for i, (left, right) in enumerate(halve_x(blocks))
        ]

    def restrict1(read):
        return halve_y(0, dot(read(0) + read(1), pair_x))

    half_rows, half_cols = iota((128, 256), 0), iota((128, 256), 1)
    to_halves = jnp.where((half_cols % 64 == half_rows // 2) & ((half_cols < 64) | (half_cols >= 192)), 0.125, 0.0).astype(jnp.bfloat16)

    def pack_message(field, value):
        pair_tmp[...] = dot(value, to_halves)
        for r in range(2):
            t = 4 * r
            message[field, r : r + 1, :] = (
                pair_tmp[t : t + 1, 0:128] + pair_tmp[t + 1 : t + 2, 0:128]
                + pair_tmp[t + 2 : t + 3, 128:256] + pair_tmp[t + 3 : t + 4, 128:256]
            )

    def gather_column(field, inbox):
        inbox[zhi, core, gy] = message[field]
        return [send(message.at[field], inbox.at[zhi, core, gy], device) for device in column]

    def gather_layer(field, inbox, wide):
        for zh in range(4):
            for y in range(4):
                tile[field, zh, 2 * y : 2 * y + 2, :] = inbox[zh, 0, y] + inbox[zh, 1, y]
        slot = xpos * 4 + ypos
        wide[slot] = tile[field]
        return [send(tile.at[field], wide.at[slot], device) for device in layer]

    local[0].wait()
    own1 = halve_xy([rho0[2 * k + 1, 8:40, :] + rho0[2 * k + 2, 8:40, :] for k in range(2)])
    for k in range(2):
        rho1[k + 2, 16:32, :] = own1[k]
    own2 = restrict1(lambda k: own1[k])
    rho2[3, 16:24, :] = own2
    pack_message(0, own2)
    local[1].wait()
    for k in range(4):
        for f, ref in ((0, rho0), (1, val0)):
            rows_out[0, f, k : k + 1, :] = ref[k + 1, 39:40, :]
            rows_out[1, f, k : k + 1, :] = ref[k + 1, 8:9, :]

    for way, (row, second) in enumerate(((31, 30), (16, 17))):
        for k in range(2):
            dens_y_out[way, 2 * k : 2 * k + 1, :] = rho1[k + 2, row : row + 1, :]
            dens_y_out[way, 2 * k + 1 : 2 * k + 2, :] = rho1[k + 2, second : second + 1, :]
    for i, (dz, dy, device) in enumerate(corners):
        plane, far_plane = (3, 2) if dz == 1 else (2, 3)
        row, second = (31, 30) if dy == 1 else (16, 17)
        for at, (p, r) in enumerate(((plane, row), (plane, second), (far_plane, row), (far_plane, second))):
            dens_d_out[i, at : at + 1, :] = rho1[p, r : r + 1, :]
    for k in (0, 5):
        smo0[k, 8:40, :] = jnp.zeros((32, 512), F32)
    for k in range(1, 5):
        smo0[k, 7:8, :] = jnp.zeros((1, 512), F32)
        smo0[k, 40:41, :] = jnp.zeros((1, 512), F32)

    pl.semaphore_wait(barrier, len(greeted))

    z_dens = [
        send(rho0.at[4, 8:40, :], rho0.at[0, 8:40, :], faces[0]),
        send(rho0.at[1, 8:40, :], rho0.at[5, 8:40, :], faces[1]),
    ]
    z_vals = [
        send(val0.at[4, 8:40, :], val0.at[0, 8:40, :], faces[0]),
        send(val0.at[1, 8:40, :], val0.at[5, 8:40, :], faces[1]),
    ]
    y_both = [
        send(rows_out.at[0, 0:2], rows_in.at[0, 0:2], faces[2]),
        send(rows_out.at[1, 0:2], rows_in.at[1, 0:2], faces[3]),
    ]

    rows2 = {dy: (slice(16, 24), slice(16 - 8 * dy, 24 - 8 * dy)) for dy in (0, 1, -1)}
    y_ways = ((1, faces[2]), (-1, faces[3]))
    z_ways = ((1, faces[0]), (-1, faces[1]))

    def fill_y(ref, planes, rows, first):
        last = first + rows - 1
        for k in planes:
            ref[k, first - 1 : first, :] = jnp.where(gy == 0, ref[k, first : first + 1, :], ref[k, first - 1 : first, :])
            ref[k, last + 1 : last + 2, :] = jnp.where(
                gy == ny - 1, ref[k, last : last + 1, :], ref[k, last + 1 : last + 2, :]
            )

    def fill_z(ref, own, planes, rows, reach):
        for i in range(reach):
            low, high = own - 1 - i * planes, own + planes + i * planes
            ref[low, rows, :] = jnp.where(gz == i, ref[low + 1, rows, :], ref[low, rows, :])
            ref[high, rows, :] = jnp.where(gz == nz - 1 - i, ref[high - 1, rows, :], ref[high, rows, :])

    for k in range(4):
        fine.faces_x(k)
    for face in (1, 2, 3):
        fine.faces_z(face)
    wait_recv(y_both)
    dens1_copies = [
        send(rho1.at[2:4, 16:32, :], rho1.at[0:2, 16:32, :], faces[0]),
        send(rho1.at[2:4, 16:32, :], rho1.at[4:6, 16:32, :], faces[1]),
        send(dens_y_out.at[0], dens_y_in.at[0], faces[2]),
        send(dens_y_out.at[1], dens_y_in.at[1], faces[3]),
    ]
    for i, (dz, dy, device) in enumerate(corners):
        dens1_copies.append(send(dens_d_out.at[i], dens_d_in.at[i], device))
    for k in range(4):
        for f, ref in ((0, rho0), (1, val0)):
            ref[k + 1, 7:8, :] = rows_in[0, f, k : k + 1, :]
            ref[k + 1, 40:41, :] = rows_in[1, f, k : k + 1, :]
    fill_y(rho0, range(1, 5), 32, 8)
    for k in range(4):
        fine.faces_y(k)
    local[2].wait()

    def smooth(plane):
        for r, m in fine.chunks():
            here, near = fine.neighbours(val0, plane, r, m)
            smo0[plane + 1, 8 + r : 8 + r + m, :] = (1.0 - OMEGA) * here + (
                src0[plane, r : r + m, :] + near
            ) * fine.idg[plane, r : r + m, :]

    for k in (1, 2):
        fine.diagonal(k)
        fine.mask_y(k, ((0, y_low), (32, y_high)))
        smooth(k)
    wait_recv(z_dens)
    fill_z(rho0, 1, 4, slice(8, 40), 1)
    for face in (0, 4):
        fine.faces_z(face)
    for k in (0, 3):
        fine.diagonal(k)
        fine.mask_y(k, ((0, y_low), (32, y_high)))
    fine.mask_z(((0, z_low), (4, z_high)))
    wait_recv(z_vals)
    smooth(3)
    smooth(0)

    for plane in range(4):
        for r, m in fine.chunks():
            here, near = fine.neighbours(smo0, plane, r, m)
            res0[plane, r : r + m, :] = src0[plane, r : r + m, :] - dg0[plane, r : r + m, :] * here + near
    for way, (row, cell) in enumerate(((32, 39), (0, 8))):
        for k in range(2):
            lower = by0[2 * k, row : row + 1, :] * smo0[2 * k + 1, cell : cell + 1, :]
            upper = by0[2 * k + 1, row : row + 1, :] * smo0[2 * k + 2, cell : cell + 1, :]
            face_rows[2 * way + k : 2 * way + k + 1, :] = lower + upper
    blocks = halve_x(
        [res0[0] + res0[1], res0[2] + res0[3], bz0[4] * smo0[4, 8:40, :], bz0[0] * smo0[1, 8:40, :], face_rows[...]]
    )
    part0, part1, give_up, give_down = [
        jnp.concatenate([halve_y(2 * i, left), halve_y(2 * i + 1, right)], axis=1)
        for i, (left, right) in enumerate(blocks[:4])
    ]
    give_rows = jnp.concatenate(blocks[4], axis=1)
    parts = (part0, part1)
    z_out[0, 0] = give_up
    z_out[0, 1] = part1
    z_out[1, 0] = give_down
    z_out[1, 1] = part0
    swap_z = [send(z_out.at[way], z_in.at[way], faces[way]) for way in range(2)]
    for way, row in ((0, 15), (1, 0)):
        for k in range(2):
            y_out[way, k : k + 1, :] = parts[k][row : row + 1]
            y_out[way, 2 + k : 3 + k, :] = give_rows[2 * way + k : 2 * way + k + 1]
    swap_y = [send(y_out.at[way], y_in.at[way], faces[2 + way]) for way in range(2)]
    slot_of, swap_d = {}, []
    for i, (dz, dy, device) in enumerate(corners):
        slot_of[dz, dy] = i
        way = (1 - dy) // 2
        plane = (1 + dz) // 2
        give, row = (give_up if dz == 1 else give_down), (15 if dy == 1 else 0)
        d_out[i, 0:1, :] = give_rows[2 * way + plane : 2 * way + plane + 1]
        d_out[i, 1:2, :] = give[row : row + 1]
        swap_d.append(send(d_out.at[i], d_in.at[i], device))
    column_dens = gather_column(0, inbox_dens)
    dens2_near = [send(rho2.at[3, 16:24, :], rho2.at[3, rows2[dy][1], :], device) for dy, device in y_ways]
    dens2_near += [
        send(rho2.at[3, 16:24, :], rho2.at[3 - dz, rows2[dy][1], :], device) for dz, dy, device in around
    ]

    def coefficients(level, planes, z_faces):
        for k in planes:
            level.faces_x(k)
            level.faces_y(k)
        for k in range(planes[0], planes[-1] + 2):
            level.faces_z(k)
        for k in planes:
            level.diagonal(k)
            level.mask_y(k, ((8, y_low), (level.rows - 8, y_high)))
        level.mask_z(z_faces)

    wait_recv(dens1_copies)
    for way, (row, second) in enumerate(((15, 14), (32, 33))):
        for k in range(2):
            rho1[k + 2, row : row + 1, :] = dens_y_in[way, 2 * k : 2 * k + 1, :]
            rho1[k + 2, second : second + 1, :] = dens_y_in[way, 2 * k + 1 : 2 * k + 2, :]
    for i, (dz, dy, device) in enumerate(corners):
        plane, far_plane = (1, 0) if dz == 1 else (4, 5)
        row, second = (15, 14) if dy == 1 else (32, 33)
        for at, (p, r) in enumerate(((plane, row), (plane, second), (far_plane, row), (far_plane, second))):
            rho1[p, r : r + 1, :] = dens_d_in[i, at : at + 1, :]
    fill_y(rho1, range(6), 16, 16)
    fill_z(rho1, 2, 2, slice(8, 40), 1)
    coefficients(middle, range(4), ((1, z_low), (3, z_high)))
    wait_recv(dens2_near)
    fill_y(rho2, (3,), 8, 16)
    fill_z(rho2, 3, 1, slice(16, 24), 1)
    coarse.span = (8, 16)
    coefficients(coarse, (2,), ((2, z_low), (3, z_high)))
    coarse.span = (0, 24)

    wait_recv(swap_z + swap_y + swap_d)
    source1 = []
    for k in range(2):
        src1[k + 2, 16:32, :] = parts[k] + z_in[k, 0]
        src1[k + 2, 16:17, :] = src1[k + 2, 16:17, :] + y_in[0, 2 + k : 3 + k, :]
        src1[k + 2, 31:32, :] = src1[k + 2, 31:32, :] + y_in[1, 2 + k : 3 + k, :]
        source1.append(src1[k + 2, 16:32, :])
        val1[k + 2, 16:32, :] = 4.0 * source1[k] * idg1[k + 1, 8:24, :]
    for dz, plane, theirs, mine in ((1, 4, z_in[1, 1], give_up), (-1, 1, z_in[0, 1], give_down)):
        src1[plane, 16:32, :] = theirs + mine
        low, high = slot_of[-dz, 1], slot_of[-dz, -1]
        src1[plane, 16:17, :] = src1[plane, 16:17, :] + d_in[low, 0:1, :]
        src1[plane, 31:32, :] = src1[plane, 31:32, :] + d_in[high, 0:1, :]
        val1[plane, 16:32, :] = 4.0 * src1[plane, 16:32, :] * idg1[plane - 1, 8:24, :]
    for dy, row in ((1, 32), (-1, 15)):
        way = (1 - dy) // 2
        for k, dz in ((0, -1), (1, 1)):
            total = y_in[1 - way, k : k + 1, :] + give_rows[2 * way + k : 2 * way + k + 1]
            total = total + d_in[slot_of[-dz, -dy], 1:2, :]
            src1[k + 2, row : row + 1, :] = total
            val1[k + 2, row : row + 1, :] = 4.0 * total * idg1[k + 1, row - 8 : row - 7, :]

    def residual1(k):
        here, near = middle.neighbours(val1, k + 1, 8, 16)
        base1[k + 2, 16:32, :] = (1.0 - OMEGA) * here + (4.0 * source1[k] + near) * idg1[k + 1, 8:24, :]
        return (1.0 - OMEGA) * source1[k] + 0.25 * near

    source2 = restrict1(residual1)
    val2[3, 16:24, :] = 16.0 * source2 * idg2[2, 8:16, :]
    copies2 = [send(val2.at[3, 16:24, :], val2.at[3, rows2[dy][1], :], device) for dy, device in y_ways]
    for dz, device in z_ways:
        copies2.append(send(val2.at[3, 16:24, :], val2.at[3 - dz, 16:24, :], device))

    def pass_on(ref, reach):
        return [
            send(ref.at[4 - reach, 8:32, :], ref.at[3 - reach, 8:32, :], faces[0]),
            send(ref.at[2 + reach, 8:32, :], ref.at[3 + reach, 8:32, :], faces[1]),
        ]

    dens2_far = pass_on(rho2, 2)
    more1 = [
        send(base1.at[3, 16:32, :], base1.at[1, 16:32, :], faces[0]),
        send(base1.at[2, 16:32, :], base1.at[4, 16:32, :], faces[1]),
    ]
    for way, row in ((0, 31), (1, 16)):
        for k in range(2):
            wide_y_out[way, k : k + 1, :] = base1[k + 2, row : row + 1, :]
        more1.append(send(wide_y_out.at[way], wide_y_in.at[way], faces[2 + way]))
    for i, (dz, dy, device) in enumerate(corners):
        plane, row = (3 if dz == 1 else 2), (31 if dy == 1 else 16)
        wide_d_out[i] = base1[plane, row : row + 1, :]
        more1.append(send(wide_d_out.at[i], wide_d_in.at[i], device))
    wait_recv(column_dens)
    layer_dens = gather_layer(0, inbox_dens, wide_dens)
    wait_recv(copies2)
    here, near = coarse.neighbours(val2, 2, 8, 8)
    pack_message(1, (1.0 - OMEGA) * source2 + 0.0625 * near)
    base2[3, 16:24, :] = (1.0 - OMEGA) * here + (16.0 * source2 + near) * idg2[2, 8:16, :]
    column_src = gather_column(1, inbox_src)
    more2 = [send(base2.at[3, 16:24, :], base2.at[3, rows2[dy][1], :], device) for dy, device in y_ways]
    more2 += [send(base2.at[3, 16:24, :], base2.at[3 - dz, rows2[dy][1], :], device) for dz, dy, device in around]
    wait_recv(dens2_far)
    dens2_last = pass_on(rho2, 3)

    wait_recv(layer_dens)
    lane, sub = iota((8, 128), 1), iota((8, 128), 0)
    right_half = lane >= 64
    first_x, last_x = (lane % 64) == 0, (lane % 64) == 63
    first_y, last_y = (lane < 64) & (sub == 0), (lane >= 64) & (sub == 7)

    def lower_y(v):
        q = pltpu.roll(v, 64, 1)
        return jnp.where(right_half, q, pltpu.roll(q, 1, 0))

    def upper_y(v):
        q = pltpu.roll(v, 64, 1)
        return jnp.where(right_half, pltpu.roll(q, 7, 0), q)

    scale3 = 0.015625
    for zh in range(4):
        for s in range(16):
            rho3[1 + 16 * zh + s] = wide_dens[s, zh]
    rho3[0] = rho3[1]
    rho3[65] = rho3[64]

    def face3(k, _):
        bz3[k] = scale3 * twice_inverse(rho3[k] + rho3[k + 1])
        return 0

    lax.fori_loop(0, 65, face3, 0)

    def coef3(k, _):
        rho = rho3[k + 1]
        edge = twice_inverse(rho + rho)
        low = twice_inverse(rho + jnp.where(first_x, rho, pltpu.roll(rho, 1, 1)))
        total = low + jnp.where(last_x, edge, pltpu.roll(low, 127, 1))
        bx3[k] = jnp.where(first_x, 0.0, scale3 * low)
        low = twice_inverse(rho + jnp.where(first_y, rho, lower_y(rho)))
        total = total + low + jnp.where(last_y, edge, upper_y(low))
        by3[k] = jnp.where(first_y, 0.0, scale3 * low)
        dg3[k] = scale3 * total + bz3[k] + bz3[k + 1]
        return 0

    lax.fori_loop(0, 64, coef3, 0, unroll=4)

    zero_plane = jnp.zeros((8, 128), F32)
    lowest = (gz + 1) // 2 - 1
    cor3[...] = jnp.zeros((6, 8, 128), F32)
    for k in (0, 1, 2, 67, 68, 69):
        dir3[k] = zero_plane
        res3[k] = zero_plane
    mul3[64] = zero_plane
    img3[64] = zero_plane

    def clear3(k, _):
        dir3[k + 3] = zero_plane
        mul3[k] = zero_plane
        return 0

    lax.fori_loop(0, 64, clear3, 0, unroll=8)

    wait_recv(column_src)
    layer_src = gather_layer(1, inbox_src, wide_src)

    z_smooth = [
        send(smo0.at[4, 8:40, :], far_smooth.at[0], faces[0]), send(smo0.at[1, 8:40, :], far_smooth.at[1], faces[1])
    ]
    for k in range(4):
        rows_out[0, 2, k : k + 1, :] = smo0[k + 1, 39:40, :]
        rows_out[1, 2, k : k + 1, :] = smo0[k + 1, 8:9, :]
    y_smooth = [send(rows_out.at[way, 2], rows_in.at[way, 2], faces[2 + way]) for way in range(2)]
    wait_recv(more2)
    base2_far = pass_on(base2, 2)

    wait_recv(dens2_last)
    wait_send(dens2_near + dens2_far + dens2_last)

    def inside_z(face):
        at = gz + face - 2
        return jnp.where((at > 0) & (at < nz), 1.0, 0.0).astype(F32)

    fill_y(rho2, range(7), 8, 16)
    fill_z(rho2, 3, 1, slice(8, 32), 3)
    coefficients(coarse, range(5), [(face, inside_z(face)) for face in range(6)])

    wait_recv(layer_src)

    for zh in range(4):
        for k in range(16):
            res3[16 * zh + k + 3] = wide_src[k, zh]

    def whole(v):
        return jnp.sum(jnp.sum(v, axis=1, keepdims=True), axis=0, keepdims=True)

    def apply(k, prev, here, later):
        bx, by = bx3[k], by3[k]
        image = (dg3[k] * here - bz3[k] * prev) - (bz3[k + 1] * later + by * lower_y(here))
        image = image - ((bx * pltpu.roll(here, 1, 1) + upper_y(by * here)) + pltpu.roll(bx * here, 127, 1))
        img3[k] = image
        return image

    def advance(k, alpha, beta):
        dir3[k + 3] = res3[k + 3] + beta * dir3[k + 3]
        image = img3[k] + beta * mul3[k]
        mul3[k] = image
        resid = res3[k + 3] - alpha * image
        res3[k + 3] = resid
        return resid

    def totals(first, next_resid):
        def plane(k, carry):
            norm, power, prev, here = carry
            later = next_resid(k + 1)
            image = apply(k, prev, here, later)
            return norm + here * here, power + here * image, here, later

        norm, power, _, _ = lax.fori_loop(0, 64, plane, (zero_plane, zero_plane, zero_plane, first), unroll=64)
        return whole(norm), whole(power)

    norm, power = totals(res3[3], lambda k: res3[k + 3])

    def sweep(step, carry):
        alpha, beta, norm = carry
        norm_next, power = totals(advance(0, alpha, beta), lambda k: advance(k, alpha, beta))
        cor3[...] = cor3[...] + alpha * dir3[pl.ds(lowest + 1, 6)]
        beta = norm_next / norm
        return norm_next / (power - beta * norm_next / alpha), beta, norm_next

    alpha, beta, _ = lax.fori_loop(0, SWEEPS - 1, sweep, (norm / power, jnp.zeros((1, 1), F32), norm))

    window = pl.ds(lowest + 1, 6)
    cor3[...] = cor3[...] + alpha * (res3[window] + beta * dir3[window])

    spread_rows, spread_cols = iota((128, 256), 0), iota((128, 256), 1)
    fine_x = spread_cols % 128
    parent = fine_x // 2
    near = parent + 2 * (fine_x % 2) - 1
    half = spread_cols // 128
    inside = (near >= 0) & (near < 64)
    from_halves = (
        jnp.where(spread_rows == parent + 64 * half, 0.75, 0.0)
        + jnp.where((spread_rows == near + 64 * half) & inside, 0.25, 0.0)
    ).astype(jnp.bfloat16)
    mixed = []
    for d in range(-3, 4):
        plane = gz + d + 4
        index = plane // 2 - lowest
        other = index + 2 * (plane % 2) - 1
        mixed.append(0.75 * cor3[index] + 0.25 * cor3[other])
    x_done = dot(jnp.concatenate(mixed, axis=0), from_halves)
    wait_recv(more1 + base2_far + z_smooth + y_smooth)
    wait_send(more1 + more2 + base2_far + z_smooth)
    for way, row in ((0, 15), (1, 32)):
        for k in range(2):
            base1[k + 2, row : row + 1, :] = wide_y_in[way, k : k + 1, :]
    for i, (dz, dy, _) in enumerate(corners):
        plane, row = (1 if dz == 1 else 4), (15 if dy == 1 else 32)
        base1[plane, row : row + 1, :] = wide_d_in[i]
    first_row, last_row = iota((8, 128), 0) == 0, iota((8, 128), 0) == 7
    window = pl.ds(pl.multiple_of(8 * gy, 8), 24)
    for k in range(7):
        even, odd = x_done[8 * k : 8 * k + 8, 0:128], x_done[8 * k : 8 * k + 8, 128:256]
        fine_rows[k, 0:8, :] = zero_plane
        fine_rows[k, 40:48, :] = zero_plane
        below = jnp.where(first_row, 0.0, pltpu.roll(odd, 1, 0))
        above = jnp.where(last_row, 0.0, pltpu.roll(even, 7, 0))
        fine_rows[k, pl.ds(8, 8, stride=4), :] = 0.75 * even + 0.25 * below
        fine_rows[k, pl.ds(9, 8, stride=4), :] = 0.75 * even + 0.25 * odd
        fine_rows[k, pl.ds(10, 8, stride=4), :] = 0.75 * odd + 0.25 * even
        fine_rows[k, pl.ds(11, 8, stride=4), :] = 0.75 * odd + 0.25 * above
        up2[k, 8:32, :] = fine_rows[k, window, :]

    def in_grid(shape, margin, first_row, rows, plane, planes):
        row = iota(shape, 0)
        at = row + first_row
        good = (row >= margin) & (row < shape[0] - margin) & (at >= 0) & (at < rows)
        return good & (plane >= 0) & (plane < planes)

    ups = []
    for k in range(5):
        here, near = coarse.neighbours(up2, k, 0, 24)
        up = base2[k + 1, 8:32, :] + (1.0 - OMEGA) * here + near * idg2[k]
        ups.append(jnp.where(in_grid((24, 128), 1, 8 * gy - 8, 8 * ny, gz + k - 2, nz), up, 0.0))

    spread_x1, spread_x0 = spread_matrix(128), spread_matrix(256)

    def prolong(ups, target, first, rows, spread_x, add):
        height = ups[0].shape[0]
        tall = 2 * height - 16
        n = height - 8
        x_done = dot(jnp.concatenate(ups, axis=0), spread_x)
        tiles = x_done.shape[1] // 128
        for t in range(tiles):
            for k in range(len(ups)):
                pair_rows[t, 0:height, :] = x_done[height * k : height * (k + 1), 128 * t : 128 * (t + 1)]
                here = 0.75 * pair_rows[t, 4 : 4 + n, :]
                fine_rows[k, pl.ds(0, n, stride=2), :] = here + 0.25 * pair_rows[t, 3 : 3 + n, :]
                fine_rows[k, pl.ds(1, n, stride=2), :] = here + 0.25 * pair_rows[t, 5 : 5 + n, :]
            cols = slice(128 * t, 128 * (t + 1))
            for k in range(6):
                parent_z = (k + first) // 2
                near_z = parent_z + 2 * ((k + first) % 2) - 1
                value = 0.75 * fine_rows[parent_z, 0:tall, :] + 0.25 * fine_rows[near_z, 0:tall, :]
                target[k, rows, cols] = target[k, rows, cols] + value if add else value

    prolong(ups, up1, 2, slice(8, 40), spread_x1, False)
    ups = []
    for k in range(4):
        parts = []
        for r, m in middle.chunks():
            here, near = middle.neighbours(up1, k, r, m)
            base = base1[k + 1, 8 + r : 8 + r + m, :]
            parts.append(base + (1.0 - OMEGA) * here + near * idg1[k, r : r + m, :])
        up = jnp.concatenate(parts, axis=0)
        ups.append(jnp.where(in_grid((32, 256), 7, 16 * gy - 8, 16 * ny, 2 * gz + k - 1, 2 * nz), up, 0.0))
    for k, plane in ((0, 0), (1, 5)):
        smo0[plane, 8:40, :] = far_smooth[k]
    for k in range(4):
        smo0[k + 1, 7:8, :] = rows_in[0, 2, k : k + 1, :]
        smo0[k + 1, 40:41, :] = rows_in[1, 2, k : k + 1, :]
    prolong(ups, smo0, 1, slice(0, 48), spread_x0, True)
    for k in range(4):
        for r, m in fine.chunks():
            here, near = fine.neighbours(smo0, k, r, m)
            out[k, r : r + m, :] = (1.0 - OMEGA) * here + (src0[k, r : r + m, :] + near) * fine.idg[k, r : r + m, :]

    wait_send(
        z_dens + z_vals + y_both + dens1_copies + copies2 + column_dens + y_smooth + layer_dens
        + column_src + layer_src + swap_z + swap_y + swap_d
    )


def coefficient_scratch(planes, rows, cols):
    own = pltpu.VMEM((planes, rows, cols), F32)
    return [own, pltpu.VMEM((planes, rows + 8, cols), F32), pltpu.VMEM((planes + 1, rows, cols), F32), own, own]


COPIES = 6 + 8 + 8 + 8 + 2 + 2 + 4 + 4 + 8 + 8 + 2 + 62 + 30


def per_device(density, right_side, pressure_guess):
    coarsest, longer = pltpu.VMEM((64, 8, 128), F32), pltpu.VMEM((65, 8, 128), F32)
    padded = pltpu.VMEM((70, 8, 128), F32)
    return pl.pallas_call(
        kernel,
        out_shape=jax.ShapeDtypeStruct(density.shape, F32),
        in_specs=[pl.BlockSpec(memory_space=pltpu.HBM)] * 3,
        out_specs=pl.BlockSpec(memory_space=pltpu.VMEM),
        scratch_shapes=[
            *[pltpu.VMEM((6, 48, 512), F32)] * 3,
            *[pltpu.VMEM((4, 32, 512), F32)] * 2,
            *coefficient_scratch(4, 32, 512),
            pltpu.VMEM((6, 48, 256), F32),
            *[pltpu.VMEM((6, 48, 256), F32)] * 4,
            *coefficient_scratch(4, 32, 256),
            pltpu.VMEM((7, 40, 128), F32),
            *[pltpu.VMEM((7, 40, 128), F32)] * 3,
            *coefficient_scratch(5, 24, 128),
            pltpu.VMEM((2, 3, 4, 512), F32),
            pltpu.VMEM((2, 3, 4, 512), F32),
            pltpu.VMEM((2, 2, 128), F32),
            pltpu.VMEM((4, 2, 4, 2, 128), F32),
            pltpu.VMEM((4, 2, 4, 2, 128), F32),
            pltpu.VMEM((2, 4, 8, 128), F32),
            pltpu.VMEM((16, 4, 8, 128), F32),
            pltpu.VMEM((16, 4, 8, 128), F32),
            pltpu.VMEM((66, 8, 128), F32),
            coarsest, coarsest, longer, coarsest,
            padded, padded, longer, longer, pltpu.VMEM((6, 8, 128), F32),
            pltpu.VMEM((8, 256), F32),
            pltpu.VMEM((8, 32, 128), F32),
            pltpu.VMEM((7, 48, 128), F32),
            pltpu.VMEM((2, 32, 512), F32),
            pltpu.VMEM((8, 512), F32),
            *[pltpu.VMEM((2, 2, 16, 256), F32)] * 2,
            *[pltpu.VMEM((2, 4, 256), F32)] * 2,
            *[pltpu.VMEM((4, 2, 256), F32)] * 2,
            *[pltpu.VMEM((2, 2, 256), F32)] * 2,
            *[pltpu.VMEM((4, 1, 256), F32)] * 2,
            *[pltpu.VMEM((2, 4, 256), F32)] * 2,
            *[pltpu.VMEM((4, 4, 256), F32)] * 2,
            pltpu.SemaphoreType.DMA((3,)),
            pltpu.SemaphoreType.DMA((COPIES,)),
            pltpu.SemaphoreType.DMA((COPIES,)),
        ],
        compiler_params=pltpu.CompilerParams(
            collective_id=0, has_side_effects=True, vmem_limit_bytes=32 * 1024 * 1024
        ),
        cost_estimate=pl.CostEstimate(flops=20_000_000, bytes_accessed=1 << 20, transcendentals=0),
    )(*[pltpu.with_memory_space_constraint(a, pltpu.HBM) for a in (density, right_side, pressure_guess)])


def solution(mesh):
    spec = P("gz", "gy", None)
    return jax.shard_map(per_device, mesh=mesh, in_specs=(spec, spec, spec), out_specs=spec, check_vma=False)
```

```python
import functools

import jax
import jax.numpy as jnp
from jax import lax
from jax.experimental import pallas as pl
from jax.experimental.pallas import tpu as pltpu
from jax.sharding import PartitionSpec as P

MESH = pl.DeviceIdType.MESH
SWEEPS = 8
OMEGA = 0.8
F32 = jnp.float32
PAD = 8


def dot(values, weights):
    rows = values.shape[0]
    if rows % 16:
        values = jnp.concatenate([values, jnp.zeros((16 - rows % 16, values.shape[1]), F32)], axis=0)
    total = values.shape[0]
    first = values.astype(jnp.bfloat16).astype(F32)
    rest = values - first
    second = rest.astype(jnp.bfloat16).astype(F32)
    parts = jnp.concatenate([first, second, rest - second], axis=0).astype(jnp.bfloat16)
    out = jnp.dot(parts, weights, preferred_element_type=F32)
    return (out[0:total] + out[total : 2 * total] + out[2 * total :])[0:rows]


def twice_inverse(total):
    guess = pltpu.reciprocal(total, approx=True)
    return guess * (4.0 - 2.0 * total * guess)


def iota(shape, axis):
    return lax.broadcasted_iota(jnp.int32, shape, axis)


def pair_matrix():
    rows, cols = iota((256, 128), 0), iota((256, 128), 1)
    return jnp.where(rows // 2 == cols, 0.125, 0.0).astype(jnp.bfloat16)


def spread_matrix(coarse):
    rows, cols = iota((coarse, 2 * coarse), 0), iota((coarse, 2 * coarse), 1)
    parent = cols // 2
    near = parent + 2 * (cols % 2) - 1
    return (jnp.where(rows == parent, 0.75, 0.0) + jnp.where(rows == near, 0.25, 0.0)).astype(jnp.bfloat16)


class Level:
    def __init__(self, shape, chunk, rho, bx, by, bz, dg, idg):
        self.planes, self.rows, self.cols = shape
        self.chunk = chunk
        self.rho, self.bx, self.by, self.bz, self.dg, self.idg = rho, bx, by, bz, dg, idg

        self.span = (0, self.rows)

    def chunks(self):
        return [(r, self.chunk) for r in range(*self.span, self.chunk)]

    def faces_x(self, plane):
        n = self.cols
        for r, m in self.chunks():
            rho = self.rho[plane + 1, PAD + r : PAD + r + m, :]
            lane = iota((m, n), 1)
            low = twice_inverse(rho + jnp.where(lane == 0, rho, pltpu.roll(rho, 1, 1)))
            high = jnp.where(lane == n - 1, twice_inverse(rho + rho), pltpu.roll(low, n - 1, 1))
            self.dg[plane, r : r + m, :] = low + high
            self.bx[plane, r : r + m, :] = jnp.where(lane == 0, 0.0, low)

    def faces_y(self, plane):
        for r, m in self.chunks():
            low = self.rho[plane + 1, PAD - 1 + r : PAD - 1 + r + m, :]
            high = self.rho[plane + 1, PAD + r : PAD + r + m, :]
            self.by[plane, r : r + m, :] = twice_inverse(low + high)
        last = self.span[1]
        low = self.rho[plane + 1, PAD - 1 + last : PAD + last, :]
        high = self.rho[plane + 1, PAD + last : PAD + last + 1, :]
        self.by[plane, last : last + 1, :] = twice_inverse(low + high)

    def faces_z(self, face):
        for r, m in self.chunks():
            low = self.rho[face, PAD + r : PAD + r + m, :]
            high = self.rho[face + 1, PAD + r : PAD + r + m, :]
            self.bz[face, r : r + m, :] = twice_inverse(low + high)

    def diagonal(self, plane):
        for r, m in self.chunks():
            total = self.dg[plane, r : r + m, :]
            total = total + self.by[plane, r : r + m, :] + self.by[plane, r + 1 : r + 1 + m, :]
            total = total + self.bz[plane, r : r + m, :] + self.bz[plane + 1, r : r + m, :]
            self.dg[plane, r : r + m, :] = total
            self.idg[plane, r : r + m, :] = (0.5 * OMEGA) * twice_inverse(total)

    def mask_y(self, plane, faces):
        for row, factor in faces:
            self.by[plane, row : row + 1, :] = self.by[plane, row : row + 1, :] * factor

    def mask_z(self, faces):
        for face, factor in faces:
            self.bz[face] = self.bz[face] * factor

    def neighbours(self, val, plane, r, m):
        n = self.cols
        rows = slice(PAD + r, PAD + r + m)
        here = val[plane + 1, rows, :]
        bx = self.bx[plane, r : r + m, :]
        total = self.bz[plane, r : r + m, :] * val[plane, rows, :]
        total = total + self.bz[plane + 1, r : r + m, :] * val[plane + 2, rows, :]
        total = total + self.by[plane, r : r + m, :] * val[plane + 1, PAD - 1 + r : PAD - 1 + r + m, :]
        total = total + self.by[plane, r + 1 : r + 1 + m, :] * val[plane + 1, PAD + 1 + r : PAD + 1 + r + m, :]
        total = total + bx * pltpu.roll(here, 1, 1)
        total = total + pltpu.roll(bx * here, n - 1, 1)
        return here, total


def kernel(
    dens_in, right_in, guess_in, out,
    rho0, val0, smo0, src0, res0, bx0, by0, bz0, dg0, idg0,
    rho1, val1, src1, base1, up1, bx1, by1, bz1, dg1, idg1,
    rho2, val2, base2, up2, bx2, by2, bz2, dg2, idg2,
    rows_out, rows_in, message, inbox_dens, inbox_src, tile, wide_dens, wide_src,
    rho3, bx3, by3, by3_up, bz3, dg3, dir3, res3, img3, mul3, cor3, pair_tmp, pair_rows, fine_rows,
    far_smooth, face_rows, z_out, z_in, y_out, y_in, d_out, d_in, wide_y_out, wide_y_in, wide_d_out, wide_d_in,
    dens_y_out, dens_y_in, dens_d_out, dens_d_in, local_sem, send_sem, recv_sem,
):
    gz, gy = lax.axis_index("gz"), lax.axis_index("gy")
    nz, ny = 128, 4
    core, ypos, xpos, zhi = gz % 2, (gz // 2) % 4, (gz // 8) % 4, gz // 32
    zpos = zhi * 4 + gy

    def gz_of(zh, x, y, c):
        return ((zh * 4 + x) * 4 + y) * 2 + c

    up_z, down_z = (gz + 1) % nz, (gz + nz - 1) % nz
    up_y, down_y = (gy + 1) % ny, (gy + ny - 1) % ny
    column = []
    for d in (8, 7, 9, 6, 10, 5, 11, 4, 12, 3, 13, 2, 14, 1, 15, 0):
        for k in range(2):
            if d or k:
                z = (zpos + d) % 16
                column.append((gz_of(z // 4, xpos, ypos, (core + k) % 2), z % 4))
    layer = []
    for i in (2, 1, 3, 0):
        for j in (2, 1, 3, 0):
            if i or j:
                layer.append((gz_of(zhi, (xpos + i) % 4, (ypos + j) % 4, core), gy))
    faces = [(up_z, gy), (down_z, gy), (gz, up_y), (gz, down_y)]
    around = []
    for dz in (1, -1):
        for dy in (0, 1, -1):
            around.append((dz, dy, ((gz + dz + nz) % nz, (gy + dy + ny) % ny)))
    corners = [(dz, dy, device) for dz, dy, device in around if dy]
    greeted = column + [device for _, _, device in around] + faces[2:] + layer

    barrier = pltpu.get_barrier_semaphore()
    for device in greeted:
        pl.semaphore_signal(barrier, inc=1, device_id=device, device_id_type=MESH)

    local = []
    for i, (source, target) in enumerate(
        ((dens_in, rho0.at[1:5, 8:40, :]), (guess_in, val0.at[1:5, 8:40, :]), (right_in, src0))
    ):
        copy = pltpu.make_async_copy(source, target, local_sem.at[i])
        copy.start()
        local.append(copy)

    count = [0]

    def send(source, target, device):
        i = count[0]
        count[0] = i + 1
        copy = pltpu.make_async_remote_copy(
            src_ref=source, dst_ref=target, send_sem=send_sem.at[i], recv_sem=recv_sem.at[i],
            device_id=device, device_id_type=MESH,
        )
        copy.start()
        return copy

    def wait_recv(copies):
        for copy in copies:
            copy.wait_recv()

    def wait_send(copies):
        for copy in copies:
            copy.wait_send()

    fine = Level((4, 32, 512), 8, rho0, bx0, by0, bz0, dg0, idg0)
    middle = Level((4, 32, 256), 16, rho1, bx1, by1, bz1, dg1, idg1)
    coarse = Level((5, 24, 128), 8, rho2, bx2, by2, bz2, dg2, idg2)

    z_low = jnp.where(gz > 0, 1.0, 0.0).astype(F32)
    z_high = jnp.where(gz < nz - 1, 1.0, 0.0).astype(F32)
    y_low = jnp.where(gy > 0, 1.0, 0.0).astype(F32)
    y_high = jnp.where(gy < ny - 1, 1.0, 0.0).astype(F32)

    pair_x = pair_matrix()

    def halve_x(blocks):
        rows = sum(block.shape[0] for block in blocks)
        summed = dot(jnp.concatenate([b[:, 0:256] for b in blocks] + [b[:, 256:512] for b in blocks], axis=0), pair_x)
        out, at = [], 0
        for block in blocks:
            n = block.shape[0]
            out.append((summed[at : at + n], summed[rows + at : rows + at + n]))
            at += n
        return out

    def halve_y(slot, value):
        n = value.shape[0]
        pair_rows[slot, 0:n, :] = value
        return pair_rows[slot, pl.ds(0, n // 2, stride=2), :] + pair_rows[slot, pl.ds(1, n // 2, stride=2), :]

    def halve_xy(blocks):
        return [
            jnp.concatenate([halve_y(2 * i, left), halve_y(2 * i + 1, right)], axis=1)
            for i, (left, right) in enumerate(halve_x(blocks))
        ]

    def restrict1(read):
        return halve_y(0, dot(read(0) + read(1), pair_x))

    half_rows, half_cols = iota((128, 256), 0), iota((128, 256), 1)
    to_halves = jnp.where((half_cols % 64 == half_rows // 2) & ((half_cols < 64) | (half_cols >= 192)), 0.125, 0.0).astype(jnp.bfloat16)

    def pack_message(field, value):
        pair_tmp[...] = dot(value, to_halves)
        for r in range(2):
            t = 4 * r
            message[field, r : r + 1, :] = (
                pair_tmp[t : t + 1, 0:128] + pair_tmp[t + 1 : t + 2, 0:128]
                + pair_tmp[t + 2 : t + 3, 128:256] + pair_tmp[t + 3 : t + 4, 128:256]
            )

    def gather_column(field, inbox):
        inbox[zhi, core, gy] = message[field]
        return [send(message.at[field], inbox.at[zhi, core, gy], device) for device in column]

    def gather_layer(field, inbox, wide):
        for zh in range(4):
            for y in range(4):
                tile[field, zh, 2 * y : 2 * y + 2, :] = inbox[zh, 0, y] + inbox[zh, 1, y]
        slot = xpos * 4 + ypos
        wide[slot] = tile[field]
        return [send(tile.at[field], wide.at[slot], device) for device in layer]

    local[0].wait()
    own1 = halve_xy([rho0[2 * k + 1, 8:40, :] + rho0[2 * k + 2, 8:40, :] for k in range(2)])
    for k in range(2):
        rho1[k + 2, 16:32, :] = own1[k]
    own2 = restrict1(lambda k: own1[k])
    rho2[3, 16:24, :] = own2
    pack_message(0, own2)
    local[1].wait()
    for k in range(4):
        for f, ref in ((0, rho0), (1, val0)):
            rows_out[0, f, k : k + 1, :] = ref[k + 1, 39:40, :]
            rows_out[1, f, k : k + 1, :] = ref[k + 1, 8:9, :]

    for way, (row, second) in enumerate(((31, 30), (16, 17))):
        for k in range(2):
            dens_y_out[way, 2 * k : 2 * k + 1, :] = rho1[k + 2, row : row + 1, :]
            dens_y_out[way, 2 * k + 1 : 2 * k + 2, :] = rho1[k + 2, second : second + 1, :]
    for i, (dz, dy, device) in enumerate(corners):
        plane, far_plane = (3, 2) if dz == 1 else (2, 3)
        row, second = (31, 30) if dy == 1 else (16, 17)
        for at, (p, r) in enumerate(((plane, row), (plane, second), (far_plane, row), (far_plane, second))):
            dens_d_out[i, at : at + 1, :] = rho1[p, r : r + 1, :]
    for k in (0, 5):
        smo0[k, 8:40, :] = jnp.zeros((32, 512), F32)
    for k in range(1, 5):
        smo0[k, 7:8, :] = jnp.zeros((1, 512), F32)
        smo0[k, 40:41, :] = jnp.zeros((1, 512), F32)

    pl.semaphore_wait(barrier, len(greeted))

    z_dens = [
        send(rho0.at[4, 8:40, :], rho0.at[0, 8:40, :], faces[0]),
        send(rho0.at[1, 8:40, :], rho0.at[5, 8:40, :], faces[1]),
    ]
    z_vals = [
        send(val0.at[4, 8:40, :], val0.at[0, 8:40, :], faces[0]),
        send(val0.at[1, 8:40, :], val0.at[5, 8:40, :], faces[1]),
    ]
    y_both = [
        send(rows_out.at[0, 0:2], rows_in.at[0, 0:2], faces[2]),
        send(rows_out.at[1, 0:2], rows_in.at[1, 0:2], faces[3]),
    ]

    dens1_copies = [
        send(rho1.at[2:4, 16:32, :], rho1.at[0:2, 16:32, :], faces[0]),
        send(rho1.at[2:4, 16:32, :], rho1.at[4:6, 16:32, :], faces[1]),
        send(dens_y_out.at[0], dens_y_in.at[0], faces[2]),
        send(dens_y_out.at[1], dens_y_in.at[1], faces[3]),
    ]
    for i, (dz, dy, device) in enumerate(corners):
        dens1_copies.append(send(dens_d_out.at[i], dens_d_in.at[i], device))

    rows2 = {dy: (slice(16, 24), slice(16 - 8 * dy, 24 - 8 * dy)) for dy in (0, 1, -1)}
    y_ways = ((1, faces[2]), (-1, faces[3]))
    z_ways = ((1, faces[0]), (-1, faces[1]))

    def fill_y(ref, planes, rows, first):
        last = first + rows - 1
        for k in planes:
            ref[k, first - 1 : first, :] = jnp.where(gy == 0, ref[k, first : first + 1, :], ref[k, first - 1 : first, :])
            ref[k, last + 1 : last + 2, :] = jnp.where(
                gy == ny - 1, ref[k, last : last + 1, :], ref[k, last + 1 : last + 2, :]
            )

    def fill_z(ref, own, planes, rows, reach):
        for i in range(reach):
            low, high = own - 1 - i * planes, own + planes + i * planes
            ref[low, rows, :] = jnp.where(gz == i, ref[low + 1, rows, :], ref[low, rows, :])
            ref[high, rows, :] = jnp.where(gz == nz - 1 - i, ref[high - 1, rows, :], ref[high, rows, :])

    for k in range(4):
        fine.faces_x(k)
    for face in (1, 2, 3):
        fine.faces_z(face)
    wait_recv(y_both)
    for k in range(4):
        for f, ref in ((0, rho0), (1, val0)):
            ref[k + 1, 7:8, :] = rows_in[0, f, k : k + 1, :]
            ref[k + 1, 40:41, :] = rows_in[1, f, k : k + 1, :]
    fill_y(rho0, range(1, 5), 32, 8)
    for k in range(4):
        fine.faces_y(k)
    local[2].wait()

    def smooth(plane):
        for r, m in fine.chunks():
            here, near = fine.neighbours(val0, plane, r, m)
            smo0[plane + 1, 8 + r : 8 + r + m, :] = (1.0 - OMEGA) * here + (
                src0[plane, r : r + m, :] + near
            ) * fine.idg[plane, r : r + m, :]

    for k in (1, 2):
        fine.diagonal(k)
        fine.mask_y(k, ((0, y_low), (32, y_high)))
        smooth(k)
    wait_recv(z_dens)
    fill_z(rho0, 1, 4, slice(8, 40), 1)
    for face in (0, 4):
        fine.faces_z(face)
    for k in (0, 3):
        fine.diagonal(k)
        fine.mask_y(k, ((0, y_low), (32, y_high)))
    fine.mask_z(((0, z_low), (4, z_high)))
    wait_recv(z_vals)
    smooth(3)
    smooth(0)

    for plane in range(4):
        for r, m in fine.chunks():
            here, near = fine.neighbours(smo0, plane, r, m)
            res0[plane, r : r + m, :] = src0[plane, r : r + m, :] - dg0[plane, r : r + m, :] * here + near
    for way, (row, cell) in enumerate(((32, 39), (0, 8))):
        for k in range(2):
            lower = by0[2 * k, row : row + 1, :] * smo0[2 * k + 1, cell : cell + 1, :]
            upper = by0[2 * k + 1, row : row + 1, :] * smo0[2 * k + 2, cell : cell + 1, :]
            face_rows[2 * way + k : 2 * way + k + 1, :] = lower + upper
    blocks = halve_x(
        [res0[0] + res0[1], res0[2] + res0[3], bz0[4] * smo0[4, 8:40, :], bz0[0] * smo0[1, 8:40, :], face_rows[...]]
    )
    part0, part1, give_up, give_down = [
        jnp.concatenate([halve_y(2 * i, left), halve_y(2 * i + 1, right)], axis=1)
        for i, (left, right) in enumerate(blocks[:4])
    ]
    give_rows = jnp.concatenate(blocks[4], axis=1)
    parts = (part0, part1)
    z_out[0, 0] = give_up
    z_out[0, 1] = part1
    z_out[1, 0] = give_down
    z_out[1, 1] = part0
    swap_z = [send(z_out.at[way], z_in.at[way], faces[way]) for way in range(2)]
    for way, row in ((0, 15), (1, 0)):
        for k in range(2):
            y_out[way, k : k + 1, :] = parts[k][row : row + 1]
            y_out[way, 2 + k : 3 + k, :] = give_rows[2 * way + k : 2 * way + k + 1]
    swap_y = [send(y_out.at[way], y_in.at[way], faces[2 + way]) for way in range(2)]
    slot_of, swap_d = {}, []
    for i, (dz, dy, device) in enumerate(corners):
        slot_of[dz, dy] = i
        way = (1 - dy) // 2
        plane = (1 + dz) // 2
        give, row = (give_up if dz == 1 else give_down), (15 if dy == 1 else 0)
        d_out[i, 0:1, :] = give_rows[2 * way + plane : 2 * way + plane + 1]
        d_out[i, 1:2, :] = give[row : row + 1]
        swap_d.append(send(d_out.at[i], d_in.at[i], device))
    column_dens = gather_column(0, inbox_dens)
    dens2_near = [send(rho2.at[3, 16:24, :], rho2.at[3, rows2[dy][1], :], device) for dy, device in y_ways]
    dens2_near += [
        send(rho2.at[3, 16:24, :], rho2.at[3 - dz, rows2[dy][1], :], device) for dz, dy, device in around
    ]

    def coefficients(level, planes, z_faces):
        for k in planes:
            level.faces_x(k)
            level.faces_y(k)
        for k in range(planes[0], planes[-1] + 2):
            level.faces_z(k)
        for k in planes:
            level.diagonal(k)
            level.mask_y(k, ((8, y_low), (level.rows - 8, y_high)))
        level.mask_z(z_faces)

    wait_recv(dens1_copies)
    for way, (row, second) in enumerate(((15, 14), (32, 33))):
        for k in range(2):
            rho1[k + 2, row : row + 1, :] = dens_y_in[way, 2 * k : 2 * k + 1, :]
            rho1[k + 2, second : second + 1, :] = dens_y_in[way, 2 * k + 1 : 2 * k + 2, :]
    for i, (dz, dy, device) in enumerate(corners):
        plane, far_plane = (1, 0) if dz == 1 else (4, 5)
        row, second = (15, 14) if dy == 1 else (32, 33)
        for at, (p, r) in enumerate(((plane, row), (plane, second), (far_plane, row), (far_plane, second))):
            rho1[p, r : r + 1, :] = dens_d_in[i, at : at + 1, :]
    fill_y(rho1, range(6), 16, 16)
    fill_z(rho1, 2, 2, slice(8, 40), 1)
    coefficients(middle, range(4), ((1, z_low), (3, z_high)))
    wait_recv(dens2_near)
    fill_y(rho2, (3,), 8, 16)
    fill_z(rho2, 3, 1, slice(16, 24), 1)
    coarse.span = (8, 16)
    coefficients(coarse, (2,), ((2, z_low), (3, z_high)))
    coarse.span = (0, 24)

    wait_recv(swap_z + swap_y + swap_d)
    source1 = []
    for k in range(2):
        src1[k + 2, 16:32, :] = parts[k] + z_in[k, 0]
        src1[k + 2, 16:17, :] = src1[k + 2, 16:17, :] + y_in[0, 2 + k : 3 + k, :]
        src1[k + 2, 31:32, :] = src1[k + 2, 31:32, :] + y_in[1, 2 + k : 3 + k, :]
        source1.append(src1[k + 2, 16:32, :])
        val1[k + 2, 16:32, :] = 4.0 * source1[k] * idg1[k + 1, 8:24, :]
    for dz, plane, theirs, mine in ((1, 4, z_in[1, 1], give_up), (-1, 1, z_in[0, 1], give_down)):
        src1[plane, 16:32, :] = theirs + mine
        low, high = slot_of[-dz, 1], slot_of[-dz, -1]
        src1[plane, 16:17, :] = src1[plane, 16:17, :] + d_in[low, 0:1, :]
        src1[plane, 31:32, :] = src1[plane, 31:32, :] + d_in[high, 0:1, :]
        val1[plane, 16:32, :] = 4.0 * src1[plane, 16:32, :] * idg1[plane - 1, 8:24, :]
    for dy, row in ((1, 32), (-1, 15)):
        way = (1 - dy) // 2
        for k, dz in ((0, -1), (1, 1)):
            total = y_in[1 - way, k : k + 1, :] + give_rows[2 * way + k : 2 * way + k + 1]
            total = total + d_in[slot_of[-dz, -dy], 1:2, :]
            src1[k + 2, row : row + 1, :] = total
            val1[k + 2, row : row + 1, :] = 4.0 * total * idg1[k + 1, row - 8 : row - 7, :]

    def residual1(k):
        here, near = middle.neighbours(val1, k + 1, 8, 16)
        base1[k + 2, 16:32, :] = (1.0 - OMEGA) * here + (4.0 * source1[k] + near) * idg1[k + 1, 8:24, :]
        return (1.0 - OMEGA) * source1[k] + 0.25 * near

    source2 = restrict1(residual1)
    val2[3, 16:24, :] = 16.0 * source2 * idg2[2, 8:16, :]
    copies2 = [send(val2.at[3, 16:24, :], val2.at[3, rows2[dy][1], :], device) for dy, device in y_ways]
    for dz, device in z_ways:
        copies2.append(send(val2.at[3, 16:24, :], val2.at[3 - dz, 16:24, :], device))

    def pass_on(ref, reach):
        return [
            send(ref.at[4 - reach, 8:32, :], ref.at[3 - reach, 8:32, :], faces[0]),
            send(ref.at[2 + reach, 8:32, :], ref.at[3 + reach, 8:32, :], faces[1]),
        ]

    dens2_far = pass_on(rho2, 2)
    more1 = [
        send(base1.at[3, 16:32, :], base1.at[1, 16:32, :], faces[0]),
        send(base1.at[2, 16:32, :], base1.at[4, 16:32, :], faces[1]),
    ]
    for way, row in ((0, 31), (1, 16)):
        for k in range(2):
            wide_y_out[way, k : k + 1, :] = base1[k + 2, row : row + 1, :]
        more1.append(send(wide_y_out.at[way], wide_y_in.at[way], faces[2 + way]))
    for i, (dz, dy, device) in enumerate(corners):
        plane, row = (3 if dz == 1 else 2), (31 if dy == 1 else 16)
        wide_d_out[i] = base1[plane, row : row + 1, :]
        more1.append(send(wide_d_out.at[i], wide_d_in.at[i], device))
    wait_recv(column_dens)
    layer_dens = gather_layer(0, inbox_dens, wide_dens)
    wait_recv(copies2)
    here, near = coarse.neighbours(val2, 2, 8, 8)
    pack_message(1, (1.0 - OMEGA) * source2 + 0.0625 * near)
    base2[3, 16:24, :] = (1.0 - OMEGA) * here + (16.0 * source2 + near) * idg2[2, 8:16, :]
    column_src = gather_column(1, inbox_src)
    more2 = [send(base2.at[3, 16:24, :], base2.at[3, rows2[dy][1], :], device) for dy, device in y_ways]
    more2 += [send(base2.at[3, 16:24, :], base2.at[3 - dz, rows2[dy][1], :], device) for dz, dy, device in around]
    wait_recv(dens2_far)
    dens2_last = pass_on(rho2, 3)

    wait_recv(layer_dens)
    lane, sub = iota((8, 128), 1), iota((8, 128), 0)
    right_half = lane >= 64
    first_x, last_x = (lane % 64) == 0, (lane % 64) == 63
    first_y, last_y = (lane < 64) & (sub == 0), (lane >= 64) & (sub == 7)

    def lower_y(v):
        q = pltpu.roll(v, 64, 1)
        return jnp.where(right_half, q, pltpu.roll(q, 1, 0))

    def upper_y(v):
        q = pltpu.roll(v, 64, 1)
        return jnp.where(right_half, pltpu.roll(q, 7, 0), q)

    scale3 = 0.015625
    for zh in range(4):
        for s in range(16):
            rho3[1 + 16 * zh + s] = wide_dens[s, zh]
    rho3[0] = rho3[1]
    rho3[65] = rho3[64]

    def face3(k, _):
        bz3[k] = scale3 * twice_inverse(rho3[k] + rho3[k + 1])
        return 0

    lax.fori_loop(0, 65, face3, 0)

    def coef3(k, _):
        rho = rho3[k + 1]
        edge = twice_inverse(rho + rho)
        low = twice_inverse(rho + jnp.where(first_x, rho, pltpu.roll(rho, 1, 1)))
        total = low + jnp.where(last_x, edge, pltpu.roll(low, 127, 1))
        bx3[k] = jnp.where(first_x, 0.0, scale3 * low)
        low = twice_inverse(rho + jnp.where(first_y, rho, lower_y(rho)))
        high = upper_y(low)
        total = total + low + jnp.where(last_y, edge, high)
        by3_up[k] = jnp.where(last_y, 0.0, scale3 * high)
        by3[k] = jnp.where(first_y, 0.0, scale3 * low)
        dg3[k] = scale3 * total + bz3[k] + bz3[k + 1]
        return 0

    lax.fori_loop(0, 64, coef3, 0, unroll=4)

    zero_plane = jnp.zeros((8, 128), F32)
    lowest = (gz + 1) // 2 - 1
    cor3[...] = jnp.zeros((6, 8, 128), F32)
    for k in (0, 1, 2, 67, 68, 69):
        dir3[k] = zero_plane
        res3[k] = zero_plane
    mul3[64] = zero_plane
    img3[64] = zero_plane

    def clear3(k, _):
        dir3[k + 3] = zero_plane
        mul3[k] = zero_plane
        return 0

    lax.fori_loop(0, 64, clear3, 0, unroll=8)

    wait_send(
        z_dens + z_vals + y_both + dens1_copies + swap_z + swap_y + swap_d + column_dens + layer_dens + copies2
    )
    wait_recv(column_src)
    layer_src = gather_layer(1, inbox_src, wide_src)

    z_smooth = [
        send(smo0.at[4, 8:40, :], far_smooth.at[0], faces[0]), send(smo0.at[1, 8:40, :], far_smooth.at[1], faces[1])
    ]
    for k in range(4):
        rows_out[0, 2, k : k + 1, :] = smo0[k + 1, 39:40, :]
        rows_out[1, 2, k : k + 1, :] = smo0[k + 1, 8:9, :]
    y_smooth = [send(rows_out.at[way, 2], rows_in.at[way, 2], faces[2 + way]) for way in range(2)]
    wait_recv(more2)
    base2_far = pass_on(base2, 2)

    wait_recv(dens2_last)
    wait_send(dens2_near + dens2_far + dens2_last + more1 + more2 + column_src)

    def inside_z(face):
        at = gz + face - 2
        return jnp.where((at > 0) & (at < nz), 1.0, 0.0).astype(F32)

    fill_y(rho2, range(7), 8, 16)
    fill_z(rho2, 3, 1, slice(8, 32), 3)
    coefficients(coarse, range(5), [(face, inside_z(face)) for face in range(6)])

    wait_recv(layer_src)

    for zh in range(4):
        for k in range(16):
            res3[16 * zh + k + 3] = wide_src[k, zh]

    def whole(v):
        return jnp.sum(jnp.sum(v, axis=1, keepdims=True), axis=0, keepdims=True)

    def apply(k, prev, here, later):
        bx = bx3[k]
        swapped = pltpu.roll(here, 64, 1)
        below = jnp.where(right_half, swapped, pltpu.roll(swapped, 1, 0))
        above = jnp.where(right_half, pltpu.roll(swapped, 7, 0), swapped)
        image = (dg3[k] * here - bz3[k] * prev) - (bz3[k + 1] * later + by3[k] * below)
        image = image - ((bx * pltpu.roll(here, 1, 1) + by3_up[k] * above) + pltpu.roll(bx * here, 127, 1))
        img3[k] = image
        return image

    def advance(k, alpha, beta):
        dir3[k + 3] = res3[k + 3] + beta * dir3[k + 3]
        image = img3[k] + beta * mul3[k]
        mul3[k] = image
        resid = res3[k + 3] - alpha * image
        res3[k + 3] = resid
        return resid

    def totals(first, next_resid):
        def plane(k, carry):
            norm, power, prev, here = carry
            later = next_resid(k + 1)
            image = apply(k, prev, here, later)
            return norm + here * here, power + here * image, here, later

        norm, power, _, _ = lax.fori_loop(0, 64, plane, (zero_plane, zero_plane, zero_plane, first), unroll=64)
        return whole(norm), whole(power)

    norm, power = totals(res3[3], lambda k: res3[k + 3])

    def sweep(step, carry):
        alpha, beta, norm = carry
        norm_next, power = totals(advance(0, alpha, beta), lambda k: advance(k, alpha, beta))
        cor3[...] = cor3[...] + alpha * dir3[pl.ds(lowest + 1, 6)]
        beta = norm_next / norm
        return norm_next / (power - beta * norm_next / alpha), beta, norm_next

    alpha, beta, _ = lax.fori_loop(0, SWEEPS - 1, sweep, (norm / power, jnp.zeros((1, 1), F32), norm))

    window = pl.ds(lowest + 1, 6)
    cor3[...] = cor3[...] + alpha * (res3[window] + beta * dir3[window])

    spread_rows, spread_cols = iota((128, 256), 0), iota((128, 256), 1)
    fine_x = spread_cols % 128
    parent = fine_x // 2
    near = parent + 2 * (fine_x % 2) - 1
    half = spread_cols // 128
    inside = (near >= 0) & (near < 64)
    from_halves = (
        jnp.where(spread_rows == parent + 64 * half, 0.75, 0.0)
        + jnp.where((spread_rows == near + 64 * half) & inside, 0.25, 0.0)
    ).astype(jnp.bfloat16)
    mixed = []
    for d in range(-3, 4):
        plane = gz + d + 4
        index = plane // 2 - lowest
        other = index + 2 * (plane % 2) - 1
        mixed.append(0.75 * cor3[index] + 0.25 * cor3[other])
    x_done = dot(jnp.concatenate(mixed, axis=0), from_halves)
    wait_recv(more1 + base2_far + z_smooth + y_smooth)
    wait_send(z_smooth)
    for way, row in ((0, 15), (1, 32)):
        for k in range(2):
            base1[k + 2, row : row + 1, :] = wide_y_in[way, k : k + 1, :]
    for i, (dz, dy, _) in enumerate(corners):
        plane, row = (1 if dz == 1 else 4), (15 if dy == 1 else 32)
        base1[plane, row : row + 1, :] = wide_d_in[i]
    first_row, last_row = iota((8, 128), 0) == 0, iota((8, 128), 0) == 7
    window = pl.ds(pl.multiple_of(8 * gy, 8), 24)
    for k in range(7):
        even, odd = x_done[8 * k : 8 * k + 8, 0:128], x_done[8 * k : 8 * k + 8, 128:256]
        fine_rows[k, 0:8, :] = zero_plane
        fine_rows[k, 40:48, :] = zero_plane
        below = jnp.where(first_row, 0.0, pltpu.roll(odd, 1, 0))
        above = jnp.where(last_row, 0.0, pltpu.roll(even, 7, 0))
        fine_rows[k, pl.ds(8, 8, stride=4), :] = 0.75 * even + 0.25 * below
        fine_rows[k, pl.ds(9, 8, stride=4), :] = 0.75 * even + 0.25 * odd
        fine_rows[k, pl.ds(10, 8, stride=4), :] = 0.75 * odd + 0.25 * even
        fine_rows[k, pl.ds(11, 8, stride=4), :] = 0.75 * odd + 0.25 * above
        up2[k, 8:32, :] = fine_rows[k, window, :]

    def in_grid(shape, margin, first_row, rows, plane, planes):
        row = iota(shape, 0)
        at = row + first_row
        good = (row >= margin) & (row < shape[0] - margin) & (at >= 0) & (at < rows)
        return good & (plane >= 0) & (plane < planes)

    ups = []
    for k in range(5):
        here, near = coarse.neighbours(up2, k, 0, 24)
        up = base2[k + 1, 8:32, :] + (1.0 - OMEGA) * here + near * idg2[k]
        ups.append(jnp.where(in_grid((24, 128), 1, 8 * gy - 8, 8 * ny, gz + k - 2, nz), up, 0.0))

    spread_x1, spread_x0 = spread_matrix(128), spread_matrix(256)

    def prolong(ups, target, first, rows, spread_x, add):
        height = ups[0].shape[0]
        tall = 2 * height - 16
        n = height - 8
        x_done = dot(jnp.concatenate(ups, axis=0), spread_x)
        tiles = x_done.shape[1] // 128
        for t in range(tiles):
            for k in range(len(ups)):
                pair_rows[t, 0:height, :] = x_done[height * k : height * (k + 1), 128 * t : 128 * (t + 1)]
                here = 0.75 * pair_rows[t, 4 : 4 + n, :]
                fine_rows[k, pl.ds(0, n, stride=2), :] = here + 0.25 * pair_rows[t, 3 : 3 + n, :]
                fine_rows[k, pl.ds(1, n, stride=2), :] = here + 0.25 * pair_rows[t, 5 : 5 + n, :]
            cols = slice(128 * t, 128 * (t + 1))
            for k in range(6):
                parent_z = (k + first) // 2
                near_z = parent_z + 2 * ((k + first) % 2) - 1
                value = 0.75 * fine_rows[parent_z, 0:tall, :] + 0.25 * fine_rows[near_z, 0:tall, :]
                target[k, rows, cols] = target[k, rows, cols] + value if add else value

    prolong(ups, up1, 2, slice(8, 40), spread_x1, False)
    ups = []
    for k in range(4):
        parts = []
        for r, m in middle.chunks():
            here, near = middle.neighbours(up1, k, r, m)
            base = base1[k + 1, 8 + r : 8 + r + m, :]
            parts.append(base + (1.0 - OMEGA) * here + near * idg1[k, r : r + m, :])
        up = jnp.concatenate(parts, axis=0)
        ups.append(jnp.where(in_grid((32, 256), 7, 16 * gy - 8, 16 * ny, 2 * gz + k - 1, 2 * nz), up, 0.0))
    for k, plane in ((0, 0), (1, 5)):
        smo0[plane, 8:40, :] = far_smooth[k]
    for k in range(4):
        smo0[k + 1, 7:8, :] = rows_in[0, 2, k : k + 1, :]
        smo0[k + 1, 40:41, :] = rows_in[1, 2, k : k + 1, :]
    prolong(ups, smo0, 1, slice(0, 48), spread_x0, True)
    for k in range(4):
        for r, m in fine.chunks():
            here, near = fine.neighbours(smo0, k, r, m)
            out[k, r : r + m, :] = (1.0 - OMEGA) * here + (src0[k, r : r + m, :] + near) * fine.idg[k, r : r + m, :]

    wait_send(y_smooth + layer_src + base2_far)


def coefficient_scratch(planes, rows, cols):
    own = pltpu.VMEM((planes, rows, cols), F32)
    return [own, pltpu.VMEM((planes, rows + 8, cols), F32), pltpu.VMEM((planes + 1, rows, cols), F32), own, own]


COPIES = 6 + 8 + 8 + 8 + 2 + 2 + 4 + 4 + 8 + 8 + 2 + 62 + 30


def per_device(density, right_side, pressure_guess):
    coarsest, longer = pltpu.VMEM((64, 8, 128), F32), pltpu.VMEM((65, 8, 128), F32)
    padded = pltpu.VMEM((70, 8, 128), F32)
    return pl.pallas_call(
        kernel,
        out_shape=jax.ShapeDtypeStruct(density.shape, F32),
        in_specs=[pl.BlockSpec(memory_space=pltpu.HBM)] * 3,
        out_specs=pl.BlockSpec(memory_space=pltpu.VMEM),
        scratch_shapes=[
            *[pltpu.VMEM((6, 48, 512), F32)] * 3,
            *[pltpu.VMEM((4, 32, 512), F32)] * 2,
            *coefficient_scratch(4, 32, 512),
            pltpu.VMEM((6, 48, 256), F32),
            *[pltpu.VMEM((6, 48, 256), F32)] * 4,
            *coefficient_scratch(4, 32, 256),
            pltpu.VMEM((7, 40, 128), F32),
            *[pltpu.VMEM((7, 40, 128), F32)] * 3,
            *coefficient_scratch(5, 24, 128),
            pltpu.VMEM((2, 3, 4, 512), F32),
            pltpu.VMEM((2, 3, 4, 512), F32),
            pltpu.VMEM((2, 2, 128), F32),
            pltpu.VMEM((4, 2, 4, 2, 128), F32),
            pltpu.VMEM((4, 2, 4, 2, 128), F32),
            pltpu.VMEM((2, 4, 8, 128), F32),
            pltpu.VMEM((16, 4, 8, 128), F32),
            pltpu.VMEM((16, 4, 8, 128), F32),
            pltpu.VMEM((66, 8, 128), F32),
            coarsest, coarsest, coarsest, longer, coarsest,
            padded, padded, longer, longer, pltpu.VMEM((6, 8, 128), F32),
            pltpu.VMEM((8, 256), F32),
            pltpu.VMEM((8, 32, 128), F32),
            pltpu.VMEM((7, 48, 128), F32),
            pltpu.VMEM((2, 32, 512), F32),
            pltpu.VMEM((8, 512), F32),
            *[pltpu.VMEM((2, 2, 16, 256), F32)] * 2,
            *[pltpu.VMEM((2, 4, 256), F32)] * 2,
            *[pltpu.VMEM((4, 2, 256), F32)] * 2,
            *[pltpu.VMEM((2, 2, 256), F32)] * 2,
            *[pltpu.VMEM((4, 1, 256), F32)] * 2,
            *[pltpu.VMEM((2, 4, 256), F32)] * 2,
            *[pltpu.VMEM((4, 4, 256), F32)] * 2,
            pltpu.SemaphoreType.DMA((3,)),
            pltpu.SemaphoreType.DMA((COPIES,)),
            pltpu.SemaphoreType.DMA((COPIES,)),
        ],
        compiler_params=pltpu.CompilerParams(
            collective_id=0, has_side_effects=True, vmem_limit_bytes=32 * 1024 * 1024
        ),
        cost_estimate=pl.CostEstimate(flops=20_000_000, bytes_accessed=1 << 20, transcendentals=0),
    )(*[pltpu.with_memory_space_constraint(a, pltpu.HBM) for a in (density, right_side, pressure_guess)])


def solution(mesh):
    spec = P("gz", "gy", None)
    return jax.shard_map(per_device, mesh=mesh, in_specs=(spec, spec, spec), out_specs=spec, check_vma=False)
```

```python
import functools

import jax
import jax.numpy as jnp
from jax import lax
from jax.experimental import pallas as pl
from jax.experimental.pallas import tpu as pltpu
from jax.sharding import PartitionSpec as P

MESH = pl.DeviceIdType.MESH
SWEEPS = 8
OMEGA = 0.8
F32 = jnp.float32
PAD = 8


def dot(values, weights):
    rows = values.shape[0]
    if rows % 16:
        values = jnp.concatenate([values, jnp.zeros((16 - rows % 16, values.shape[1]), F32)], axis=0)
    total = values.shape[0]
    first = values.astype(jnp.bfloat16).astype(F32)
    rest = values - first
    second = rest.astype(jnp.bfloat16).astype(F32)
    parts = jnp.concatenate([first, second, rest - second], axis=0).astype(jnp.bfloat16)
    out = jnp.dot(parts, weights, preferred_element_type=F32)
    return (out[0:total] + out[total : 2 * total] + out[2 * total :])[0:rows]


def twice_inverse(total):
    guess = pltpu.reciprocal(total, approx=True)
    return guess * (4.0 - 2.0 * total * guess)


def iota(shape, axis):
    return lax.broadcasted_iota(jnp.int32, shape, axis)


def pair_matrix():
    rows, cols = iota((256, 128), 0), iota((256, 128), 1)
    return jnp.where(rows // 2 == cols, 0.125, 0.0).astype(jnp.bfloat16)


def spread_matrix(coarse):
    rows, cols = iota((coarse, 2 * coarse), 0), iota((coarse, 2 * coarse), 1)
    parent = cols // 2
    near = parent + 2 * (cols % 2) - 1
    return (jnp.where(rows == parent, 0.75, 0.0) + jnp.where(rows == near, 0.25, 0.0)).astype(jnp.bfloat16)


class Level:
    def __init__(self, shape, chunk, rho, bx, by, bz, dg, idg):
        self.planes, self.rows, self.cols = shape
        self.chunk = chunk
        self.rho, self.bx, self.by, self.bz, self.dg, self.idg = rho, bx, by, bz, dg, idg

        self.span = (0, self.rows)

    def chunks(self):
        return [(r, self.chunk) for r in range(*self.span, self.chunk)]

    def faces_x(self, plane):
        n = self.cols
        for r, m in self.chunks():
            rho = self.rho[plane + 1, PAD + r : PAD + r + m, :]
            lane = iota((m, n), 1)
            low = twice_inverse(rho + jnp.where(lane == 0, rho, pltpu.roll(rho, 1, 1)))
            high = jnp.where(lane == n - 1, twice_inverse(rho + rho), pltpu.roll(low, n - 1, 1))
            self.dg[plane, r : r + m, :] = low + high
            self.bx[plane, r : r + m, :] = jnp.where(lane == 0, 0.0, low)

    def faces_y(self, plane):
        for r, m in self.chunks():
            low = self.rho[plane + 1, PAD - 1 + r : PAD - 1 + r + m, :]
            high = self.rho[plane + 1, PAD + r : PAD + r + m, :]
            self.by[plane, r : r + m, :] = twice_inverse(low + high)
        last = self.span[1]
        low = self.rho[plane + 1, PAD - 1 + last : PAD + last, :]
        high = self.rho[plane + 1, PAD + last : PAD + last + 1, :]
        self.by[plane, last : last + 1, :] = twice_inverse(low + high)

    def faces_z(self, face):
        for r, m in self.chunks():
            low = self.rho[face, PAD + r : PAD + r + m, :]
            high = self.rho[face + 1, PAD + r : PAD + r + m, :]
            self.bz[face, r : r + m, :] = twice_inverse(low + high)

    def diagonal(self, plane):
        for r, m in self.chunks():
            total = self.dg[plane, r : r + m, :]
            total = total + self.by[plane, r : r + m, :] + self.by[plane, r + 1 : r + 1 + m, :]
            total = total + self.bz[plane, r : r + m, :] + self.bz[plane + 1, r : r + m, :]
            self.dg[plane, r : r + m, :] = total
            self.idg[plane, r : r + m, :] = (0.5 * OMEGA) * twice_inverse(total)

    def mask_y(self, plane, faces):
        for row, factor in faces:
            self.by[plane, row : row + 1, :] = self.by[plane, row : row + 1, :] * factor

    def mask_z(self, faces):
        for face, factor in faces:
            self.bz[face] = self.bz[face] * factor

    def neighbours(self, val, plane, r, m):
        n = self.cols
        rows = slice(PAD + r, PAD + r + m)
        here = val[plane + 1, rows, :]
        bx = self.bx[plane, r : r + m, :]
        total = self.bz[plane, r : r + m, :] * val[plane, rows, :]
        total = total + self.bz[plane + 1, r : r + m, :] * val[plane + 2, rows, :]
        total = total + self.by[plane, r : r + m, :] * val[plane + 1, PAD - 1 + r : PAD - 1 + r + m, :]
        total = total + self.by[plane, r + 1 : r + 1 + m, :] * val[plane + 1, PAD + 1 + r : PAD + 1 + r + m, :]
        total = total + bx * pltpu.roll(here, 1, 1)
        total = total + pltpu.roll(bx * here, n - 1, 1)
        return here, total


def kernel(
    dens_in, right_in, guess_in, out,
    rho0, val0, smo0, src0, res0, bx0, by0, bz0, dg0, idg0,
    rho1, val1, src1, base1, up1, bx1, by1, bz1, dg1, idg1,
    rho2, val2, base2, up2, bx2, by2, bz2, dg2, idg2,
    rows_out, rows_in, message, inbox_dens, inbox_src, tile, wide_dens, wide_src,
    rho3, bx3, by3, by3_up, bz3, dg3, dir3, res3, img3, mul3, cor3, pair_tmp, pair_rows, fine_rows,
    far_smooth, face_rows, z_out, z_in, y_out, y_in, d_out, d_in, wide_y_out, wide_y_in, wide_d_out, wide_d_in,
    dens_y_out, dens_y_in, dens_d_out, dens_d_in, local_sem, send_sem, recv_sem,
):
    gz, gy = lax.axis_index("gz"), lax.axis_index("gy")
    nz, ny = 128, 4
    core, ypos, xpos, zhi = gz % 2, (gz // 2) % 4, (gz // 8) % 4, gz // 32
    zpos = zhi * 4 + gy

    def gz_of(zh, x, y, c):
        return ((zh * 4 + x) * 4 + y) * 2 + c

    up_z, down_z = (gz + 1) % nz, (gz + nz - 1) % nz
    up_y, down_y = (gy + 1) % ny, (gy + ny - 1) % ny
    column = []
    for d in (8, 7, 9, 6, 10, 5, 11, 4, 12, 3, 13, 2, 14, 1, 15, 0):
        for k in range(2):
            if d or k:
                z = (zpos + d) % 16
                column.append((gz_of(z // 4, xpos, ypos, (core + k) % 2), z % 4))
    layer = []
    for i in (2, 1, 3, 0):
        for j in (2, 1, 3, 0):
            if i or j:
                layer.append((gz_of(zhi, (xpos + i) % 4, (ypos + j) % 4, core), gy))
    faces = [(up_z, gy), (down_z, gy), (gz, up_y), (gz, down_y)]
    around = []
    for dz in (1, -1):
        for dy in (0, 1, -1):
            around.append((dz, dy, ((gz + dz + nz) % nz, (gy + dy + ny) % ny)))
    corners = [(dz, dy, device) for dz, dy, device in around if dy]
    greeted = column + [device for _, _, device in around] + layer

    barrier = pltpu.get_barrier_semaphore()
    for device in greeted:
        pl.semaphore_signal(barrier, inc=1, device_id=device, device_id_type=MESH)

    local = []
    for i, (source, target) in enumerate(
        ((dens_in, rho0.at[1:5, 8:40, :]), (guess_in, val0.at[1:5, 8:40, :]), (right_in, src0))
    ):
        copy = pltpu.make_async_copy(source, target, local_sem.at[i])
        copy.start()
        local.append(copy)

    count = [0]

    def send(source, target, device):
        i = count[0]
        count[0] = i + 1
        copy = pltpu.make_async_remote_copy(
            src_ref=source, dst_ref=target, send_sem=send_sem.at[i], recv_sem=recv_sem.at[i],
            device_id=device, device_id_type=MESH,
        )
        copy.start()
        return copy

    def wait_recv(copies):
        for copy in copies:
            copy.wait_recv()

    def wait_send(copies):
        for copy in copies:
            copy.wait_send()

    fine = Level((4, 32, 512), 8, rho0, bx0, by0, bz0, dg0, idg0)
    middle = Level((4, 32, 256), 16, rho1, bx1, by1, bz1, dg1, idg1)
    coarse = Level((5, 24, 128), 8, rho2, bx2, by2, bz2, dg2, idg2)

    z_low = jnp.where(gz > 0, 1.0, 0.0).astype(F32)
    z_high = jnp.where(gz < nz - 1, 1.0, 0.0).astype(F32)
    y_low = jnp.where(gy > 0, 1.0, 0.0).astype(F32)
    y_high = jnp.where(gy < ny - 1, 1.0, 0.0).astype(F32)

    pair_x = pair_matrix()

    def halve_x(blocks):
        rows = sum(block.shape[0] for block in blocks)
        summed = dot(jnp.concatenate([b[:, 0:256] for b in blocks] + [b[:, 256:512] for b in blocks], axis=0), pair_x)
        out, at = [], 0
        for block in blocks:
            n = block.shape[0]
            out.append((summed[at : at + n], summed[rows + at : rows + at + n]))
            at += n
        return out

    def halve_y(slot, value):
        n = value.shape[0]
        pair_rows[slot, 0:n, :] = value
        return pair_rows[slot, pl.ds(0, n // 2, stride=2), :] + pair_rows[slot, pl.ds(1, n // 2, stride=2), :]

    def halve_xy(blocks):
        return [
            jnp.concatenate([halve_y(2 * i, left), halve_y(2 * i + 1, right)], axis=1)
            for i, (left, right) in enumerate(halve_x(blocks))
        ]

    def restrict1(read):
        return halve_y(0, dot(read(0) + read(1), pair_x))

    half_rows, half_cols = iota((128, 256), 0), iota((128, 256), 1)
    to_halves = jnp.where((half_cols % 64 == half_rows // 2) & ((half_cols < 64) | (half_cols >= 192)), 0.125, 0.0).astype(jnp.bfloat16)

    def pack_message(field, value):
        pair_tmp[...] = dot(value, to_halves)
        for r in range(2):
            t = 4 * r
            message[field, r : r + 1, :] = (
                pair_tmp[t : t + 1, 0:128] + pair_tmp[t + 1 : t + 2, 0:128]
                + pair_tmp[t + 2 : t + 3, 128:256] + pair_tmp[t + 3 : t + 4, 128:256]
            )

    def gather_column(field, inbox):
        inbox[zhi, core, gy] = message[field]
        return [send(message.at[field], inbox.at[zhi, core, gy], device) for device in column]

    def gather_layer(field, inbox, wide):
        for zh in range(4):
            for y in range(4):
                tile[field, zh, 2 * y : 2 * y + 2, :] = inbox[zh, 0, y] + inbox[zh, 1, y]
        slot = xpos * 4 + ypos
        wide[slot] = tile[field]
        return [send(tile.at[field], wide.at[slot], device) for device in layer]

    local[0].wait()
    own1 = halve_xy([rho0[2 * k + 1, 8:40, :] + rho0[2 * k + 2, 8:40, :] for k in range(2)])
    for k in range(2):
        rho1[k + 2, 16:32, :] = own1[k]
    own2 = restrict1(lambda k: own1[k])
    rho2[3, 16:24, :] = own2
    pack_message(0, own2)
    local[1].wait()
    for k in range(4):
        for f, ref in ((0, rho0), (1, val0)):
            rows_out[0, f, k : k + 1, :] = ref[k + 1, 39:40, :]
            rows_out[1, f, k : k + 1, :] = ref[k + 1, 8:9, :]

    for way, (row, second) in enumerate(((31, 30), (16, 17))):
        for k in range(2):
            dens_y_out[way, 2 * k : 2 * k + 1, :] = rho1[k + 2, row : row + 1, :]
            dens_y_out[way, 2 * k + 1 : 2 * k + 2, :] = rho1[k + 2, second : second + 1, :]
    for i, (dz, dy, device) in enumerate(corners):
        plane, far_plane = (3, 2) if dz == 1 else (2, 3)
        row, second = (31, 30) if dy == 1 else (16, 17)
        for at, (p, r) in enumerate(((plane, row), (plane, second), (far_plane, row), (far_plane, second))):
            dens_d_out[i, at : at + 1, :] = rho1[p, r : r + 1, :]
    for k in (0, 5):
        smo0[k, 8:40, :] = jnp.zeros((32, 512), F32)
    for k in range(1, 5):
        smo0[k, 7:8, :] = jnp.zeros((1, 512), F32)
        smo0[k, 40:41, :] = jnp.zeros((1, 512), F32)

    pl.semaphore_wait(barrier, len(greeted))

    z_dens = [
        send(rho0.at[4, 8:40, :], rho0.at[0, 8:40, :], faces[0]),
        send(rho0.at[1, 8:40, :], rho0.at[5, 8:40, :], faces[1]),
    ]
    z_vals = [
        send(val0.at[4, 8:40, :], val0.at[0, 8:40, :], faces[0]),
        send(val0.at[1, 8:40, :], val0.at[5, 8:40, :], faces[1]),
    ]
    y_both = [
        send(rows_out.at[0, 0:2], rows_in.at[0, 0:2], faces[2]),
        send(rows_out.at[1, 0:2], rows_in.at[1, 0:2], faces[3]),
    ]

    dens1_copies = [
        send(rho1.at[2:4, 16:32, :], rho1.at[0:2, 16:32, :], faces[0]),
        send(rho1.at[2:4, 16:32, :], rho1.at[4:6, 16:32, :], faces[1]),
        send(dens_y_out.at[0], dens_y_in.at[0], faces[2]),
        send(dens_y_out.at[1], dens_y_in.at[1], faces[3]),
    ]
    for i, (dz, dy, device) in enumerate(corners):
        dens1_copies.append(send(dens_d_out.at[i], dens_d_in.at[i], device))

    rows2 = {dy: (slice(16, 24), slice(16 - 8 * dy, 24 - 8 * dy)) for dy in (0, 1, -1)}
    y_ways = ((1, faces[2]), (-1, faces[3]))
    z_ways = ((1, faces[0]), (-1, faces[1]))

    def fill_y(ref, planes, rows, first):
        last = first + rows - 1
        for k in planes:
            ref[k, first - 1 : first, :] = jnp.where(gy == 0, ref[k, first : first + 1, :], ref[k, first - 1 : first, :])
            ref[k, last + 1 : last + 2, :] = jnp.where(
                gy == ny - 1, ref[k, last : last + 1, :], ref[k, last + 1 : last + 2, :]
            )

    def fill_z(ref, own, planes, rows, reach):
        for i in range(reach):
            low, high = own - 1 - i * planes, own + planes + i * planes
            ref[low, rows, :] = jnp.where(gz == i, ref[low + 1, rows, :], ref[low, rows, :])
            ref[high, rows, :] = jnp.where(gz == nz - 1 - i, ref[high - 1, rows, :], ref[high, rows, :])

    for k in range(4):
        fine.faces_x(k)
    for face in (1, 2, 3):
        fine.faces_z(face)
    wait_recv(y_both)
    for k in range(4):
        for f, ref in ((0, rho0), (1, val0)):
            ref[k + 1, 7:8, :] = rows_in[0, f, k : k + 1, :]
            ref[k + 1, 40:41, :] = rows_in[1, f, k : k + 1, :]
    fill_y(rho0, range(1, 5), 32, 8)
    for k in range(4):
        fine.faces_y(k)
    local[2].wait()

    def smooth(plane):
        for r, m in fine.chunks():
            here, near = fine.neighbours(val0, plane, r, m)
            smo0[plane + 1, 8 + r : 8 + r + m, :] = (1.0 - OMEGA) * here + (
                src0[plane, r : r + m, :] + near
            ) * fine.idg[plane, r : r + m, :]

    for k in (1, 2):
        fine.diagonal(k)
        fine.mask_y(k, ((0, y_low), (32, y_high)))
        smooth(k)
    wait_recv(z_dens)
    fill_z(rho0, 1, 4, slice(8, 40), 1)
    for face in (0, 4):
        fine.faces_z(face)
    for k in (0, 3):
        fine.diagonal(k)
        fine.mask_y(k, ((0, y_low), (32, y_high)))
    fine.mask_z(((0, z_low), (4, z_high)))
    wait_recv(z_vals)
    smooth(3)
    smooth(0)

    for plane in range(4):
        for r, m in fine.chunks():
            here, near = fine.neighbours(smo0, plane, r, m)
            res0[plane, r : r + m, :] = src0[plane, r : r + m, :] - dg0[plane, r : r + m, :] * here + near
    for way, (row, cell) in enumerate(((32, 39), (0, 8))):
        for k in range(2):
            lower = by0[2 * k, row : row + 1, :] * smo0[2 * k + 1, cell : cell + 1, :]
            upper = by0[2 * k + 1, row : row + 1, :] * smo0[2 * k + 2, cell : cell + 1, :]
            face_rows[2 * way + k : 2 * way + k + 1, :] = lower + upper
    blocks = halve_x(
        [res0[0] + res0[1], res0[2] + res0[3], bz0[4] * smo0[4, 8:40, :], bz0[0] * smo0[1, 8:40, :], face_rows[...]]
    )
    part0, part1, give_up, give_down = [
        jnp.concatenate([halve_y(2 * i, left), halve_y(2 * i + 1, right)], axis=1)
        for i, (left, right) in enumerate(blocks[:4])
    ]
    give_rows = jnp.concatenate(blocks[4], axis=1)
    parts = (part0, part1)
    z_out[0, 0] = give_up
    z_out[0, 1] = part1
    z_out[1, 0] = give_down
    z_out[1, 1] = part0
    swap_z = [send(z_out.at[way], z_in.at[way], faces[way]) for way in range(2)]
    for way, row in ((0, 15), (1, 0)):
        for k in range(2):
            y_out[way, k : k + 1, :] = parts[k][row : row + 1]
            y_out[way, 2 + k : 3 + k, :] = give_rows[2 * way + k : 2 * way + k + 1]
    swap_y = [send(y_out.at[way], y_in.at[way], faces[2 + way]) for way in range(2)]
    slot_of, swap_d = {}, []
    for i, (dz, dy, device) in enumerate(corners):
        slot_of[dz, dy] = i
        way = (1 - dy) // 2
        plane = (1 + dz) // 2
        give, row = (give_up if dz == 1 else give_down), (15 if dy == 1 else 0)
        d_out[i, 0:1, :] = give_rows[2 * way + plane : 2 * way + plane + 1]
        d_out[i, 1:2, :] = give[row : row + 1]
        swap_d.append(send(d_out.at[i], d_in.at[i], device))
    column_dens = gather_column(0, inbox_dens)
    dens2_near = [send(rho2.at[3, 16:24, :], rho2.at[3, rows2[dy][1], :], device) for dy, device in y_ways]
    dens2_near += [
        send(rho2.at[3, 16:24, :], rho2.at[3 - dz, rows2[dy][1], :], device) for dz, dy, device in around
    ]

    def coefficients(level, planes, z_faces):
        for k in planes:
            level.faces_x(k)
            level.faces_y(k)
        for k in range(planes[0], planes[-1] + 2):
            level.faces_z(k)
        for k in planes:
            level.diagonal(k)
            level.mask_y(k, ((8, y_low), (level.rows - 8, y_high)))
        level.mask_z(z_faces)

    wait_recv(dens1_copies)
    for way, (row, second) in enumerate(((15, 14), (32, 33))):
        for k in range(2):
            rho1[k + 2, row : row + 1, :] = dens_y_in[way, 2 * k : 2 * k + 1, :]
            rho1[k + 2, second : second + 1, :] = dens_y_in[way, 2 * k + 1 : 2 * k + 2, :]
    for i, (dz, dy, device) in enumerate(corners):
        plane, far_plane = (1, 0) if dz == 1 else (4, 5)
        row, second = (15, 14) if dy == 1 else (32, 33)
        for at, (p, r) in enumerate(((plane, row), (plane, second), (far_plane, row), (far_plane, second))):
            rho1[p, r : r + 1, :] = dens_d_in[i, at : at + 1, :]
    fill_y(rho1, range(6), 16, 16)
    fill_z(rho1, 2, 2, slice(8, 40), 1)
    coefficients(middle, range(4), ((1, z_low), (3, z_high)))
    wait_recv(dens2_near)
    fill_y(rho2, (3,), 8, 16)
    fill_z(rho2, 3, 1, slice(16, 24), 1)
    coarse.span = (8, 16)
    coefficients(coarse, (2,), ((2, z_low), (3, z_high)))
    coarse.span = (0, 24)

    wait_recv(swap_z + swap_y + swap_d)
    source1 = []
    for k in range(2):
        src1[k + 2, 16:32, :] = parts[k] + z_in[k, 0]
        src1[k + 2, 16:17, :] = src1[k + 2, 16:17, :] + y_in[0, 2 + k : 3 + k, :]
        src1[k + 2, 31:32, :] = src1[k + 2, 31:32, :] + y_in[1, 2 + k : 3 + k, :]
        source1.append(src1[k + 2, 16:32, :])
        val1[k + 2, 16:32, :] = 4.0 * source1[k] * idg1[k + 1, 8:24, :]
    for dz, plane, theirs, mine in ((1, 4, z_in[1, 1], give_up), (-1, 1, z_in[0, 1], give_down)):
        src1[plane, 16:32, :] = theirs + mine
        low, high = slot_of[-dz, 1], slot_of[-dz, -1]
        src1[plane, 16:17, :] = src1[plane, 16:17, :] + d_in[low, 0:1, :]
        src1[plane, 31:32, :] = src1[plane, 31:32, :] + d_in[high, 0:1, :]
        val1[plane, 16:32, :] = 4.0 * src1[plane, 16:32, :] * idg1[plane - 1, 8:24, :]
    for dy, row in ((1, 32), (-1, 15)):
        way = (1 - dy) // 2
        for k, dz in ((0, -1), (1, 1)):
            total = y_in[1 - way, k : k + 1, :] + give_rows[2 * way + k : 2 * way + k + 1]
            total = total + d_in[slot_of[-dz, -dy], 1:2, :]
            src1[k + 2, row : row + 1, :] = total
            val1[k + 2, row : row + 1, :] = 4.0 * total * idg1[k + 1, row - 8 : row - 7, :]

    def residual1(k):
        here, near = middle.neighbours(val1, k + 1, 8, 16)
        base1[k + 2, 16:32, :] = (1.0 - OMEGA) * here + (4.0 * source1[k] + near) * idg1[k + 1, 8:24, :]
        return (1.0 - OMEGA) * source1[k] + 0.25 * near

    source2 = restrict1(residual1)
    val2[3, 16:24, :] = 16.0 * source2 * idg2[2, 8:16, :]
    copies2 = [send(val2.at[3, 16:24, :], val2.at[3, rows2[dy][1], :], device) for dy, device in y_ways]
    for dz, device in z_ways:
        copies2.append(send(val2.at[3, 16:24, :], val2.at[3 - dz, 16:24, :], device))

    def pass_on(ref, reach):
        return [
            send(ref.at[4 - reach, 8:32, :], ref.at[3 - reach, 8:32, :], faces[0]),
            send(ref.at[2 + reach, 8:32, :], ref.at[3 + reach, 8:32, :], faces[1]),
        ]

    dens2_far = pass_on(rho2, 2)
    more1 = [
        send(base1.at[3, 16:32, :], base1.at[1, 16:32, :], faces[0]),
        send(base1.at[2, 16:32, :], base1.at[4, 16:32, :], faces[1]),
    ]
    for way, row in ((0, 31), (1, 16)):
        for k in range(2):
            wide_y_out[way, k : k + 1, :] = base1[k + 2, row : row + 1, :]
        more1.append(send(wide_y_out.at[way], wide_y_in.at[way], faces[2 + way]))
    for i, (dz, dy, device) in enumerate(corners):
        plane, row = (3 if dz == 1 else 2), (31 if dy == 1 else 16)
        wide_d_out[i] = base1[plane, row : row + 1, :]
        more1.append(send(wide_d_out.at[i], wide_d_in.at[i], device))
    wait_recv(column_dens)
    layer_dens = gather_layer(0, inbox_dens, wide_dens)
    wait_recv(copies2)
    here, near = coarse.neighbours(val2, 2, 8, 8)
    pack_message(1, (1.0 - OMEGA) * source2 + 0.0625 * near)
    base2[3, 16:24, :] = (1.0 - OMEGA) * here + (16.0 * source2 + near) * idg2[2, 8:16, :]
    column_src = gather_column(1, inbox_src)
    more2 = [send(base2.at[3, 16:24, :], base2.at[3, rows2[dy][1], :], device) for dy, device in y_ways]
    more2 += [send(base2.at[3, 16:24, :], base2.at[3 - dz, rows2[dy][1], :], device) for dz, dy, device in around]
    wait_recv(dens2_far)
    dens2_last = pass_on(rho2, 3)

    wait_recv(layer_dens)
    lane, sub = iota((8, 128), 1), iota((8, 128), 0)
    right_half = lane >= 64
    first_x, last_x = (lane % 64) == 0, (lane % 64) == 63
    first_y, last_y = (lane < 64) & (sub == 0), (lane >= 64) & (sub == 7)

    def lower_y(v):
        q = pltpu.roll(v, 64, 1)
        return jnp.where(right_half, q, pltpu.roll(q, 1, 0))

    def upper_y(v):
        q = pltpu.roll(v, 64, 1)
        return jnp.where(right_half, pltpu.roll(q, 7, 0), q)

    scale3 = 0.015625
    for zh in range(4):
        for s in range(16):
            rho3[1 + 16 * zh + s] = wide_dens[s, zh]
    rho3[0] = rho3[1]
    rho3[65] = rho3[64]

    def face3(k, _):
        bz3[k] = scale3 * twice_inverse(rho3[k] + rho3[k + 1])
        return 0

    lax.fori_loop(0, 65, face3, 0)

    def coef3(k, _):
        rho = rho3[k + 1]
        edge = twice_inverse(rho + rho)
        low = twice_inverse(rho + jnp.where(first_x, rho, pltpu.roll(rho, 1, 1)))
        total = low + jnp.where(last_x, edge, pltpu.roll(low, 127, 1))
        bx3[k] = jnp.where(first_x, 0.0, scale3 * low)
        low = twice_inverse(rho + jnp.where(first_y, rho, lower_y(rho)))
        high = upper_y(low)
        total = total + low + jnp.where(last_y, edge, high)
        by3_up[k] = jnp.where(last_y, 0.0, scale3 * high)
        by3[k] = jnp.where(first_y, 0.0, scale3 * low)
        dg3[k] = scale3 * total + bz3[k] + bz3[k + 1]
        return 0

    lax.fori_loop(0, 64, coef3, 0, unroll=4)

    zero_plane = jnp.zeros((8, 128), F32)
    lowest = (gz + 1) // 2 - 1
    cor3[...] = jnp.zeros((6, 8, 128), F32)
    for k in (0, 1, 2, 67, 68, 69):
        dir3[k] = zero_plane
        res3[k] = zero_plane
    mul3[64] = zero_plane
    img3[64] = zero_plane

    def clear3(k, _):
        dir3[k + 3] = zero_plane
        mul3[k] = zero_plane
        return 0

    lax.fori_loop(0, 64, clear3, 0, unroll=8)

    wait_send(
        z_dens + z_vals + y_both + dens1_copies + swap_z + swap_y + swap_d + column_dens + layer_dens + copies2
    )
    wait_recv(column_src)
    layer_src = gather_layer(1, inbox_src, wide_src)

    z_smooth = [
        send(smo0.at[4, 8:40, :], far_smooth.at[0], faces[0]), send(smo0.at[1, 8:40, :], far_smooth.at[1], faces[1])
    ]
    for k in range(4):
        rows_out[0, 2, k : k + 1, :] = smo0[k + 1, 39:40, :]
        rows_out[1, 2, k : k + 1, :] = smo0[k + 1, 8:9, :]
    y_smooth = [send(rows_out.at[way, 2], rows_in.at[way, 2], faces[2 + way]) for way in range(2)]
    wait_recv(more2)
    base2_far = pass_on(base2, 2)

    wait_recv(dens2_last)
    wait_send(dens2_near + dens2_far + dens2_last + more1 + more2 + column_src)

    def inside_z(face):
        at = gz + face - 2
        return jnp.where((at > 0) & (at < nz), 1.0, 0.0).astype(F32)

    fill_y(rho2, range(7), 8, 16)
    fill_z(rho2, 3, 1, slice(8, 32), 3)
    coefficients(coarse, range(5), [(face, inside_z(face)) for face in range(6)])

    wait_recv(layer_src)

    for zh in range(4):
        for k in range(16):
            res3[16 * zh + k + 3] = wide_src[k, zh]

    def whole(v):
        return jnp.sum(jnp.sum(v, axis=1, keepdims=True), axis=0, keepdims=True)

    def apply(k, prev, here, later):
        bx = bx3[k]
        swapped = pltpu.roll(here, 64, 1)
        below = jnp.where(right_half, swapped, pltpu.roll(swapped, 1, 0))
        above = jnp.where(right_half, pltpu.roll(swapped, 7, 0), swapped)
        image = (dg3[k] * here - bz3[k] * prev) - (bz3[k + 1] * later + by3[k] * below)
        image = image - ((bx * pltpu.roll(here, 1, 1) + by3_up[k] * above) + pltpu.roll(bx * here, 127, 1))
        img3[k] = image
        return image

    def advance(k, alpha, beta):
        dir3[k + 3] = res3[k + 3] + beta * dir3[k + 3]
        image = img3[k] + beta * mul3[k]
        mul3[k] = image
        resid = res3[k + 3] - alpha * image
        res3[k + 3] = resid
        return resid

    def totals(first, next_resid):
        def plane(k, carry):
            norm, power, prev, here = carry
            later = next_resid(k + 1)
            image = apply(k, prev, here, later)
            return norm + here * here, power + here * image, here, later

        norm, power, _, _ = lax.fori_loop(0, 64, plane, (zero_plane, zero_plane, zero_plane, first), unroll=64)
        return whole(norm), whole(power)

    norm, power = totals(res3[3], lambda k: res3[k + 3])

    def sweep(step, carry):
        alpha, beta, norm = carry
        norm_next, power = totals(advance(0, alpha, beta), lambda k: advance(k, alpha, beta))
        cor3[...] = cor3[...] + alpha * dir3[pl.ds(lowest + 1, 6)]
        beta = norm_next / norm
        return norm_next / (power - beta * norm_next / alpha), beta, norm_next

    alpha, beta, _ = lax.fori_loop(0, SWEEPS - 1, sweep, (norm / power, jnp.zeros((1, 1), F32), norm))

    window = pl.ds(lowest + 1, 6)
    cor3[...] = cor3[...] + alpha * (res3[window] + beta * dir3[window])

    spread_rows, spread_cols = iota((128, 256), 0), iota((128, 256), 1)
    fine_x = spread_cols % 128
    parent = fine_x // 2
    near = parent + 2 * (fine_x % 2) - 1
    half = spread_cols // 128
    inside = (near >= 0) & (near < 64)
    from_halves = (
        jnp.where(spread_rows == parent + 64 * half, 0.75, 0.0)
        + jnp.where((spread_rows == near + 64 * half) & inside, 0.25, 0.0)
    ).astype(jnp.bfloat16)
    mixed = []
    for d in range(-3, 4):
        plane = gz + d + 4
        index = plane // 2 - lowest
        other = index + 2 * (plane % 2) - 1
        mixed.append(0.75 * cor3[index] + 0.25 * cor3[other])
    x_done = dot(jnp.concatenate(mixed, axis=0), from_halves)
    wait_recv(more1 + base2_far + z_smooth + y_smooth)
    wait_send(z_smooth)
    for way, row in ((0, 15), (1, 32)):
        for k in range(2):
            base1[k + 2, row : row + 1, :] = wide_y_in[way, k : k + 1, :]
    for i, (dz, dy, _) in enumerate(corners):
        plane, row = (1 if dz == 1 else 4), (15 if dy == 1 else 32)
        base1[plane, row : row + 1, :] = wide_d_in[i]
    first_row, last_row = iota((8, 128), 0) == 0, iota((8, 128), 0) == 7
    window = pl.ds(pl.multiple_of(8 * gy, 8), 24)
    for k in range(7):
        even, odd = x_done[8 * k : 8 * k + 8, 0:128], x_done[8 * k : 8 * k + 8, 128:256]
        fine_rows[k, 0:8, :] = zero_plane
        fine_rows[k, 40:48, :] = zero_plane
        below = jnp.where(first_row, 0.0, pltpu.roll(odd, 1, 0))
        above = jnp.where(last_row, 0.0, pltpu.roll(even, 7, 0))
        fine_rows[k, pl.ds(8, 8, stride=4), :] = 0.75 * even + 0.25 * below
        fine_rows[k, pl.ds(9, 8, stride=4), :] = 0.75 * even + 0.25 * odd
        fine_rows[k, pl.ds(10, 8, stride=4), :] = 0.75 * odd + 0.25 * even
        fine_rows[k, pl.ds(11, 8, stride=4), :] = 0.75 * odd + 0.25 * above
        up2[k, 8:32, :] = fine_rows[k, window, :]

    def in_grid(shape, margin, first_row, rows, plane, planes):
        row = iota(shape, 0)
        at = row + first_row
        good = (row >= margin) & (row < shape[0] - margin) & (at >= 0) & (at < rows)
        return good & (plane >= 0) & (plane < planes)

    ups = []
    for k in range(5):
        here, near = coarse.neighbours(up2, k, 0, 24)
        up = base2[k + 1, 8:32, :] + (1.0 - OMEGA) * here + near * idg2[k]
        ups.append(jnp.where(in_grid((24, 128), 1, 8 * gy - 8, 8 * ny, gz + k - 2, nz), up, 0.0))

    spread_x1, spread_x0 = spread_matrix(128), spread_matrix(256)

    def prolong(ups, target, first, rows, spread_x, add):
        height = ups[0].shape[0]
        tall = 2 * height - 16
        n = height - 8
        x_done = dot(jnp.concatenate(ups, axis=0), spread_x)
        tiles = x_done.shape[1] // 128
        for t in range(tiles):
            for k in range(len(ups)):
                pair_rows[t, 0:height, :] = x_done[height * k : height * (k + 1), 128 * t : 128 * (t + 1)]
                here = 0.75 * pair_rows[t, 4 : 4 + n, :]
                fine_rows[k, pl.ds(0, n, stride=2), :] = here + 0.25 * pair_rows[t, 3 : 3 + n, :]
                fine_rows[k, pl.ds(1, n, stride=2), :] = here + 0.25 * pair_rows[t, 5 : 5 + n, :]
            cols = slice(128 * t, 128 * (t + 1))
            for k in range(6):
                parent_z = (k + first) // 2
                near_z = parent_z + 2 * ((k + first) % 2) - 1
                if add and k in (0, 5):
                    kept, taken = slice(8, tall - 8), slice(8, tall - 8)
                else:
                    kept, taken = rows, slice(0, tall)
                value = 0.75 * fine_rows[parent_z, taken, :] + 0.25 * fine_rows[near_z, taken, :]
                target[k, kept, cols] = target[k, kept, cols] + value if add else value

    prolong(ups, up1, 2, slice(8, 40), spread_x1, False)
    ups = []
    for k in range(4):
        parts = []
        for r, m in middle.chunks():
            here, near = middle.neighbours(up1, k, r, m)
            base = base1[k + 1, 8 + r : 8 + r + m, :]
            parts.append(base + (1.0 - OMEGA) * here + near * idg1[k, r : r + m, :])
        up = jnp.concatenate(parts, axis=0)
        ups.append(jnp.where(in_grid((32, 256), 7, 16 * gy - 8, 16 * ny, 2 * gz + k - 1, 2 * nz), up, 0.0))
    for k, plane in ((0, 0), (1, 5)):
        smo0[plane, 8:40, :] = far_smooth[k]
    for k in range(4):
        smo0[k + 1, 7:8, :] = rows_in[0, 2, k : k + 1, :]
        smo0[k + 1, 40:41, :] = rows_in[1, 2, k : k + 1, :]
    prolong(ups, smo0, 1, slice(0, 48), spread_x0, True)
    for k in range(4):
        for r, m in fine.chunks():
            here, near = fine.neighbours(smo0, k, r, m)
            out[k, r : r + m, :] = (1.0 - OMEGA) * here + (src0[k, r : r + m, :] + near) * fine.idg[k, r : r + m, :]

    wait_send(y_smooth + layer_src + base2_far)


def coefficient_scratch(planes, rows, cols):
    own = pltpu.VMEM((planes, rows, cols), F32)
    return [own, pltpu.VMEM((planes, rows + 8, cols), F32), pltpu.VMEM((planes + 1, rows, cols), F32), own, own]


COPIES = 6 + 8 + 8 + 8 + 2 + 2 + 4 + 4 + 8 + 8 + 2 + 62 + 30


def per_device(density, right_side, pressure_guess):
    coarsest, longer = pltpu.VMEM((64, 8, 128), F32), pltpu.VMEM((65, 8, 128), F32)
    padded = pltpu.VMEM((70, 8, 128), F32)
    return pl.pallas_call(
        kernel,
        out_shape=jax.ShapeDtypeStruct(density.shape, F32),
        in_specs=[pl.BlockSpec(memory_space=pltpu.HBM)] * 3,
        out_specs=pl.BlockSpec(memory_space=pltpu.VMEM),
        scratch_shapes=[
            *[pltpu.VMEM((6, 48, 512), F32)] * 3,
            *[pltpu.VMEM((4, 32, 512), F32)] * 2,
            *coefficient_scratch(4, 32, 512),
            pltpu.VMEM((6, 48, 256), F32),
            *[pltpu.VMEM((6, 48, 256), F32)] * 4,
            *coefficient_scratch(4, 32, 256),
            pltpu.VMEM((7, 40, 128), F32),
            *[pltpu.VMEM((7, 40, 128), F32)] * 3,
            *coefficient_scratch(5, 24, 128),
            pltpu.VMEM((2, 3, 4, 512), F32),
            pltpu.VMEM((2, 3, 4, 512), F32),
            pltpu.VMEM((2, 2, 128), F32),
            pltpu.VMEM((4, 2, 4, 2, 128), F32),
            pltpu.VMEM((4, 2, 4, 2, 128), F32),
            pltpu.VMEM((2, 4, 8, 128), F32),
            pltpu.VMEM((16, 4, 8, 128), F32),
            pltpu.VMEM((16, 4, 8, 128), F32),
            pltpu.VMEM((66, 8, 128), F32),
            coarsest, coarsest, coarsest, longer, coarsest,
            padded, padded, longer, longer, pltpu.VMEM((6, 8, 128), F32),
            pltpu.VMEM((8, 256), F32),
            pltpu.VMEM((8, 32, 128), F32),
            pltpu.VMEM((7, 48, 128), F32),
            pltpu.VMEM((2, 32, 512), F32),
            pltpu.VMEM((8, 512), F32),
            *[pltpu.VMEM((2, 2, 16, 256), F32)] * 2,
            *[pltpu.VMEM((2, 4, 256), F32)] * 2,
            *[pltpu.VMEM((4, 2, 256), F32)] * 2,
            *[pltpu.VMEM((2, 2, 256), F32)] * 2,
            *[pltpu.VMEM((4, 1, 256), F32)] * 2,
            *[pltpu.VMEM((2, 4, 256), F32)] * 2,
            *[pltpu.VMEM((4, 4, 256), F32)] * 2,
            pltpu.SemaphoreType.DMA((3,)),
            pltpu.SemaphoreType.DMA((COPIES,)),
            pltpu.SemaphoreType.DMA((COPIES,)),
        ],
        compiler_params=pltpu.CompilerParams(
            collective_id=0, has_side_effects=True, vmem_limit_bytes=32 * 1024 * 1024
        ),
        cost_estimate=pl.CostEstimate(flops=20_000_000, bytes_accessed=1 << 20, transcendentals=0),
    )(*[pltpu.with_memory_space_constraint(a, pltpu.HBM) for a in (density, right_side, pressure_guess)])


def solution(mesh):
    spec = P("gz", "gy", None)
    return jax.shard_map(per_device, mesh=mesh, in_specs=(spec, spec, spec), out_specs=spec, check_vma=False)
```
